256 devices in a mesh: section: 32 (over y_lo, z, core), dp: 8 (over y_hi, x).
Axes of the slice: x: 4, y: 4 (y_hi: 2, y_lo: 2; y = y_hi * 2 + y_lo), z: 8, core: 2. Of those that a mesh axis runs over, the one named last changes fastest.
Arguments:
- forward_codes: int32 [32, 3072, 2048], P('section', 'dp'), may hold values from 0 to 4095
- forward_scales: bfloat16 [32, 3072, 192], P('section', 'dp'), may hold values from 0.019897461 to 0.25
- stored_base: bfloat16 [32, 256, 6144], P('section', 'dp'), may hold values from -6 to 6
- sample_ids: int32 [32, 3072], P('section', 'dp'), may hold values from 0 to 31
- backward_codes: bfloat16 [32, 3072, 6144], P('section', 'dp'), may hold values from 0 to 255
- backward_scales: bfloat16 [32, 3072, 192], P('section', 'dp'), may hold values from 4.9829483e-05 to 0.00049972534
- norm_gain: float32 [32, 6144], P('section'), may hold values from 0.5 to 2
- w_down: bfloat16 [32, 6144, 128], P('section'), may hold values from -0.078125 to 0.078125
- w_up: bfloat16 [32, 6144, 128], P('section'), may hold values from -0.5 to 0.5
Outputs:
- feedback: bfloat16 [32, 3072, 6144], P('section', 'dp')
- grad_down: float32 [32, 6144, 128], P('section', 'dp')
- grad_up: float32 [32, 6144, 128], P('section', 'dp')
The draws below stay inside these ranges and needn't reach their ends.
Inputs may be any that keep to these rules, and one draw needn't show every extreme that they name: `forward_codes`: each word holds 3 codes of 4 bits of consecutive features, lowest bits first. sample_ids[s, t] counts from the first stored row of the dp block of token t.
All inputs are finite; a program needn't handle non-finite values.
Results may differ from the reference program's by a relative error of at most 0.0072.
Values may be sent and summed in bfloat16 or wider, within the bound.
No kernel may reach another device: no remote copies, remote signals or barrier semaphores. Data moves between devices by JAX's collectives and lax.ppermute only.
A program may use at most 192 MiB of HBM per device.

```python
import math
import jax
import jax.numpy as jnp
from jax import lax

D = 6144
RANK = 128
BLOCK = 32
TOK_DEV = 384
SAMP_DEV = 32
SECTIONS = 32
TOKENS = 3072
SAMPLES = 256


def draw_backward_codes(key, part):
    key = jax.random.fold_in(key, 11)
    uniform_values = jax.random.uniform(key, (SECTIONS, TOKENS, D), jnp.float32)
    return jnp.minimum(jnp.floor(uniform_values * 256.0), 255.0).astype(jnp.bfloat16)


def touch_ends(entries, key, least, top_value):
    spot = [jax.random.randint(jax.random.fold_in(key, axis), (), 0, length) for axis, length in enumerate(entries.shape)]
    main_axis = entries.shape.index(max(entries.shape))
    next_to = spot[:main_axis] + [(spot[main_axis] + 1) % entries.shape[main_axis]] + spot[main_axis + 1:]
    return entries.at[tuple(spot)].set(least).at[tuple(next_to)].set(top_value)


def steps_of(key, shape, pieces, smallest, top_value):
    factor_of, own = 1.0, jax.random.fold_in(key, 6)
    for dim, blocks in pieces:
        heights = jnp.exp(jax.random.uniform(jax.random.fold_in(own, dim), (blocks,), jnp.float32, smallest / len(pieces), top_value / len(pieces)))
        factor_of = factor_of * jnp.repeat(heights, shape[dim] // blocks).reshape([-1 if axis == dim else 1 for axis in range(len(shape))])
    return factor_of


def centred(rng, extent, width, bound, split=(), held_as=jnp.bfloat16):
    array = width * jax.random.normal(rng, extent, jnp.float32)
    if split:
        array = array * steps_of(rng, extent, split, -0.22, 0.18)
    return jnp.clip(array, -bound, bound).astype(held_as)


def setup_inputs(seed: int = 0) -> dict:
    streams_of = jax.random.split(jax.random.key(seed), 10)
    return {
        "forward_codes": touch_ends(jax.random.randint(streams_of[0], (SECTIONS, TOKENS, D // 3), 0, 4096), jax.random.fold_in(streams_of[0], 1), 0, 4095).astype(jnp.int32),
        "forward_scales": jnp.clip(jnp.exp(math.log(0.25) - 2.5308688 * jax.random.uniform(streams_of[1], (SECTIONS, TOKENS, D // BLOCK), jnp.float32) ** steps_of(streams_of[1], (SECTIONS, TOKENS, D // BLOCK), ((0, 32), (1, 8)), -0.2, 0.2)), 0.019897461, 0.25).astype(jnp.bfloat16),
        "stored_base": centred(streams_of[2], (SECTIONS, SAMPLES, D), 1.0, 6.0, ((0, 32), (1, 8))),
        "sample_ids": touch_ends(jax.random.randint(streams_of[3], (SECTIONS, TOKENS), 0, SAMP_DEV), jax.random.fold_in(streams_of[3], 1), 0, SAMP_DEV - 1).astype(jnp.int32),
        "backward_codes": draw_backward_codes(jax.random.fold_in(streams_of[9], 71), 0),
        "backward_scales": jnp.clip(jnp.exp(math.log(0.00049972534) - 2.3054518 * jax.random.uniform(streams_of[5], (SECTIONS, TOKENS, D // BLOCK), jnp.float32) ** steps_of(streams_of[5], (SECTIONS, TOKENS, D // BLOCK), ((0, 32), (1, 8)), -0.2, 0.2)), 4.982948303222656e-05, 0.00049972534).astype(jnp.bfloat16),
        "norm_gain": jnp.clip(jnp.exp(math.log(2.0) - 1.3862944 * jax.random.uniform(streams_of[6], (SECTIONS, D), jnp.float32) ** steps_of(streams_of[6], (SECTIONS, D), ((0, 32),), -0.2, 0.2)), 0.5, 2.0),
        "w_down": centred(streams_of[7], (SECTIONS, D, RANK), D ** -0.5, 0.078125, ((0, 32),)),
        "w_up": centred(streams_of[8], (SECTIONS, D, RANK), RANK ** -0.5, 0.5, ((0, 32),)),
    }


def unpack_codes(packed):
    offsets_bits = jnp.arange(3, dtype=jnp.int32) * 4
    unpacked = jnp.bitwise_and(jnp.right_shift(packed[..., None], offsets_bits), 15)
    return unpacked.reshape(packed.shape[0], -1)

def scale_blocks(values, scales):
    shaped = values.reshape(values.shape[0], scales.shape[-1], -1)
    return (shaped * scales.astype(jnp.float32)[:, :, None]).reshape(values.shape)

def reference(forward_codes, forward_scales, stored_base, sample_ids, backward_codes, backward_scales, norm_gain, w_down, w_up):
    offsets = jnp.arange(TOKENS, dtype=jnp.int32) // TOK_DEV * SAMP_DEV

    def message(index):
        picked = jnp.take(stored_base[index], (sample_ids[index] + offsets).astype(jnp.int32), axis=0)
        codes = (unpack_codes(forward_codes[index]) - 8).astype(jnp.float32)
        return (picked.astype(jnp.float32) + scale_blocks(codes, forward_scales[index])).astype(jnp.bfloat16)

    def grad_message(index):
        codes = backward_codes[index].astype(jnp.float32) - 128.0
        return scale_blocks(codes, backward_scales[index]).astype(jnp.bfloat16)

    def one_section(index):
        own_message = message(index)
        incoming = message((index - 1) % SECTIONS).astype(jnp.float32)
        out_grad = grad_message((index + 1) % SECTIONS)
        center = incoming - lax.optimization_barrier(jnp.mean(incoming, axis=1, keepdims=True))
        variance = lax.optimization_barrier(jnp.mean(center * center, axis=1, keepdims=True))
        hidden = (norm_gain[index] * center / jnp.sqrt(variance + 1e-05)).astype(jnp.bfloat16)
        pre = jnp.dot(hidden, w_down[index], preferred_element_type=jnp.float32)
        act_value, gelu_back = jax.vjp(jax.nn.gelu, pre)
        act = act_value.astype(jnp.bfloat16)
        lifted = lax.dot_general(act, w_up[index], (((1,), (1,)), ((), ())), preferred_element_type=jnp.float32)
        feedback = (incoming + lifted - own_message.astype(jnp.float32)).astype(jnp.bfloat16)
        dact = jnp.dot(out_grad, w_up[index], preferred_element_type=jnp.float32)
        dpre = gelu_back(dact)[0].astype(jnp.bfloat16)
        grad_down = lax.dot_general(hidden, dpre, (((0,), (0,)), ((), ())), preferred_element_type=jnp.float32)
        grad_up = lax.dot_general(out_grad, act, (((0,), (0,)), ((), ())), preferred_element_type=jnp.float32)
        return (feedback, grad_down, grad_up)
    feedback, grad_down, grad_up = lax.map(one_section, jnp.arange(SECTIONS, dtype=jnp.int32))
    return (feedback, grad_down, grad_up)
```

```python
import functools
import math

import jax
import jax.numpy as jnp
from jax import lax
from jax.experimental import pallas as pl
from jax.experimental.pallas import tpu as pltpu
from jax.sharding import PartitionSpec as P

D = 6144
R = 128
TOK = 384
PIECE = D // 8
QUARTER = D // 4
F32 = jnp.float32
BF16 = jnp.bfloat16
ROWS = 32
CHUNK = 96
MIB = 1 << 20
ROOT_2_PI = math.sqrt(2.0 / math.pi)


def params(mib):
    return pltpu.CompilerParams(vmem_limit_bytes=mib * MIB)


def cost(flops, moved):
    return pl.CostEstimate(flops=flops, bytes_accessed=moved, transcendentals=0)


def lanes(shape):
    return lax.broadcasted_iota(jnp.int32, shape, 1)


def spread_scales(scales, tile, rows):
    part = scales[:, : 128] if tile < 32 else scales[:, 128 : 256]
    at = lanes((rows, 128)) // 32 + 4 * (tile % 32)
    return jnp.take_along_axis(part, at, axis=1)


def message_kernel(codes_ref, scales_ref, base_ref, ids_ref, out_ref):
    rows = codes_ref.shape[0]
    scales = jnp.concatenate(
        [scales_ref[...].astype(F32), jnp.zeros((rows, 64), F32)], axis=1
    )
    picks = (ids_ref[...] == lanes((rows, 32))).astype(BF16)
    lane = lanes((rows, 128))
    for block in range(16):
        words = codes_ref[:, block * 128 : (block + 1) * 128]
        base = jnp.dot(
            picks, base_ref[:, block * 384 : (block + 1) * 384], preferred_element_type=F32
        )
        for j in range(3):
            spot = lane + 128 * j
            word = jnp.take_along_axis(words, spot // 3, axis=1)
            code = jnp.right_shift(word, (spot % 3) * 4) & 15
            step = spread_scales(scales, block * 3 + j, rows)
            value = base[:, j * 128 : (j + 1) * 128] + step * (code - 8).astype(F32)
            out_ref[:, (block * 3 + j) * 128 : (block * 3 + j + 1) * 128] = value.astype(BF16)


def make_message(codes, scales, base, ids, first, count):
    skip = first // ROWS
    return pl.pallas_call(
        message_kernel,
        grid=(count // ROWS,),
        in_specs=[
            pl.BlockSpec((ROWS, D // 3), lambda i: (i + skip, 0)),
            pl.BlockSpec((ROWS, D // 32), lambda i: (i + skip, 0)),
            pl.BlockSpec((32, D), lambda i: (0, 0)),
            pl.BlockSpec((ROWS, 1), lambda i: (i + skip, 0)),
        ],
        out_specs=pl.BlockSpec((ROWS, D), lambda i: (i, 0)),
        out_shape=jax.ShapeDtypeStruct((count, D), BF16),
        compiler_params=params(16),
        cost_estimate=cost(count * D * 80, count * D * 4),
        name="message",
    )(codes, scales, base, ids)


def gradient_kernel(codes_ref, scales_ref, out_ref):
    rows = codes_ref.shape[0]
    scales = jnp.concatenate(
        [scales_ref[...].astype(F32), jnp.zeros((rows, 64), F32)], axis=1
    )
    for tile in range(48):
        part = slice(tile * 128, (tile + 1) * 128)
        step = spread_scales(scales, tile, rows)
        out_ref[:, part] = (step * (codes_ref[:, part].astype(F32) - 128.0)).astype(BF16)


def make_gradient(codes, scales):
    return pl.pallas_call(
        gradient_kernel,
        grid=(TOK // ROWS,),
        in_specs=[
            pl.BlockSpec((ROWS, D), lambda i: (i, 0)),
            pl.BlockSpec((ROWS, D // 32), lambda i: (i, 0)),
        ],
        out_specs=pl.BlockSpec((ROWS, D), lambda i: (i, 0)),
        out_shape=jax.ShapeDtypeStruct((TOK, D), BF16),
        compiler_params=params(16),
        cost_estimate=cost(TOK * D * 20, TOK * D * 4),
        name="gradient",
    )(codes, scales)


def hidden_kernel(first, message_ref, gain_ref, out_ref):
    x = message_ref[...].astype(F32)
    center = x - jnp.sum(x, axis=1, keepdims=True) * (1.0 / D)
    variance = jnp.sum(center * center, axis=1, keepdims=True) * (1.0 / D)
    out_ref[...] = (gain_ref[...] * center * lax.rsqrt(variance + 1e-05)).astype(BF16)


def make_hidden(message, gain):
    count = message.shape[0]
    return pl.pallas_call(
        functools.partial(hidden_kernel, 0),
        grid=(count // ROWS,),
        in_specs=[
            pl.BlockSpec((ROWS, D), lambda i: (i, 0)),
            pl.BlockSpec((1, D), lambda i: (0, 0)),
        ],
        out_specs=pl.BlockSpec((ROWS, D), lambda i: (i, 0)),
        out_shape=jax.ShapeDtypeStruct((count, D), BF16),
        compiler_params=params(16),
        cost_estimate=cost(count * D * 20, count * D * 4),
        name="hidden",
    )(message, gain)


def tanh_of(pre):
    return jnp.tanh(ROOT_2_PI * (pre + 0.044715 * (pre * pre * pre)))


def down_kernel(*refs):
    *hidden_refs, weight_ref, pre_ref, act_ref = refs
    weight = weight_ref[...]
    at = 0
    for hidden_ref in hidden_refs:
        rows = hidden_ref.shape[0]
        pre = jnp.dot(hidden_ref[...], weight, preferred_element_type=F32)
        pre_ref[at : at + rows, :] = pre
        act_ref[at : at + rows, :] = (0.5 * pre * (1.0 + tanh_of(pre))).astype(BF16)
        at += rows


def project_down(hiddens, weight):
    return pl.pallas_call(
        down_kernel,
        out_shape=(
            jax.ShapeDtypeStruct((TOK, R), F32),
            jax.ShapeDtypeStruct((TOK, R), BF16),
        ),
        compiler_params=params(24),
        cost_estimate=cost(2 * TOK * D * R, TOK * D * 2 + D * R * 2),
        name="down",
    )(*hiddens, weight)


def back_kernel(place_ref, grad_ref, chip_ref, *refs):
    *quarter_refs, out_ref = refs
    total = jnp.zeros((TOK, R), F32)
    for j, quarter_ref in enumerate(quarter_refs):
        quarter = lax.rem(place_ref[0] + j, 4)
        at = pl.multiple_of(quarter * QUARTER, QUARTER)
        weight = quarter_ref[...] + chip_ref[pl.ds(at, QUARTER), :]
        total += jnp.dot(
            grad_ref[:, pl.ds(at, QUARTER)], weight, preferred_element_type=F32
        )
    out_ref[...] = total.astype(BF16)


def project_back(place, grad, chip, quarters):
    whole = pl.BlockSpec(memory_space=pltpu.VMEM)
    return pl.pallas_call(
        back_kernel,
        in_specs=[pl.BlockSpec(memory_space=pltpu.SMEM)] + [whole] * 6,
        out_specs=whole,
        out_shape=jax.ShapeDtypeStruct((TOK, R), BF16),
        compiler_params=params(24),
        cost_estimate=cost(2 * TOK * D * R, TOK * D * 2 + D * R * 4),
        name="back",
    )(place, grad, chip, *quarters)


def transposed(left, right):
    return lax.dot_general(left, right, (((0,), (0,)), ((), ())), preferred_element_type=F32)


def grad_up_kernel(place_ref, act_ref, grad_ref, kept_ref, sent_ref):
    act = act_ref[...]
    for half, out_ref in ((0, kept_ref), (1, sent_ref)):
        for j in range(4):
            piece = (place_ref[1] ^ half) * 4 + lax.rem(place_ref[0] + j, 4)
            at = pl.multiple_of(piece * PIECE, PIECE)
            out_ref[j] = transposed(act, grad_ref[:, pl.ds(at, PIECE)]).astype(BF16)


def partial_grad_up(place, act, grad):
    whole = pl.BlockSpec(memory_space=pltpu.VMEM)
    shape = jax.ShapeDtypeStruct((4, R, PIECE), BF16)
    return pl.pallas_call(
        grad_up_kernel,
        in_specs=[pl.BlockSpec(memory_space=pltpu.SMEM)] + [whole] * 2,
        out_specs=(whole,) * 2,
        out_shape=(shape,) * 2,
        compiler_params=params(24),
        cost_estimate=cost(2 * TOK * D * R, TOK * D * 2 + D * R * 2),
        name="grad_up",
    )(place, act, grad)


def grad_down_kernel(place_ref, pre_ref, dact_ref, *refs):
    *hidden_refs, out0, out1, out2, out3 = refs
    pre = pre_ref[...]
    t = tanh_of(pre)
    slope = 0.5 * (1.0 + t) + (0.5 * ROOT_2_PI) * pre * (1.0 - t * t) * (
        1.0 + (3.0 * 0.044715) * (pre * pre)
    )
    dpre = (dact_ref[...].astype(F32) * slope).astype(BF16)
    for j, out_ref in enumerate((out0, out1, out2, out3)):
        for half in range(2):
            piece = (place_ref[1] ^ half) * 4 + lax.rem(place_ref[0] + j, 4)
            at = pl.multiple_of(piece * PIECE, PIECE)
            total = jnp.zeros((R, PIECE), F32)
            row = 0
            for hidden_ref in hidden_refs:
                rows = hidden_ref.shape[0]
                total += transposed(
                    dpre[row : row + rows], hidden_ref[:, pl.ds(at, PIECE)]
                )
                row += rows
            out_ref[half] = total.astype(BF16)


def partial_grad_down(place, pre, dact, hiddens):
    whole = pl.BlockSpec(memory_space=pltpu.VMEM)
    shape = jax.ShapeDtypeStruct((2, R, PIECE), BF16)
    return pl.pallas_call(
        grad_down_kernel,
        in_specs=[pl.BlockSpec(memory_space=pltpu.SMEM)] + [whole] * (2 + len(hiddens)),
        out_specs=(whole,) * 4,
        out_shape=(shape,) * 4,
        compiler_params=params(24),
        cost_estimate=cost(2 * TOK * D * R, TOK * D * 2 + D * R * 2),
        name="grad_down",
    )(place, pre, dact, *hiddens)


def add_kernel(*refs):
    *in_refs, out_ref = refs
    total = in_refs[0][...].astype(F32)
    for ref in in_refs[1:]:
        total += ref[...].astype(F32)
    out_ref[...] = total.astype(BF16)


def add_parts(parts):
    return pl.pallas_call(
        add_kernel,
        out_shape=jax.ShapeDtypeStruct(parts[0].shape, BF16),
        compiler_params=params(16),
        cost_estimate=cost(parts[0].size, parts[0].size * 2 * (len(parts) + 1)),
        name="add",
    )(*parts)


def finish_kernel(*refs):
    *in_refs, out_ref = refs
    total = in_refs[0][...].astype(F32)
    for ref in in_refs[1:]:
        total += ref[...].astype(F32)
    out_ref[...] = total.T


def finish(parts):
    return pl.pallas_call(
        finish_kernel,
        out_shape=jax.ShapeDtypeStruct((PIECE, R), F32),
        compiler_params=params(16),
        cost_estimate=cost(R * PIECE, R * PIECE * 8),
        name="finish",
    )(*parts)


def feedback_kernel(x_ref, own_ref, act_ref, weight_ref, *refs):
    out_ref = refs[-1]
    act = act_ref[...]
    for part in range(4):
        at = slice(part * QUARTER, (part + 1) * QUARTER)
        lifted = lax.dot_general(
            act, weight_ref[at, :], (((1,), (1,)), ((), ())), preferred_element_type=F32
        )
        value = x_ref[:, at].astype(F32) + lifted - own_ref[:, at].astype(F32)
        out_ref[:, at] = value.astype(BF16)


def make_feedback(x, own, own_first, act, weight, first, before):
    count = x.shape[0]
    rows = 48
    skip, own_skip = first // rows, own_first // rows
    specs = [
        pl.BlockSpec((rows, D), lambda i: (i, 0)),
        pl.BlockSpec((rows, D), lambda i: (i + own_skip, 0)),
        pl.BlockSpec((rows, R), lambda i: (i + skip, 0)),
        pl.BlockSpec((D, R), lambda i: (0, 0)),
    ]
    operands = [x, own, act, weight]
    if before is not None:
        specs.append(pl.BlockSpec(memory_space=pl.ANY))
        operands.append(before)
    return pl.pallas_call(
        feedback_kernel,
        grid=(count // rows,),
        in_specs=specs,
        out_specs=pl.BlockSpec((rows, D), lambda i: (i + skip, 0)),
        out_shape=jax.ShapeDtypeStruct((TOK, D), BF16),
        input_output_aliases={} if before is None else {4: 0},
        compiler_params=params(16),
        cost_estimate=cost(2 * count * D * R, count * D * 6 + D * R * 2),
        name="feedback",
    )(*operands)


def body(
    forward_codes,
    forward_scales,
    stored_base,
    sample_ids,
    backward_codes,
    backward_scales,
    norm_gain,
    w_down,
    w_up,
):
    sections = lax.axis_size("section")
    replicas = lax.axis_size("dp")
    across = replicas // 2
    both = ("section", "dp")

    def along(value, distance):
        pairs = [(s, (s + distance) % sections) for s in range(sections)]
        return lax.ppermute(value, "section", pairs)

    def among(value, flip_y, step_x, section_step=0, only_even=False):
        pairs = []
        for s in range(sections):
            if only_even and s % 2:
                continue
            for d in range(replicas):
                y, x = divmod(d, across)
                source = (y ^ flip_y) * across + (x + step_x) % across
                goal = ((s + section_step) % sections) * replicas + d
                pairs.append((s * replicas + source, goal))
        return lax.ppermute(value, both, pairs)

    replica = lax.axis_index("dp")
    place = jnp.stack([replica % across, replica // across]).astype(jnp.int32)

    up = w_up[0]
    quarter = lax.dynamic_slice(up, ((replica % across) * QUARTER, 0), (QUARTER, R))
    quarter0 = lax.ppermute(
        quarter, "section", [(s, (s + 1) % sections) for s in range(1, sections, 2)]
    )
    chip = lax.ppermute(up, "section", [(s, s + 1) for s in range(0, sections, 2)])
    down_next = along(w_down[0], -1)
    gain_next = along(norm_gain, -1)

    codes, scales, base = forward_codes[0], forward_scales[0], stored_base[0]
    ids = sample_ids.reshape(TOK, 1)
    spans = [(0, CHUNK), (CHUNK, TOK - CHUNK)]
    messages = [make_message(codes, scales, base, ids, a, n) for a, n in spans]
    pieces = [
        (messages[0], 0, 0),
        (messages[1], 0, CHUNK),
        (messages[1], CHUNK, 2 * CHUNK),
        (messages[1], 2 * CHUNK, 3 * CHUNK),
    ]
    arrived = [along(m[at : at + CHUNK], 1) for m, at, _ in pieces]
    quarters = [quarter0] + [among(quarter0, 0, j, only_even=True) for j in range(1, 4)]
    gradient = make_gradient(backward_codes[0], backward_scales[0])
    hiddens = [make_hidden(m, gain_next) for m in messages]

    dact_before = project_back(place, gradient, chip, quarters)
    pre_next, act_next = project_down(hiddens, down_next)
    dact_next = along(dact_before, -2)
    act_own = along(act_next, 1)
    act_before = along(act_next, 2)

    kept, sent = partial_grad_up(place, act_before, gradient)
    to_x = partial_grad_down(place, pre_next, dact_next, hiddens)
    up_half = add_parts([kept, among(sent, 1, 0)])
    down_half = add_parts([to_x[0]] + [among(to_x[j], 0, -j) for j in range(1, 4)])
    grad_up = finish([among(up_half[j], 0, -j, section_step=-1) for j in range(4)])
    grad_down = finish(
        [among(down_half[half], half, 0, section_step=1) for half in range(2)]
    )

    feedback = None
    for (own, own_first, first), x in zip(pieces, arrived):
        feedback = make_feedback(x, own, own_first, act_own, up, first, feedback)
    return (feedback[None], grad_down[None], grad_up[None])


def solution(mesh):
    in_specs = (
        P("section", "dp", None),
        P("section", "dp", None),
        P("section", "dp", None),
        P("section", "dp"),
        P("section", "dp", None),
        P("section", "dp", None),
        P("section", None),
        P("section", None, None),
        P("section", None, None),
    )
    out_specs = (P("section", "dp", None), P("section", "dp", None), P("section", "dp", None))
    return jax.shard_map(body, mesh=mesh, in_specs=in_specs, out_specs=out_specs, check_vma=False)
```

```python
import functools
import math

import jax
import jax.numpy as jnp
from jax import lax
from jax.experimental import pallas as pl
from jax.experimental.pallas import tpu as pltpu
from jax.sharding import PartitionSpec as P

D = 6144
R = 128
TOK = 384
PIECE = D // 8
QUARTER = D // 4
F32 = jnp.float32
BF16 = jnp.bfloat16
ROWS = 48
SPANS = (96, 144, 96, 48)
VMEM = 14
MIB = 1 << 20
ROOT_2_PI = math.sqrt(2.0 / math.pi)


def launch(
    kernel, name, operands, specs, shapes, out_specs,
    grid=(1,), prefetch=0, scratch=(), aliases=None, needs=(), carried=(),
):
    n_in, n_out = len(operands), len(shapes)
    first_carried = n_in + len(needs)
    n_all = first_carried + len(carried)
    anywhere = pl.BlockSpec(memory_space=pl.ANY)
    aliases = dict(aliases or {})
    for k in range(len(carried)):
        aliases[first_carried + k] = n_out + k

    def wrapped(*refs):
        rest = refs[n_all + n_out + len(carried) :]
        kernel(*refs[:n_in], *refs[n_all : n_all + n_out], *rest)

    out = pl.pallas_call(
        wrapped,
        grid_spec=pltpu.PrefetchScalarGridSpec(
            num_scalar_prefetch=prefetch,
            grid=grid,
            in_specs=[*specs, *[anywhere] * (len(needs) + len(carried))],
            out_specs=[*out_specs, *[anywhere] * len(carried)],
            scratch_shapes=scratch,
        ),
        out_shape=[
            *shapes, *[jax.ShapeDtypeStruct(c.shape, c.dtype) for c in carried]
        ],
        input_output_aliases=aliases,
        compiler_params=pltpu.CompilerParams(vmem_limit_bytes=VMEM * MIB),
        cost_estimate=pl.CostEstimate(flops=1, bytes_accessed=1, transcendentals=0),
        name=name,
    )(*operands, *needs, *carried)
    return list(out)


def array(shape, dtype):
    return jax.ShapeDtypeStruct(shape, dtype)


def rows_of(rows, width, skip=0):
    return pl.BlockSpec((rows, width), lambda i, *_: (i + skip, 0))


def whole(*shape):
    return pl.BlockSpec(shape, lambda i, *_: (0,) * len(shape))


def lanes(shape):
    return lax.broadcasted_iota(jnp.int32, shape, 1)


def spread_scales(scales, tile, rows):
    part = scales[:, : 128] if tile < 32 else scales[:, 128 : 256]
    at = lanes((rows, 128)) // 32 + 4 * (tile % 32)
    return jnp.take_along_axis(part, at, axis=1)


def message_kernel(codes_ref, scales_ref, base_ref, ids_ref, out_ref):
    rows = codes_ref.shape[0]
    scales = jnp.concatenate(
        [scales_ref[...].astype(F32), jnp.zeros((rows, 64), F32)], axis=1
    )
    picks = (ids_ref[...] == lanes((rows, 32))).astype(BF16)
    lane = lanes((rows, 128))
    for block in range(16):
        words = codes_ref[:, block * 128 : (block + 1) * 128]
        base = jnp.dot(
            picks, base_ref[:, block * 384 : (block + 1) * 384], preferred_element_type=F32
        )
        for j in range(3):
            spot = lane + 128 * j
            word = jnp.take_along_axis(words, spot // 3, axis=1)
            code = jnp.right_shift(word, (spot % 3) * 4) & 15
            step = spread_scales(scales, block * 3 + j, rows)
            value = base[:, j * 128 : (j + 1) * 128] + step * (code - 8).astype(F32)
            out_ref[:, (block * 3 + j) * 128 : (block * 3 + j + 1) * 128] = value.astype(BF16)


def make_message(codes, scales, base, ids, first, count):
    skip = first // ROWS
    return launch(
        message_kernel, "message", [codes, scales, base, ids],
        [
            rows_of(ROWS, D // 3, skip), rows_of(ROWS, D // 32, skip),
            whole(32, D), rows_of(ROWS, 1, skip),
        ],
        [array((count, D), BF16)], [rows_of(ROWS, D)], grid=(count // ROWS,),
    )[0]


def gradient_kernel(codes_ref, scales_ref, out_ref):
    rows = codes_ref.shape[0]
    scales = jnp.concatenate(
        [scales_ref[...].astype(F32), jnp.zeros((rows, 64), F32)], axis=1
    )
    for tile in range(48):
        part = slice(tile * 128, (tile + 1) * 128)
        step = spread_scales(scales, tile, rows)
        out_ref[:, part] = (step * (codes_ref[:, part].astype(F32) - 128.0)).astype(BF16)


def make_gradient(codes, scales):
    return launch(
        gradient_kernel, "gradient", [codes, scales],
        [rows_of(ROWS, D), rows_of(ROWS, D // 32)],
        [array((TOK, D), BF16)], [rows_of(ROWS, D)], grid=(TOK // ROWS,),
    )[0]


def hidden_kernel(ends, gain_ref, *refs):
    *message_refs, out_ref = refs
    step = pl.program_id(0)
    start = 0
    for end, message_ref in zip(ends, message_refs):

        @pl.when((step >= start) & (step < end))
        def _(message_ref=message_ref):
            x = message_ref[...].astype(F32)
            center = x - jnp.sum(x, axis=1, keepdims=True) * (1.0 / D)
            variance = jnp.sum(center * center, axis=1, keepdims=True) * (1.0 / D)
            out_ref[...] = (gain_ref[...] * center * lax.rsqrt(variance + 1e-05)).astype(BF16)

        start = end


def make_hidden(messages, gain):
    specs, ends, start = [], [], 0
    for message in messages:
        tiles = message.shape[0] // ROWS
        specs.append(
            pl.BlockSpec(
                (ROWS, D), lambda i, a=start, n=tiles: (jnp.clip(i - a, 0, n - 1), 0)
            )
        )
        start += tiles
        ends.append(start)
    return launch(
        functools.partial(hidden_kernel, tuple(ends)), "hidden", [gain, *messages],
        [whole(1, D), *specs],
        [array((TOK, D), BF16)], [rows_of(ROWS, D)], grid=(TOK // ROWS,),
    )[0]


def tanh_of(pre):
    return jnp.tanh(ROOT_2_PI * (pre + 0.044715 * (pre * pre * pre)))


def down_kernel(hidden_ref, weight_ref, pre_ref, act_ref):
    pre = jnp.dot(hidden_ref[...], weight_ref[...], preferred_element_type=F32)
    pre_ref[...] = pre
    act_ref[...] = (0.5 * pre * (1.0 + tanh_of(pre))).astype(BF16)


def project_down(hidden, weight, **ties):
    rows = TOK // 2
    return launch(
        down_kernel, "down", [hidden, weight],
        [rows_of(rows, D), whole(D, R)],
        [array((TOK, R), F32), array((TOK, R), BF16)], [rows_of(rows, R)] * 2, grid=(2,), **ties,
    )


def back_kernel(grad_ref, weight_ref, out_ref):
    out_ref[...] = jnp.dot(
        grad_ref[...], weight_ref[...], preferred_element_type=F32
    ).astype(BF16)


def project_back(grad, weight, **ties):
    rows = TOK // 2
    return launch(
        back_kernel, "back", [grad, weight],
        [rows_of(rows, D), whole(D, R)],
        [array((TOK, R), BF16)], [rows_of(rows, R)], grid=(2,), **ties,
    )


def transposed(left, right):
    return lax.dot_general(left, right, (((0,), (0,)), ((), ())), preferred_element_type=F32)


def store_partial(total, kept_ref, sent_ref):
    step = pl.program_id(0)

    @pl.when(step < 4)
    def _():
        kept_ref[0] = total

    @pl.when(step >= 4)
    def _():
        sent_ref[0] = total.astype(BF16)


def grad_up_kernel(order_ref, wide_ref, act_ref, kept_ref, sent_ref):
    store_partial(transposed(act_ref[...], wide_ref[...]), kept_ref, sent_ref)


def grad_down_kernel(order_ref, wide_ref, pre_ref, dact_ref, kept_ref, sent_ref, dpre_ref):
    @pl.when(pl.program_id(0) == 0)
    def _():
        pre = pre_ref[...]
        t = tanh_of(pre)
        slope = 0.5 * (1.0 + t) + (0.5 * ROOT_2_PI) * pre * (1.0 - t * t) * (
            1.0 + (3.0 * 0.044715) * (pre * pre)
        )
        dpre_ref[...] = (dact_ref[...].astype(F32) * slope).astype(BF16)

    store_partial(transposed(dpre_ref[...], wide_ref[...]), kept_ref, sent_ref)


def partial_grad(kernel, name, order, wide, *narrow, **ties):
    return launch(
        kernel, name, [order, wide, *narrow],
        [
            pl.BlockSpec((TOK, PIECE), lambda i, order: (0, order[i])),
            *[whole(TOK, R)] * len(narrow),
        ],
        [array((4, R, PIECE), F32), array((4, R, PIECE), BF16)],
        [
            pl.BlockSpec((1, R, PIECE), lambda i, order: (jnp.minimum(i, 3), 0, 0)),
            pl.BlockSpec((1, R, PIECE), lambda i, order: (jnp.maximum(i - 4, 0), 0, 0)),
        ],
        grid=(8,), prefetch=1, **ties,
    )


def halve_kernel(kept_ref, came_ref, keep_ref, send_ref):
    keep_ref[...] = kept_ref[:2] + came_ref[:2].astype(F32)
    send_ref[...] = (kept_ref[2:] + came_ref[2:].astype(F32)).astype(BF16)


def halve(kept, came, **ties):
    return launch(
        halve_kernel, "halve", [kept, came], [whole(4, R, PIECE)] * 2,
        [array((2, R, PIECE), F32), array((2, R, PIECE), BF16)], [whole(2, R, PIECE)] * 2,
        **ties,
    )


def split_kernel(kept_ref, came_ref, *out_refs):
    for half, out_ref in enumerate(out_refs):
        out_ref[...] = (kept_ref[half] + came_ref[half].astype(F32)).astype(BF16)


def split(kept, came, **ties):
    return launch(
        split_kernel, "split", [kept, came], [whole(2, R, PIECE)] * 2,
        [array((R, PIECE), BF16)] * 2, [whole(R, PIECE)] * 2, **ties,
    )


def finish_kernel(*refs):
    *in_refs, out_ref = refs
    total = in_refs[0][...].astype(F32)
    for ref in in_refs[1:]:
        total += ref[...].astype(F32)
    out_ref[...] = total.T


def finish(parts):
    return launch(
        finish_kernel, "finish", parts, [whole(R, PIECE)] * len(parts),
        [array((PIECE, R), F32)], [whole(PIECE, R)],
    )[0]


def feedback_kernel(x_ref, own_ref, act_ref, weight_ref, out_ref, done_ref):
    done_ref[...] = jnp.zeros_like(done_ref)
    act = act_ref[...]
    for part in range(4):
        at = slice(part * QUARTER, (part + 1) * QUARTER)
        lifted = lax.dot_general(
            act, weight_ref[at, :], (((1,), (1,)), ((), ())), preferred_element_type=F32
        )
        value = x_ref[:, at].astype(F32) + lifted - own_ref[:, at].astype(F32)
        out_ref[:, at] = value.astype(BF16)


def make_feedback(x, own, act, weight, first, before):
    skip = first // ROWS
    shape = array((TOK, D), BF16)
    operands = [x, own, act, weight]
    specs = [rows_of(ROWS, D), rows_of(ROWS, D), rows_of(ROWS, R, skip), whole(D, R)]
    kernel, aliases = feedback_kernel, {}
    if before is not None:
        operands, aliases = [*operands, before], {4: 0}
        specs = [*specs, pl.BlockSpec(memory_space=pl.ANY)]

        def kernel(x_ref, own_ref, act_ref, weight_ref, before_ref, out_ref, done_ref):
            feedback_kernel(x_ref, own_ref, act_ref, weight_ref, out_ref, done_ref)

    return launch(
        kernel, "feedback", operands, specs, [shape, array((8, 128), F32)],
        [rows_of(ROWS, D, skip), whole(8, 128)],
        grid=(x.shape[0] // ROWS,), aliases=aliases,
    )


def body(
    forward_codes,
    forward_scales,
    stored_base,
    sample_ids,
    backward_codes,
    backward_scales,
    norm_gain,
    w_down,
    w_up,
):
    sections = lax.axis_size("section")
    replicas = lax.axis_size("dp")
    across = replicas // 2
    both = ("section", "dp")

    def along(value, distance):
        pairs = [(s, (s + distance) % sections) for s in range(sections)]
        return lax.ppermute(value, "section", pairs)

    def among(value, flip_x, flip_y=0, section_step=0):
        pairs = []
        for s in range(sections):
            for d in range(replicas):
                y, x = divmod(d, across)
                source = (y ^ flip_y) * across + (x ^ flip_x)
                goal = ((s + section_step) % sections) * replicas + d
                pairs.append((s * replicas + source, goal))
        return lax.ppermute(value, both, pairs)

    replica = lax.axis_index("dp")
    x_at, y_at = replica % across, replica // across

    def order_of(flips):
        return jnp.stack(
            [((y_at ^ half) * across + (x_at ^ flip)) for flip in flips for half in range(2)]
        ).astype(jnp.int32)

    up = w_up[0]
    up_before = along(up, 1)
    down_next = along(w_down[0], -1)
    gain_next = along(norm_gain, -1)

    codes, scales, base = forward_codes[0], forward_scales[0], stored_base[0]
    ids = sample_ids.reshape(TOK, 1)
    firsts = [sum(SPANS[:k]) for k in range(len(SPANS))]
    messages = [make_message(codes, scales, base, ids, a, n) for a, n in zip(firsts, SPANS)]
    gradient = make_gradient(backward_codes[0], backward_scales[0])
    hidden = make_hidden(messages, gain_next)

    pre_next, act_next = project_down(hidden, down_next, needs=[up_before])
    act_before = along(act_next, 2)
    act_own = along(act_next, 1)
    arrived0 = along(messages[0], 1)
    dact_before = project_back(gradient, up_before, needs=[act_next])[0]
    dact_next = along(dact_before, -2)

    def feedback_of(own, x, at, before):
        return make_feedback(x, own, act_own, up, firsts[at], before)

    up_kept, up_sent, message1, message2 = partial_grad(
        grad_up_kernel, "grad_up", order_of((0, 1, 3, 2)), gradient, act_before,
        needs=[act_own, arrived0, dact_next], carried=messages[1:3],
    )
    arrived1 = along(message1, 1)
    arrived2 = along(message2, 1)
    down_kept, down_sent = partial_grad(
        grad_down_kernel, "grad_down", order_of((0, 3, 1, 2)), hidden, pre_next, dact_next,
        scratch=[pltpu.VMEM((TOK, R), BF16)],
    )
    feedback, done = feedback_of(messages[0], arrived0, 0, None)
    up_kept, up_sent, message3 = halve(
        up_kept, among(up_sent, 3), needs=[arrived1, done], carried=messages[3:4]
    )
    arrived3 = along(message3, 1)
    down_kept, down_sent = halve(down_kept, among(down_sent, 1))
    feedback, done = feedback_of(message1, arrived1, 1, feedback)
    up_parts = split(up_kept, among(up_sent, 1), needs=[arrived2, done])
    down_parts = split(down_kept, among(down_sent, 3))
    grad_up = finish([among(up_parts[half], 0, half, -1) for half in range(2)])
    grad_down = finish([among(down_parts[half], 0, half, 1) for half in range(2)])
    feedback, _ = feedback_of(message2, arrived2, 2, feedback)
    feedback, _ = feedback_of(message3, arrived3, 3, feedback)
    return (feedback[None], grad_down[None], grad_up[None])


def solution(mesh):
    in_specs = (
        P("section", "dp", None),
        P("section", "dp", None),
        P("section", "dp", None),
        P("section", "dp"),
        P("section", "dp", None),
        P("section", "dp", None),
        P("section", None),
        P("section", None, None),
        P("section", None, None),
    )
    out_specs = (P("section", "dp", None), P("section", "dp", None), P("section", "dp", None))
    return jax.shard_map(body, mesh=mesh, in_specs=in_specs, out_specs=out_specs, check_vma=False)
```

```python
import functools
import math

import jax
import jax.numpy as jnp
from jax import lax
from jax.experimental import pallas as pl
from jax.experimental.pallas import tpu as pltpu
from jax.sharding import PartitionSpec as P

D = 6144
R = 128
TOK = 384
PIECE = D // 8
F32 = jnp.float32
BF16 = jnp.bfloat16
TILE = 48
SPANS = (96, 144, 96, 48)
MIB = 1 << 20
ROOT_2_PI = math.sqrt(2.0 / math.pi)
HBM = pl.BlockSpec(memory_space=pltpu.HBM)
VMEM = pl.BlockSpec(memory_space=pltpu.VMEM)
SMEM = pl.BlockSpec(memory_space=pltpu.SMEM)
ANY = pl.BlockSpec(memory_space=pl.ANY)


def array(shape, dtype):
    return jax.ShapeDtypeStruct(shape, dtype)


def launch(kernel, name, ins, outs, scratch=(), aliases=None, needs=(), carried=(), grant=63):
    n_in, n_out = len(ins), len(outs)
    first_carried = n_in + len(needs)
    n_all = first_carried + len(carried)
    aliases = dict(aliases or {})
    for k in range(len(carried)):
        aliases[first_carried + k] = n_out + k

    def wrapped(*refs):
        rest = refs[n_all + n_out + len(carried) :]
        kernel(*refs[:n_in], *refs[n_all : n_all + n_out], *rest)

    return pl.pallas_call(
        wrapped,
        in_specs=[where for _, where in ins] + [ANY] * (len(needs) + len(carried)),
        out_specs=[where for _, where in outs] + [ANY] * len(carried),
        out_shape=[out for out, _ in outs] + [array(c.shape, c.dtype) for c in carried],
        scratch_shapes=scratch,
        input_output_aliases=aliases,
        compiler_params=pltpu.CompilerParams(vmem_limit_bytes=grant * MIB),
        cost_estimate=pl.CostEstimate(flops=1, bytes_accessed=1, transcendentals=0),
        name=name,
    )(*[value for value, _ in ins], *needs, *carried)


def sems(count):
    return pltpu.SemaphoreType.DMA((count,))


def tile_at(i, base=0):
    return pl.ds(pl.multiple_of(base + i * TILE, 16), TILE)


def lanes(shape):
    return lax.broadcasted_iota(jnp.int32, shape, 1)


def spread_scales(scales_ref, rows, tile):
    half, at = divmod(tile, 32)
    part = scales_ref[rows, half * 128 : half * 128 + 128]
    return jnp.take_along_axis(part, lanes((TILE, 128)) // 32 + 4 * at, axis=1)


def turn_scales(scales_ref, turned_ref):
    turned_ref[:, : D // 32] = scales_ref[...].astype(F32).T


def message_kernel(
    first, spans, codes_hbm, scales_hbm, base_hbm, ids_hbm, *refs
):
    n = len(spans)
    out_hbms, stats_hbm = refs[:n], refs[n]
    (codes_ref, scales_ref, base_ref, ids_ref, turned_ref, picks_ref, out_ref, stats_ref,
     code_sems, in_sems, out_sems, stats_sem) = refs[n + 1 :]
    count = sum(spans)
    tiles = count // TILE
    small = [
        pltpu.make_async_copy(src, dst, in_sems.at[k])
        for k, (src, dst) in enumerate(
            ((scales_hbm, scales_ref), (ids_hbm, ids_ref), (base_hbm, base_ref))
        )
    ]

    def codes_copy(i):
        return pltpu.make_async_copy(
            codes_hbm.at[tile_at(i, first)], codes_ref.at[tile_at(i)], code_sems.at[i]
        )

    def out_copy(i, out_hbm, start):
        return pltpu.make_async_copy(
            out_ref.at[tile_at(i)], out_hbm.at[tile_at(i, -start)], out_sems.at[i]
        )

    for copy in small:
        copy.start()
    for i in range(tiles):
        codes_copy(i).start()
    for copy in small:
        copy.wait()
    turn_scales(scales_ref, turned_ref)
    hits = lax.broadcasted_iota(jnp.int32, (32, TOK), 0) == ids_ref[...]
    picks_ref[...] = hits.astype(F32).T.astype(BF16)
    lane = lanes((TILE, 128))
    bounds = [sum(spans[:k]) for k in range(n + 1)]

    def one_tile(i, carry):
        codes_copy(i).wait()
        here, rows = tile_at(i), tile_at(i, first)
        picks = picks_ref[rows, :]
        total = jnp.zeros((TILE, 128), F32)
        for block in range(16):
            words = codes_ref[here, block * 128 : (block + 1) * 128]
            base = jnp.dot(
                picks, base_ref[:, block * 384 : (block + 1) * 384], preferred_element_type=F32
            )
            for j in range(3):
                spot = lane + 128 * j
                word = jnp.take_along_axis(words, spot // 3, axis=1)
                code = jnp.right_shift(word, (spot % 3) * 4) & 15
                tile = block * 3 + j
                step = spread_scales(turned_ref, rows, tile)
                value = base[:, j * 128 : (j + 1) * 128] + step * (code - 8).astype(F32)
                value = value.astype(BF16)
                out_ref[here, tile * 128 : (tile + 1) * 128] = value
                total += value.astype(F32)
        for out_hbm, start, end in zip(out_hbms, bounds, bounds[1:]):

            @pl.when((i >= start // TILE) & (i < end // TILE))
            def _(out_hbm=out_hbm, start=start):
                out_copy(i, out_hbm, start).start()

        mean = jnp.sum(total, axis=1, keepdims=True) * (1.0 / D)
        total = jnp.zeros((TILE, 128), F32)
        for tile in range(48):
            center = out_ref[here, tile * 128 : (tile + 1) * 128].astype(F32) - mean
            total += center * center
        variance = jnp.sum(total, axis=1, keepdims=True) * (1.0 / D)
        stats_ref[here, :128] = jnp.broadcast_to(mean, (TILE, 128))
        stats_ref[here, 128:] = jnp.broadcast_to(lax.rsqrt(variance + 1e-05), (TILE, 128))
        return carry

    lax.fori_loop(0, tiles, one_tile, 0)
    stats_copy = pltpu.make_async_copy(stats_ref, stats_hbm, stats_sem.at[0])
    stats_copy.start()
    for out_hbm, start, end in zip(out_hbms, bounds, bounds[1:]):
        for i in range(start // TILE, end // TILE):
            out_copy(i, out_hbm, start).wait()
    stats_copy.wait()


def make_messages(codes, scales, base, ids, first, spans, **ties):
    count = sum(spans)
    return launch(
        functools.partial(message_kernel, first, spans), "message",
        [(codes, HBM), (scales, HBM), (base, HBM), (ids, HBM)],
        [(array((span, D), BF16), HBM) for span in spans] + [(array((count, 256), F32), HBM)],
        [
            pltpu.VMEM((count, D // 3), jnp.int32), pltpu.VMEM((D // 32, TOK), BF16),
            pltpu.VMEM((32, D), BF16), pltpu.VMEM((1, TOK), jnp.int32),
            pltpu.VMEM((TOK, 256), F32), pltpu.VMEM((TOK, 32), BF16),
            pltpu.VMEM((count, D), BF16), pltpu.VMEM((count, 256), F32),
            sems(count // TILE), sems(3), sems(count // TILE), sems(1),
        ],
        **ties,
    )


def gradient_kernel(
    codes_hbm, scales_hbm, out_hbm,
    codes_ref, scales_ref, turned_ref, out_ref, code_sems, in_sem, out_sems,
):
    tiles = TOK // TILE
    scales_copy = pltpu.make_async_copy(scales_hbm, scales_ref, in_sem.at[0])
    scales_copy.start()

    def codes_copy(i):
        return pltpu.make_async_copy(
            codes_hbm.at[tile_at(i)], codes_ref.at[tile_at(i)], code_sems.at[i]
        )

    def out_copy(i):
        return pltpu.make_async_copy(
            out_ref.at[:, tile_at(i)], out_hbm.at[:, tile_at(i)], out_sems.at[i]
        )

    for i in range(tiles):
        codes_copy(i).start()
    scales_copy.wait()
    turn_scales(scales_ref, turned_ref)

    def one_tile(i, carry):
        codes_copy(i).wait()
        rows = tile_at(i)
        for tile in range(48):
            step = spread_scales(turned_ref, rows, tile)
            codes = codes_ref[rows, tile * 128 : (tile + 1) * 128].astype(F32)
            piece, at = divmod(tile, 6)
            out_ref[piece, rows, at * 128 : (at + 1) * 128] = (step * (codes - 128.0)).astype(
                BF16
            )
        out_copy(i).start()
        return carry

    lax.fori_loop(0, tiles, one_tile, 0)
    for i in range(tiles):
        out_copy(i).wait()


def make_gradient(codes, scales, **ties):
    return launch(
        gradient_kernel, "gradient", [(codes, HBM), (scales, HBM)],
        [(array((8, TOK, PIECE), BF16), HBM)],
        [
            pltpu.VMEM((TOK, D), BF16), pltpu.VMEM((D // 32, TOK), BF16),
            pltpu.VMEM((TOK, 256), F32), pltpu.VMEM((8, TOK, PIECE), BF16),
            sems(TOK // TILE), sems(1), sems(TOK // TILE),
        ],
        **ties,
    )[0]


def tanh_of(pre):
    return jnp.tanh(ROOT_2_PI * (pre + 0.044715 * (pre * pre * pre)))


def down_kernel(spans, n_stats, weight_hbm, gain_ref, *refs):
    n = len(spans)
    message_hbms, stats_hbms = refs[:n], refs[n : n + n_stats]
    (pre_ref, act_ref, hidden_hbm, message_ref, stats_ref, weight_ref, hidden_ref,
     message_sems, stats_sems, weight_sems, out_sems) = refs[n + n_stats :]
    bounds = [sum(spans[:k]) for k in range(n + 1)]
    stats_copies, row = [], 0
    for k, stats_hbm in enumerate(stats_hbms):
        count = stats_hbm.shape[0]
        stats_copies.append(
            pltpu.make_async_copy(
                stats_hbm, stats_ref.at[pl.ds(row, count)], stats_sems.at[k]
            )
        )
        row += count
    copies = []
    for p in range(8):
        columns = pl.ds(p * PIECE, PIECE)
        copies.append([
            pltpu.make_async_copy(
                weight_hbm.at[columns], weight_ref.at[columns], weight_sems.at[p]
            )
        ] + [
            pltpu.make_async_copy(
                hbm.at[:, columns], message_ref.at[p, pl.ds(start, span)],
                message_sems.at[p * n + k],
            )
            for k, (hbm, start, span) in enumerate(zip(message_hbms, bounds, spans))
        ])
    for copy in stats_copies + [c for group in copies for c in group]:
        copy.start()
    for copy in stats_copies:
        copy.wait()
    out_copies = []
    for p in range(8):
        for copy in copies[p]:
            copy.wait()
        columns = slice(p * PIECE, (p + 1) * PIECE)
        for t in range(TOK // TILE):
            rows = slice(t * TILE, (t + 1) * TILE)
            for c in range(PIECE // 128):
                at = slice(c * 128, (c + 1) * 128)
                center = message_ref[p, rows, at].astype(F32) - stats_ref[rows, :128]
                gain = gain_ref[:, p * PIECE + c * 128 : p * PIECE + (c + 1) * 128]
                hidden_ref[p, rows, at] = (gain * center * stats_ref[rows, 128:]).astype(BF16)
        copy = pltpu.make_async_copy(hidden_ref.at[p], hidden_hbm.at[p], out_sems.at[p])
        copy.start()
        out_copies.append(copy)
        part = jnp.dot(hidden_ref[p], weight_ref[columns, :], preferred_element_type=F32)
        if p == 0:
            pre_ref[...] = part
        else:
            pre_ref[...] += part
    pre = pre_ref[...]
    act_ref[...] = (0.5 * pre * (1.0 + tanh_of(pre))).astype(BF16)
    for copy in out_copies:
        copy.wait()


def project_down(messages, stats, gain, weight, **ties):
    spans = tuple(m.shape[0] for m in messages)
    return launch(
        functools.partial(down_kernel, spans, len(stats)), "down",
        [(weight, HBM), (gain, VMEM)] + [(v, HBM) for v in (*messages, *stats)],
        [
            (array((TOK, R), F32), VMEM), (array((TOK, R), BF16), VMEM),
            (array((8, TOK, PIECE), BF16), HBM),
        ],
        [
            pltpu.VMEM((8, TOK, PIECE), BF16), pltpu.VMEM((TOK, 256), F32),
            pltpu.VMEM((D, R), BF16), pltpu.VMEM((8, TOK, PIECE), BF16),
            sems(8 * len(spans)), sems(len(stats)), sems(8), sems(8),
        ],
        **ties,
    )


def back_kernel(grad_hbm, weight_hbm, out_ref, grad_ref, weight_ref, grad_sems, weight_sems):
    copies = []
    for p in range(8):
        columns = pl.ds(p * PIECE, PIECE)
        copies.append((
            pltpu.make_async_copy(
                weight_hbm.at[columns], weight_ref.at[columns], weight_sems.at[p]
            ),
            pltpu.make_async_copy(grad_hbm.at[p], grad_ref.at[p], grad_sems.at[p]),
        ))
    for group in copies:
        for copy in group:
            copy.start()
    total = jnp.zeros((TOK, R), F32)
    for p in range(8):
        for copy in copies[p]:
            copy.wait()
        total += jnp.dot(
            grad_ref[p], weight_ref[p * PIECE : (p + 1) * PIECE, :], preferred_element_type=F32
        )
    out_ref[...] = total.astype(BF16)


def project_back(grad, weight, **ties):
    return launch(
        back_kernel, "back", [(grad, HBM), (weight, HBM)], [(array((TOK, R), BF16), VMEM)],
        [pltpu.VMEM((8, TOK, PIECE), BF16), pltpu.VMEM((D, R), BF16), sems(8), sems(8)],
        **ties,
    )


def transposed(left, right):
    return lax.dot_general(left, right, (((0,), (0,)), ((), ())), preferred_element_type=F32)


def grad_kernel(narrow_of, order_ref, wide_hbm, *refs):
    (*narrow_refs, kept_hbm, sent_hbm,
     wide_ref, kept_ref, sent_ref, wide_sems, out_sems) = refs
    copies = [
        pltpu.make_async_copy(wide_hbm.at[order_ref[i]], wide_ref.at[i], wide_sems.at[i])
        for i in range(8)
    ]
    for copy in copies:
        copy.start()
    narrow = narrow_of(*narrow_refs)
    out_copies = []
    for i, copy in enumerate(copies):
        copy.wait()
        total = transposed(narrow, wide_ref[i])
        if i < 4:
            sent_ref[i] = total.astype(BF16)
            pair = sent_ref.at[i], sent_hbm.at[i]
        else:
            kept_ref[i - 4] = total
            pair = kept_ref.at[i - 4], kept_hbm.at[i - 4]
        out_copies.append(pltpu.make_async_copy(*pair, out_sems.at[i]))
        out_copies[-1].start()
    for copy in out_copies:
        copy.wait()


def read_act(act_ref):
    return act_ref[...]


def make_dpre(pre_ref, dact_ref):
    pre = pre_ref[...]
    t = tanh_of(pre)
    slope = 0.5 * (1.0 + t) + (0.5 * ROOT_2_PI) * pre * (1.0 - t * t) * (
        1.0 + (3.0 * 0.044715) * (pre * pre)
    )
    return (dact_ref[...].astype(F32) * slope).astype(BF16)


def partial_grad(narrow_of, name, order, wide, *narrow, **ties):
    return launch(
        functools.partial(grad_kernel, narrow_of), name,
        [(order, SMEM), (wide, HBM)] + [(value, VMEM) for value in narrow],
        [(array((4, R, PIECE), F32), HBM), (array((4, R, PIECE), BF16), HBM)],
        [
            pltpu.VMEM((8, TOK, PIECE), BF16), pltpu.VMEM((4, R, PIECE), F32),
            pltpu.VMEM((4, R, PIECE), BF16), sems(8), sems(8),
        ],
        **ties,
    )


def halve_kernel(kept_ref, came_ref, keep_ref, send_ref):
    keep_ref[...] = kept_ref[:2] + came_ref[:2].astype(F32)
    send_ref[...] = (kept_ref[2:] + came_ref[2:].astype(F32)).astype(BF16)


def halve(kept, came, **ties):
    return launch(
        halve_kernel, "halve", [(kept, VMEM), (came, VMEM)],
        [(array((2, R, PIECE), F32), VMEM), (array((2, R, PIECE), BF16), VMEM)], grant=8, **ties,
    )


def split_kernel(kept_ref, came_ref, *out_refs):
    for half, out_ref in enumerate(out_refs):
        out_ref[...] = (kept_ref[half] + came_ref[half].astype(F32)).astype(BF16)


def split(kept, came, **ties):
    return launch(
        split_kernel, "split", [(kept, VMEM), (came, VMEM)],
        [(array((R, PIECE), BF16), VMEM)] * 2, grant=8, **ties,
    )


def finish_kernel(one_ref, two_ref, out_ref):
    out_ref[...] = (one_ref[...].astype(F32) + two_ref[...].astype(F32)).T


def finish(parts):
    return pl.pallas_call(
        finish_kernel,
        out_shape=array((PIECE, R), F32),
        in_specs=[VMEM] * 2,
        cost_estimate=pl.CostEstimate(flops=1, bytes_accessed=1, transcendentals=0),
        name="finish",
    )(*parts)


def feedback_kernel(
    first, count, x_hbm, own_hbm, act_ref, weight_hbm, *refs
):
    (out_hbm, done_ref, x_ref, own_ref, out_ref, weight_ref,
     x_sems, own_sems, out_sems, weight_sems) = refs[-10:]
    done_ref[...] = jnp.zeros_like(done_ref)
    weight_copies = []
    for part in range(8):
        at = pl.ds(part * PIECE, PIECE)
        weight_copies.append(
            pltpu.make_async_copy(weight_hbm.at[at], weight_ref.at[at], weight_sems.at[part])
        )
    copies = []
    for i in range(count // TILE):
        rows = pl.ds(i * TILE, TILE)
        copies.append((
            pltpu.make_async_copy(x_hbm.at[rows], x_ref.at[rows], x_sems.at[i]),
            pltpu.make_async_copy(own_hbm.at[rows], own_ref.at[rows], own_sems.at[i]),
        ))
    for copy in [*copies[0], *weight_copies, *(c for group in copies[1:] for c in group)]:
        copy.start()
    out_copies = []
    for i in range(count // TILE):
        for copy in copies[i]:
            copy.wait()
        rows = slice(i * TILE, (i + 1) * TILE)
        act = act_ref[first + i * TILE : first + (i + 1) * TILE, :]
        for part in range(8):
            at = slice(part * PIECE, (part + 1) * PIECE)
            if i == 0:
                weight_copies[part].wait()
            lifted = lax.dot_general(
                act, weight_ref[at, :], (((1,), (1,)), ((), ())), preferred_element_type=F32
            )
            value = x_ref[rows, at].astype(F32) + lifted - own_ref[rows, at].astype(F32)
            out_ref[rows, at] = value.astype(BF16)
        copy = pltpu.make_async_copy(
            out_ref.at[pl.ds(i * TILE, TILE)],
            out_hbm.at[pl.ds(first + i * TILE, TILE)],
            out_sems.at[i],
        )
        copy.start()
        out_copies.append(copy)
    for copy in out_copies:
        copy.wait()


def make_feedback(x, own, act, weight, first, before):
    count = x.shape[0]
    ins = [(x, HBM), (own, HBM), (act, VMEM), (weight, HBM)]
    if before is not None:
        ins.append((before, HBM))
    return launch(
        functools.partial(feedback_kernel, first, count), "feedback", ins,
        [(array((TOK, D), BF16), HBM), (array((8, 128), F32), VMEM)],
        [pltpu.VMEM((count, D), BF16)] * 3
        + [pltpu.VMEM((D, R), BF16)] + [sems(count // TILE)] * 3 + [sems(8)],
        aliases={} if before is None else {4: 0},
    )


def body(
    forward_codes,
    forward_scales,
    stored_base,
    sample_ids,
    backward_codes,
    backward_scales,
    norm_gain,
    w_down,
    w_up,
):
    sections = lax.axis_size("section")
    replicas = lax.axis_size("dp")
    across = replicas // 2
    both = ("section", "dp")

    def along(value, distance):
        pairs = [(s, (s + distance) % sections) for s in range(sections)]
        return lax.ppermute(value, "section", pairs)

    def among(value, flip_x, flip_y=0, section_step=0):
        pairs = []
        for s in range(sections):
            for d in range(replicas):
                y, x = divmod(d, across)
                source = (y ^ flip_y) * across + (x ^ flip_x)
                goal = ((s + section_step) % sections) * replicas + d
                pairs.append((s * replicas + source, goal))
        return lax.ppermute(value, both, pairs)

    replica = lax.axis_index("dp")
    x_at, y_at = replica % across, replica // across

    def order_of(flips):
        return jnp.stack(
            [((y_at ^ half) * across + (x_at ^ flip)) for flip in flips for half in range(2)]
        ).astype(jnp.int32)

    up = w_up[0]
    up_before = along(up, 1)
    down_next = along(w_down[0], -1)
    gain_next = along(norm_gain, -1)

    codes, base = forward_codes[0], stored_base[0]
    scales = forward_scales[0].T
    firsts = [sum(SPANS[:k]) for k in range(len(SPANS))]
    message0, stats0 = make_messages(codes, scales, base, sample_ids, 0, SPANS[:1])
    *later, stats1 = make_messages(
        codes, scales, base, sample_ids, SPANS[0], SPANS[1:], needs=[stats0]
    )
    messages = [message0, *later]
    gradient = make_gradient(backward_codes[0], backward_scales[0].T, needs=[stats1])

    pre_next, act_next, hidden = project_down(
        messages, [stats0, stats1], gain_next, down_next, needs=[up_before, gradient]
    )
    act_before = along(act_next, 2)
    act_own = along(act_next, 1)
    arrived0 = along(messages[0], 1)
    dact_before = project_back(gradient, up_before, needs=[act_next])[0]
    dact_next = along(dact_before, -2)

    def feedback_of(own, x, at, before):
        return make_feedback(x, own, act_own, up, firsts[at], before)

    up_kept, up_sent, message1, message2 = partial_grad(
        read_act, "grad_up", order_of((3, 2, 0, 1)), gradient, act_before,
        needs=[act_own, arrived0, dact_next], carried=messages[1:3],
    )
    arrived1 = along(message1, 1)
    arrived2 = along(message2, 1)
    down_kept, down_sent = partial_grad(
        make_dpre, "grad_down", order_of((1, 2, 0, 3)), hidden, pre_next, dact_next,
    )
    feedback, done = feedback_of(messages[0], arrived0, 0, None)
    up_kept, up_sent, message3 = halve(
        up_kept, among(up_sent, 3), needs=[arrived1, done], carried=messages[3:4]
    )
    arrived3 = along(message3, 1)
    down_kept, down_sent = halve(down_kept, among(down_sent, 1))
    feedback, done = feedback_of(message1, arrived1, 1, feedback)
    up_parts = split(up_kept, among(up_sent, 1), needs=[arrived2, done])
    down_parts = split(down_kept, among(down_sent, 3))
    grad_up = finish([among(up_parts[half], 0, half, -1) for half in range(2)])
    grad_down = finish([among(down_parts[half], 0, half, 1) for half in range(2)])
    feedback, _ = feedback_of(message2, arrived2, 2, feedback)
    feedback, _ = feedback_of(message3, arrived3, 3, feedback)
    return (feedback[None], grad_down[None], grad_up[None])


def solution(mesh):
    in_specs = (
        P("section", "dp", None),
        P("section", "dp", None),
        P("section", "dp", None),
        P("section", "dp"),
        P("section", "dp", None),
        P("section", "dp", None),
        P("section", None),
        P("section", None, None),
        P("section", None, None),
    )
    out_specs = (P("section", "dp", None), P("section", "dp", None), P("section", "dp", None))
    return jax.shard_map(body, mesh=mesh, in_specs=in_specs, out_specs=out_specs, check_vma=False)
```

```python
import functools
import math

import jax
import jax.numpy as jnp
from jax import lax
from jax.experimental import pallas as pl
from jax.experimental.pallas import tpu as pltpu
from jax.sharding import PartitionSpec as P

D = 6144
R = 128
TOK = 384
PIECE = D // 8
F32 = jnp.float32
BF16 = jnp.bfloat16
TILE = 48
SPANS = (96, 144, 96, 48)
MIB = 1 << 20
ROOT_2_PI = math.sqrt(2.0 / math.pi)
VMEM = pl.BlockSpec(memory_space=pltpu.VMEM)
ANY = pl.BlockSpec(memory_space=pl.ANY)


def array(shape, dtype):
    return jax.ShapeDtypeStruct(shape, dtype)


def launch(
    kernel, name, ins, outs, scratch=(), grid=(), aliases=None, needs=(), carried=(), grant=14
):
    n_in, n_out = len(ins), len(outs)
    first_carried = n_in + len(needs)
    n_all = first_carried + len(carried)
    aliases = dict(aliases or {})
    for k in range(len(carried)):
        aliases[first_carried + k] = n_out + k

    def wrapped(*refs):
        rest = refs[n_all + n_out + len(carried) :]
        kernel(*refs[:n_in], *refs[n_all : n_all + n_out], *rest)

    return pl.pallas_call(
        wrapped,
        grid=grid,
        in_specs=[spec for _, spec in ins] + [ANY] * (len(needs) + len(carried)),
        out_specs=[spec for _, spec in outs] + [ANY] * len(carried),
        out_shape=[out for out, _ in outs] + [array(c.shape, c.dtype) for c in carried],
        scratch_shapes=scratch,
        input_output_aliases=aliases,
        compiler_params=pltpu.CompilerParams(vmem_limit_bytes=grant * MIB),
        cost_estimate=pl.CostEstimate(flops=1, bytes_accessed=1, transcendentals=0),
        name=name,
    )(*[value for value, _ in ins], *needs, *carried)


def rows_of(width, skip=0):
    return pl.BlockSpec((TILE, width), lambda i: (i + skip, 0))


def rows_between(start, end, width):
    return pl.BlockSpec((TILE, width), lambda i: (jnp.clip(i - start, 0, end - start - 1), 0))


def whole(*shape):
    return pl.BlockSpec(shape, lambda i: (0,) * len(shape))


def lanes(shape):
    return lax.broadcasted_iota(jnp.int32, shape, 1)


def spread_scales(scales_ref, rows, tile):
    half, at = divmod(tile, 32)
    part = scales_ref[rows, half * 128 : half * 128 + 128]
    return jnp.take_along_axis(part, lanes((TILE, 128)) // 32 + 4 * at, axis=1)


def turn_scales(scales_ref, turned_ref):
    turned_ref[:, : D // 32] = scales_ref[...].astype(F32).T


def tile_at(i):
    return pl.ds(pl.multiple_of(i * TILE, 16), TILE)


def message_kernel(first, bounds, codes_ref, scales_ref, base_ref, ids_ref, *refs):
    *out_refs, turned_ref, picks_ref = refs
    step = pl.program_id(0)

    @pl.when(step == 0)
    def _():
        turn_scales(scales_ref, turned_ref)
        hits = lax.broadcasted_iota(jnp.int32, (32, TOK), 0) == ids_ref[...]
        picks_ref[...] = hits.astype(F32).T.astype(BF16)

    def fill(out_ref):
        rows = tile_at(step + first // TILE)
        picks = picks_ref[rows, :]
        lane = lanes((TILE, 128))
        for block in range(16):
            words = codes_ref[:, block * 128 : (block + 1) * 128]
            base = jnp.dot(
                picks, base_ref[:, block * 384 : (block + 1) * 384], preferred_element_type=F32
            )
            for j in range(3):
                spot = lane + 128 * j
                word = jnp.take_along_axis(words, spot // 3, axis=1)
                code = jnp.right_shift(word, (spot % 3) * 4) & 15
                tile = block * 3 + j
                scale = spread_scales(turned_ref, rows, tile)
                value = base[:, j * 128 : (j + 1) * 128] + scale * (code - 8).astype(F32)
                out_ref[:, tile * 128 : (tile + 1) * 128] = value.astype(BF16)

    if len(out_refs) == 1:
        fill(out_refs[0])
        return
    for out_ref, (start, end) in zip(out_refs, bounds):

        @pl.when((step >= start) & (step < end))
        def _(out_ref=out_ref):
            fill(out_ref)


def make_messages(codes, scales, base, ids, first, spans, **ties):
    ends = [sum(spans[: k + 1]) // TILE for k in range(len(spans))]
    bounds = list(zip([0, *ends], ends))
    return launch(
        functools.partial(message_kernel, first, bounds), "message",
        [
            (codes, rows_of(D // 3, first // TILE)), (scales, whole(D // 32, TOK)),
            (base, whole(32, D)), (ids, whole(1, TOK)),
        ],
        [
            (array((span, D), BF16), rows_between(start, end, D))
            for span, (start, end) in zip(spans, bounds)
        ],
        [pltpu.VMEM((TOK, 256), F32), pltpu.VMEM((TOK, 32), BF16)],
        grid=(ends[-1],), **ties,
    )


def gradient_kernel(codes_ref, scales_ref, out_ref, turned_ref):
    step = pl.program_id(0)

    @pl.when(step == 0)
    def _():
        turn_scales(scales_ref, turned_ref)

    for tile in range(48):
        part = slice(tile * 128, (tile + 1) * 128)
        scale = spread_scales(turned_ref, tile_at(step), tile)
        out_ref[:, part] = (scale * (codes_ref[:, part].astype(F32) - 128.0)).astype(BF16)


def make_gradient(codes, scales, **ties):
    return launch(
        gradient_kernel, "gradient",
        [(codes, rows_of(D)), (scales, whole(D // 32, TOK))],
        [(array((TOK, D), BF16), rows_of(D))], [pltpu.VMEM((TOK, 256), F32)],
        grid=(TOK // TILE,), **ties,
    )[0]


def hidden_kernel(bounds, gain_ref, *refs):
    *message_refs, out_ref = refs
    step = pl.program_id(0)
    for message_ref, (start, end) in zip(message_refs, bounds):

        @pl.when((step >= start) & (step < end))
        def _(message_ref=message_ref):
            x = message_ref[...].astype(F32)
            center = x - jnp.sum(x, axis=1, keepdims=True) * (1.0 / D)
            variance = jnp.sum(center * center, axis=1, keepdims=True) * (1.0 / D)
            out_ref[...] = (gain_ref[...] * center * lax.rsqrt(variance + 1e-05)).astype(BF16)


def make_hidden(messages, gain, **ties):
    ends = [sum(m.shape[0] for m in messages[: k + 1]) // TILE for k in range(len(messages))]
    bounds = list(zip([0, *ends], ends))
    return launch(
        functools.partial(hidden_kernel, bounds), "hidden",
        [(gain, whole(1, D))]
        + [(m, rows_between(start, end, D)) for m, (start, end) in zip(messages, bounds)],
        [(array((TOK, D), BF16), rows_of(D))], grid=(TOK // TILE,), **ties,
    )[0]


def tanh_of(pre):
    return jnp.tanh(ROOT_2_PI * (pre + 0.044715 * (pre * pre * pre)))


def down_kernel(hidden_ref, weight_ref, pre_ref, act_ref):
    pre = jnp.dot(hidden_ref[...], weight_ref[...], preferred_element_type=F32)
    pre_ref[...] = pre
    act_ref[...] = (0.5 * pre * (1.0 + tanh_of(pre))).astype(BF16)


def project_down(hidden, weight, **ties):
    return launch(
        down_kernel, "down", [(hidden, VMEM), (weight, VMEM)],
        [(array((TOK, R), F32), VMEM), (array((TOK, R), BF16), VMEM)], **ties,
    )


def back_kernel(grad_ref, weight_ref, out_ref):
    out_ref[...] = jnp.dot(
        grad_ref[...], weight_ref[...], preferred_element_type=F32
    ).astype(BF16)


def project_back(grad, weight, **ties):
    return launch(
        back_kernel, "back", [(grad, VMEM), (weight, VMEM)],
        [(array((TOK, R), BF16), VMEM)], **ties,
    )


def transposed(left, right):
    return lax.dot_general(left, right, (((0,), (0,)), ((), ())), preferred_element_type=F32)


def grad_kernel(narrow_of, flips, wide_ref, *refs):
    *narrow_refs, kept_ref, sent_ref = refs
    narrow = narrow_of(*narrow_refs)
    replica = lax.axis_index("dp")
    x_at, y_at = lax.rem(replica, 4), lax.div(replica, 4)
    for i, flip in enumerate(flips):
        for half in range(2):
            piece = (y_at ^ half) * 4 + (x_at ^ flip)
            columns = pl.ds(pl.multiple_of(piece * PIECE, 128), PIECE)
            total = transposed(narrow, wide_ref[:, columns])
            if i < 2:
                kept_ref[2 * i + half] = total
            else:
                sent_ref[2 * i - 4 + half] = total.astype(BF16)


def read_act(act_ref):
    return act_ref[...]


def make_dpre(pre_ref, dact_ref):
    pre = pre_ref[...]
    t = tanh_of(pre)
    slope = 0.5 * (1.0 + t) + (0.5 * ROOT_2_PI) * pre * (1.0 - t * t) * (
        1.0 + (3.0 * 0.044715) * (pre * pre)
    )
    return (dact_ref[...].astype(F32) * slope).astype(BF16)


def partial_grad(narrow_of, name, flips, wide, *narrow, **ties):
    return launch(
        functools.partial(grad_kernel, narrow_of, flips), name,
        [(value, VMEM) for value in (wide, *narrow)],
        [(array((4, R, PIECE), F32), VMEM), (array((4, R, PIECE), BF16), VMEM)], **ties,
    )


def halve_kernel(kept_ref, came_ref, keep_ref, send_ref):
    keep_ref[...] = kept_ref[:2] + came_ref[:2].astype(F32)
    send_ref[...] = (kept_ref[2:] + came_ref[2:].astype(F32)).astype(BF16)


def halve(kept, came, **ties):
    return launch(
        halve_kernel, "halve", [(kept, VMEM), (came, VMEM)],
        [(array((2, R, PIECE), F32), VMEM), (array((2, R, PIECE), BF16), VMEM)], **ties,
    )


def split_kernel(kept_ref, came_ref, *out_refs):
    for half, out_ref in enumerate(out_refs):
        out_ref[...] = (kept_ref[half] + came_ref[half].astype(F32)).astype(BF16)


def split(kept, came, **ties):
    return launch(
        split_kernel, "split", [(kept, VMEM), (came, VMEM)],
        [(array((R, PIECE), BF16), VMEM)] * 2, **ties,
    )


def finish_kernel(one_ref, two_ref, out_ref):
    out_ref[...] = (one_ref[...].astype(F32) + two_ref[...].astype(F32)).T


def finish(parts):
    return launch(
        finish_kernel, "finish", [(part, VMEM) for part in parts],
        [(array((PIECE, R), F32), pl.BlockSpec((PIECE, R)))],
    )[0]


def feedback_kernel(first, count, before, x_ref, own_ref, act_ref, weight_ref, *refs):
    *rest, out_ref, out_sems = refs
    if before:
        rest = rest[1:]
    out_hbm = rest[0]
    for done_ref in rest[1:]:
        done_ref[...] = jnp.zeros_like(done_ref)
    copies = []
    for i in range(count // TILE):
        rows = slice(i * TILE, (i + 1) * TILE)
        act = act_ref[first + i * TILE : first + (i + 1) * TILE, :]
        for part in range(4):
            at = slice(part * 2 * PIECE, (part + 1) * 2 * PIECE)
            lifted = lax.dot_general(
                act, weight_ref[at, :], (((1,), (1,)), ((), ())), preferred_element_type=F32
            )
            value = x_ref[rows, at].astype(F32) + lifted - own_ref[rows, at].astype(F32)
            out_ref[rows, at] = value.astype(BF16)
        copies.append(
            pltpu.make_async_copy(
                out_ref.at[pl.ds(i * TILE, TILE)],
                out_hbm.at[pl.ds(first + i * TILE, TILE)],
                out_sems.at[i],
            )
        )
        copies[-1].start()
    for copy in copies:
        copy.wait()


def make_feedback(x, own, act, weight, first, before, marked):
    count = x.shape[0]
    ins = [(x, VMEM), (own, VMEM), (act, VMEM), (weight, VMEM)]
    if before is not None:
        ins.append((before, ANY))
    return launch(
        functools.partial(feedback_kernel, first, count, before is not None), "feedback", ins,
        [(array((TOK, D), BF16), ANY)] + [(array((8, 128), F32), VMEM)] * marked,
        [pltpu.VMEM((count, D), BF16), pltpu.SemaphoreType.DMA((count // TILE,))],
        aliases={} if before is None else {4: 0},
    )


def body(
    forward_codes,
    forward_scales,
    stored_base,
    sample_ids,
    backward_codes,
    backward_scales,
    norm_gain,
    w_down,
    w_up,
):
    sections = lax.axis_size("section")
    replicas = lax.axis_size("dp")
    across = replicas // 2
    both = ("section", "dp")

    def along(value, distance):
        pairs = [(s, (s + distance) % sections) for s in range(sections)]
        return lax.ppermute(value, "section", pairs)

    def among(value, flip_x, flip_y=0, section_step=0):
        pairs = []
        for s in range(sections):
            for d in range(replicas):
                y, x = divmod(d, across)
                source = (y ^ flip_y) * across + (x ^ flip_x)
                goal = ((s + section_step) % sections) * replicas + d
                pairs.append((s * replicas + source, goal))
        return lax.ppermute(value, both, pairs)

    up = w_up[0]
    up_before = along(up, 1)
    down_next = along(w_down[0], -1)
    gain_next = along(norm_gain, -1)

    codes, base = forward_codes[0], stored_base[0]
    scales = forward_scales[0].T
    firsts = [sum(SPANS[:k]) for k in range(len(SPANS))]
    message0 = make_messages(codes, scales, base, sample_ids, 0, SPANS[:1])[0]
    later = make_messages(codes, scales, base, sample_ids, SPANS[0], SPANS[1:], needs=[message0])
    messages = [message0, *later]
    gradient = make_gradient(backward_codes[0], backward_scales[0].T, needs=[later[0]])
    hidden = make_hidden(messages, gain_next, needs=[gradient])

    pre_next, act_next = project_down(hidden, down_next, needs=[up_before])
    act_before = along(act_next, 2)
    act_own = along(act_next, 1)
    arrived0 = along(messages[0], 1)
    dact_before = project_back(gradient, up_before, needs=[act_next])[0]
    dact_next = along(dact_before, -2)

    def feedback_of(own, x, at, before, marked=False):
        return make_feedback(x, own, act_own, up, firsts[at], before, marked)

    up_kept, up_sent, message1, message2 = partial_grad(
        read_act, "grad_up", (0, 1, 3, 2), gradient, act_before,
        needs=[act_own, arrived0, dact_next], carried=messages[1:3],
    )
    arrived1 = along(message1, 1)
    arrived2 = along(message2, 1)
    down_kept, down_sent = partial_grad(
        make_dpre, "grad_down", (0, 3, 1, 2), hidden, pre_next, dact_next,
    )
    feedback, done = feedback_of(messages[0], arrived0, 0, None, True)
    up_kept, up_sent, message3 = halve(
        up_kept, among(up_sent, 3), needs=[arrived1, done], carried=messages[3:4]
    )
    arrived3 = along(message3, 1)
    down_kept, down_sent = halve(down_kept, among(down_sent, 1))
    feedback, done = feedback_of(message1, arrived1, 1, feedback, True)
    up_parts = split(up_kept, among(up_sent, 1), needs=[arrived2, done])
    down_parts = split(down_kept, among(down_sent, 3))
    grad_up = finish([among(up_parts[half], 0, half, -1) for half in range(2)])
    grad_down = finish([among(down_parts[half], 0, half, 1) for half in range(2)])
    feedback = feedback_of(message2, arrived2, 2, feedback)[0]
    feedback = feedback_of(message3, arrived3, 3, feedback)[0]
    return (feedback[None], grad_down[None], grad_up[None])


def solution(mesh):
    in_specs = (
        P("section", "dp", None),
        P("section", "dp", None),
        P("section", "dp", None),
        P("section", "dp"),
        P("section", "dp", None),
        P("section", "dp", None),
        P("section", None),
        P("section", None, None),
        P("section", None, None),
    )
    out_specs = (P("section", "dp", None), P("section", "dp", None), P("section", "dp", None))
    return jax.shard_map(body, mesh=mesh, in_specs=in_specs, out_specs=out_specs, check_vma=False)
```

```python
import functools
import math

import jax
import jax.numpy as jnp
from jax import lax
from jax.experimental import pallas as pl
from jax.experimental.pallas import tpu as pltpu
from jax.sharding import PartitionSpec as P

D = 6144
R = 128
TOK = 384
PIECE = D // 8
F32 = jnp.float32
BF16 = jnp.bfloat16
TILE = 48
BLOCK = 384
HALF = D // 2
SPANS = (96, 144, 96, 48)
MIB = 1 << 20
ROOT_2_PI = math.sqrt(2.0 / math.pi)
VMEM = pl.BlockSpec(memory_space=pltpu.VMEM)
ANY = pl.BlockSpec(memory_space=pl.ANY)


def array(shape, dtype):
    return jax.ShapeDtypeStruct(shape, dtype)


def launch(
    kernel, name, ins, outs, scratch=(), grid=(), aliases=None, needs=(), carried=(), grant=14
):
    n_in, n_out = len(ins), len(outs)
    first_carried = n_in + len(needs)
    n_all = first_carried + len(carried)
    aliases = dict(aliases or {})
    for k in range(len(carried)):
        aliases[first_carried + k] = n_out + k

    def wrapped(*refs):
        rest = refs[n_all + n_out + len(carried) :]
        kernel(*refs[:n_in], *refs[n_all : n_all + n_out], *rest)

    return pl.pallas_call(
        wrapped,
        grid=grid,
        in_specs=[spec for _, spec in ins] + [ANY] * (len(needs) + len(carried)),
        out_specs=[spec for _, spec in outs] + [ANY] * len(carried),
        out_shape=[out for out, _ in outs] + [array(c.shape, c.dtype) for c in carried],
        scratch_shapes=scratch,
        input_output_aliases=aliases,
        compiler_params=pltpu.CompilerParams(vmem_limit_bytes=grant * MIB),
        cost_estimate=pl.CostEstimate(flops=1, bytes_accessed=1, transcendentals=0),
        name=name,
    )(*[value for value, _ in ins], *needs, *carried)


def hand_on(value, after):
    return launch(lambda: None, "hand_on", [], [], needs=[after], carried=[value], grant=1)[0]


def lanes(shape):
    return lax.broadcasted_iota(jnp.int32, shape, 1)


def block_at(b):
    return pl.ds(pl.multiple_of(b * BLOCK, 128), BLOCK)


def one_hot_blocks(b):
    shape = (D // 32, BLOCK)
    spot = lax.broadcasted_iota(jnp.int32, shape, 0) - b * (BLOCK // 32)
    return (spot == lanes(shape) // 32).astype(F32).astype(BF16)


def exact(left, right):
    return jnp.dot(left, right, preferred_element_type=F32)


def chunks_of(out_refs):
    found, start = [], 0
    for ref in out_refs:
        count = ref.shape[0]
        for row in range(0, count, 96):
            found.append((ref, row, start + row, min(96, count - row)))
        start += count
    return found


def message_kernel(first, codes_ref, scales_ref, base_ref, ids_ref, *refs):
    *out_refs, stats_ref, turned_ref, picks_ref, pivot_ref, sum_ref, square_ref = refs
    count = stats_ref.shape[0]
    mine = slice(first, first + count)
    turned_ref[...] = scales_ref[...].astype(F32).T[mine].astype(BF16)
    hits = lax.broadcasted_iota(jnp.int32, (32, TOK), 0) == ids_ref[...]
    picks_ref[...] = hits.astype(F32).T[mine].astype(BF16)
    chunks = chunks_of(out_refs)

    def decode(b, take):
        spread = one_hot_blocks(b)
        base_block = base_ref[:, block_at(b)]
        words_at = pl.ds(pl.multiple_of(b * 128, 128), 128)
        for ref, row, at, n in chunks:
            rows = slice(at, at + n)
            scale = exact(turned_ref[rows, :], spread)
            base = exact(picks_ref[rows, :], base_block)
            words = codes_ref[first + at : first + at + n, words_at]
            lane = lanes((n, 128))
            values = []
            for j in range(3):
                spot = lane + 128 * j
                word = jnp.take_along_axis(words, spot // 3, axis=1)
                code = jnp.right_shift(word, (spot % 3) * 4) & 15
                part = slice(j * 128, (j + 1) * 128)
                value = base[:, part] + scale[:, part] * (code - 8).astype(F32)
                value = value.astype(BF16)
                ref[row : row + n, pl.ds(pl.multiple_of(b * BLOCK + j * 128, 128), 128)] = value
                values.append(value.astype(F32))
            take(rows, n, values)

    def begin(rows, n, values):
        pivot = jnp.sum(values[0] + values[1] + values[2], axis=1, keepdims=True) / BLOCK
        pivot = jnp.broadcast_to(pivot, (n, 128))
        pivot_ref[rows, :] = pivot
        away = [value - pivot for value in values]
        sum_ref[rows, :] = away[0] + away[1] + away[2]
        square_ref[rows, :] = away[0] * away[0] + away[1] * away[1] + away[2] * away[2]

    def go_on(rows, n, values):
        pivot = pivot_ref[rows, :]
        away = [value - pivot for value in values]
        sum_ref[rows, :] += away[0] + away[1] + away[2]
        square_ref[rows, :] += away[0] * away[0] + away[1] * away[1] + away[2] * away[2]

    def one_block(b, carry):
        decode(b, go_on)
        return carry

    decode(0, begin)
    lax.fori_loop(1, D // BLOCK, one_block, 0)
    shift = jnp.sum(sum_ref[...], axis=1, keepdims=True) * (1.0 / D)
    square = jnp.sum(square_ref[...], axis=1, keepdims=True) * (1.0 / D)
    variance = jnp.maximum(square - shift * shift, 0.0)
    stats_ref[:, :128] = pivot_ref[...] + shift
    stats_ref[:, 128:] = jnp.broadcast_to(lax.rsqrt(variance + 1e-05), (count, 128))


def make_messages(codes, scales, base, ids, first, spans, **ties):
    count = sum(spans)
    return launch(
        functools.partial(message_kernel, first), "message",
        [(value, VMEM) for value in (codes, scales, base, ids)],
        [(array((span, D), BF16), VMEM) for span in spans] + [(array((count, 256), F32), VMEM)],
        [pltpu.VMEM((count, D // 32), BF16), pltpu.VMEM((count, 32), BF16)]
        + [pltpu.VMEM((count, 128), F32)] * 3,
        **ties,
    )


def gradient_kernel(codes_ref, scales_ref, out_ref, turned_ref):
    turned_ref[...] = scales_ref[...].astype(F32).T.astype(BF16)

    def one_block(b, carry):
        spread = one_hot_blocks(b)
        for at in range(0, TOK, 96):
            rows = slice(at, at + 96)
            scale = exact(turned_ref[rows, :], spread)
            codes = codes_ref[rows, block_at(b)].astype(F32)
            out_ref[rows, block_at(b)] = (scale * (codes - 128.0)).astype(BF16)
        return carry

    lax.fori_loop(0, D // BLOCK, one_block, 0)


def make_gradient(codes, scales, **ties):
    return launch(
        gradient_kernel, "gradient", [(codes, VMEM), (scales, VMEM)],
        [(array((TOK, D), BF16), VMEM)], [pltpu.VMEM((TOK, D // 32), BF16)], **ties,
    )[0]


def hidden_kernel(n, gain_ref, *refs):
    message_refs, stats_refs, out_ref = refs[:n], refs[n:-1], refs[-1]
    stats = [
        (ref, row) for ref, row, _, rows in chunks_of(stats_refs) for row in range(row, row + rows, TILE)
    ]
    messages = [
        (ref, row) for ref, row, _, rows in chunks_of(message_refs) for row in range(row, row + rows, TILE)
    ]

    def one_block(b, carry):
        at = pl.ds(pl.multiple_of(b * 128, 128), 128)
        gain = gain_ref[:, at]
        for t, ((ref, row), (stats_ref, stats_row)) in enumerate(zip(messages, stats)):
            x = ref[row : row + TILE, at].astype(F32)
            mean = stats_ref[stats_row : stats_row + TILE, :128]
            scale = stats_ref[stats_row : stats_row + TILE, 128:]
            out_ref[t * TILE : (t + 1) * TILE, at] = (gain * (x - mean) * scale).astype(BF16)
        return carry

    lax.fori_loop(0, D // 128, one_block, 0)


def make_hidden(messages, stats, gain, **ties):
    return launch(
        functools.partial(hidden_kernel, len(messages)), "hidden",
        [(value, VMEM) for value in (gain, *messages, *stats)],
        [(array((TOK, D), BF16), VMEM)], **ties,
    )[0]


def tanh_of(pre):
    return jnp.tanh(ROOT_2_PI * (pre + 0.044715 * (pre * pre * pre)))


def down_kernel(hidden_ref, weight_ref, pre_ref, act_ref):
    pre = jnp.dot(hidden_ref[...], weight_ref[...], preferred_element_type=F32)
    pre_ref[...] = pre
    act_ref[...] = (0.5 * pre * (1.0 + tanh_of(pre))).astype(BF16)


def project_down(hidden, weight, **ties):
    return launch(
        down_kernel, "down", [(hidden, VMEM), (weight, VMEM)],
        [(array((TOK, R), F32), VMEM), (array((TOK, R), BF16), VMEM)], **ties,
    )


def pick_half_kernel(weight_ref, out_ref, sem):
    half = lax.rem(lax.axis_index("dp"), 2)
    rows = pl.ds(pl.multiple_of(half * HALF, HALF), HALF)
    copy = pltpu.make_async_copy(weight_ref.at[rows], out_ref, sem.at[0])
    copy.start()
    copy.wait()


def pick_half(weight):
    return launch(
        pick_half_kernel, "pick_half", [(weight, ANY)], [(array((HALF, R), BF16), VMEM)],
        [pltpu.SemaphoreType.DMA((1,))],
    )[0]


def back_kernel(grad_ref, chip_ref, mine_ref, other_ref, out_ref):
    half = lax.rem(lax.axis_index("dp"), 2)
    total = jnp.zeros((TOK, R), F32)
    for where, part_ref in ((half, mine_ref), (1 - half, other_ref)):
        at = pl.ds(pl.multiple_of(where * HALF, HALF), HALF)
        weight = part_ref[...] + chip_ref[at, :]
        total += jnp.dot(grad_ref[:, at], weight, preferred_element_type=F32)
    out_ref[...] = total.astype(BF16)


def project_back(grad, chip, mine, other, **ties):
    return launch(
        back_kernel, "back", [(value, VMEM) for value in (grad, chip, mine, other)],
        [(array((TOK, R), BF16), VMEM)], **ties,
    )


def transposed(left, right):
    return lax.dot_general(left, right, (((0,), (0,)), ((), ())), preferred_element_type=F32)


def grad_kernel(narrow_of, flips, wide_ref, *refs):
    *narrow_refs, kept_ref, sent_ref = refs
    narrow = narrow_of(*narrow_refs)
    replica = lax.axis_index("dp")
    x_at, y_at = lax.rem(replica, 4), lax.div(replica, 4)
    for i, flip in enumerate(flips):
        for half in range(2):
            piece = (y_at ^ half) * 4 + (x_at ^ flip)
            columns = pl.ds(pl.multiple_of(piece * PIECE, 128), PIECE)
            total = transposed(narrow, wide_ref[:, columns])
            if i < 2:
                kept_ref[2 * i + half] = total
            else:
                sent_ref[2 * i - 4 + half] = total.astype(BF16)


def read_act(act_ref):
    return act_ref[...]


def make_dpre(pre_ref, dact_ref):
    pre = pre_ref[...]
    t = tanh_of(pre)
    slope = 0.5 * (1.0 + t) + (0.5 * ROOT_2_PI) * pre * (1.0 - t * t) * (
        1.0 + (3.0 * 0.044715) * (pre * pre)
    )
    return (dact_ref[...].astype(F32) * slope).astype(BF16)


def partial_grad(narrow_of, name, flips, wide, *narrow, **ties):
    return launch(
        functools.partial(grad_kernel, narrow_of, flips), name,
        [(value, VMEM) for value in (wide, *narrow)],
        [(array((4, R, PIECE), F32), VMEM), (array((4, R, PIECE), BF16), VMEM)], **ties,
    )


def halve_kernel(kept_ref, came_ref, keep_ref, send_ref):
    keep_ref[...] = kept_ref[:2] + came_ref[:2].astype(F32)
    send_ref[...] = (kept_ref[2:] + came_ref[2:].astype(F32)).astype(BF16)


def halve(kept, came, **ties):
    return launch(
        halve_kernel, "halve", [(kept, VMEM), (came, VMEM)],
        [(array((2, R, PIECE), F32), VMEM), (array((2, R, PIECE), BF16), VMEM)], **ties,
    )


def split_kernel(kept_ref, came_ref, *out_refs):
    for half, out_ref in enumerate(out_refs):
        out_ref[...] = (kept_ref[half] + came_ref[half].astype(F32)).astype(BF16)


def split(kept, came, **ties):
    return launch(
        split_kernel, "split", [(kept, VMEM), (came, VMEM)],
        [(array((R, PIECE), BF16), VMEM)] * 2, **ties,
    )


def finish_kernel(one_ref, two_ref, out_ref):
    out_ref[...] = (one_ref[...].astype(F32) + two_ref[...].astype(F32)).T


def finish(parts):
    return launch(
        finish_kernel, "finish", [(part, VMEM) for part in parts],
        [(array((PIECE, R), F32), pl.BlockSpec((PIECE, R)))],
    )[0]


def feedback_kernel(first, count, before, x_ref, own_ref, act_ref, weight_ref, *refs):
    *rest, out_ref, out_sems = refs
    if before:
        rest = rest[1:]
    out_hbm = rest[0]
    for done_ref in rest[1:]:
        done_ref[...] = jnp.zeros_like(done_ref)
    copies = []
    for i in range(count // TILE):
        rows = slice(i * TILE, (i + 1) * TILE)
        act = act_ref[first + i * TILE : first + (i + 1) * TILE, :]
        for part in range(4):
            at = slice(part * 2 * PIECE, (part + 1) * 2 * PIECE)
            lifted = lax.dot_general(
                act, weight_ref[at, :], (((1,), (1,)), ((), ())), preferred_element_type=F32
            )
            value = x_ref[rows, at].astype(F32) + lifted - own_ref[rows, at].astype(F32)
            out_ref[rows, at] = value.astype(BF16)
        copies.append(
            pltpu.make_async_copy(
                out_ref.at[pl.ds(i * TILE, TILE)],
                out_hbm.at[pl.ds(first + i * TILE, TILE)],
                out_sems.at[i],
            )
        )
        copies[-1].start()
    for copy in copies:
        copy.wait()


def make_feedback(x, own, act, weight, first, before, marked):
    count = x.shape[0]
    ins = [(x, VMEM), (own, VMEM), (act, VMEM), (weight, VMEM)]
    if before is not None:
        ins.append((before, ANY))
    return launch(
        functools.partial(feedback_kernel, first, count, before is not None), "feedback", ins,
        [(array((TOK, D), BF16), ANY)] + [(array((8, 128), F32), VMEM)] * marked,
        [pltpu.VMEM((count, D), BF16), pltpu.SemaphoreType.DMA((count // TILE,))],
        aliases={} if before is None else {4: 0},
    )


def body(
    forward_codes,
    forward_scales,
    stored_base,
    sample_ids,
    backward_codes,
    backward_scales,
    norm_gain,
    w_down,
    w_up,
):
    sections = lax.axis_size("section")
    replicas = lax.axis_size("dp")
    across = replicas // 2
    both = ("section", "dp")

    def along(value, distance):
        pairs = [(s, (s + distance) % sections) for s in range(sections)]
        return lax.ppermute(value, "section", pairs)

    def among(value, flip_x, flip_y=0, section_step=0, stride=1):
        pairs = []
        for s in range(0, sections, stride):
            for d in range(replicas):
                y, x = divmod(d, across)
                source = (y ^ flip_y) * across + (x ^ flip_x)
                goal = ((s + section_step) % sections) * replicas + d
                pairs.append((s * replicas + source, goal))
        return lax.ppermute(value, both, pairs)

    up = w_up[0]
    odd_to_even = [(s, (s + 1) % sections) for s in range(1, sections, 2)]
    even_to_odd = [(s, s + 1) for s in range(0, sections, 2)]
    up_mine = lax.ppermute(pick_half(up), "section", odd_to_even)
    up_chip = lax.ppermute(up, "section", even_to_odd)
    down_next = along(w_down[0], -1)
    gain_next = along(norm_gain, -1)

    codes, base = forward_codes[0], stored_base[0]
    scales = forward_scales[0].T
    firsts = [sum(SPANS[:k]) for k in range(len(SPANS))]
    message0, stats0 = make_messages(codes, scales, base, sample_ids, 0, SPANS[:1])
    message1, stats1 = make_messages(
        codes, scales, base, sample_ids, firsts[1], SPANS[1:2], needs=[message0]
    )
    up_mine = hand_on(up_mine, message1)
    up_other = among(up_mine, 1, stride=2)
    *later, stats2 = make_messages(
        codes, scales, base, sample_ids, firsts[2], SPANS[2:], needs=[message1]
    )
    messages = [message0, message1, *later]
    gradient = make_gradient(backward_codes[0], backward_scales[0].T, needs=[later[0]])
    hidden = make_hidden(messages, [stats0, stats1, stats2], gain_next, needs=[gradient])

    pre_next, act_next = project_down(hidden, down_next, needs=[up_chip, up_other])
    act_before = along(act_next, 2)
    act_own = along(act_next, 1)
    arrived0 = along(messages[0], 1)
    dact_before = project_back(
        gradient, up_chip, up_mine, up_other, needs=[act_next]
    )[0]
    dact_next = along(dact_before, -2)

    def feedback_of(own, x, at, before, marked=False):
        return make_feedback(x, own, act_own, up, firsts[at], before, marked)

    up_kept, up_sent, message1, message2 = partial_grad(
        read_act, "grad_up", (0, 1, 3, 2), gradient, act_before,
        needs=[act_own, arrived0, dact_next], carried=messages[1:3],
    )
    arrived1 = along(message1, 1)
    arrived2 = along(message2, 1)
    down_kept, down_sent = partial_grad(
        make_dpre, "grad_down", (0, 3, 1, 2), hidden, pre_next, dact_next,
    )
    feedback, done = feedback_of(messages[0], arrived0, 0, None, True)
    up_kept, up_sent, message3 = halve(
        up_kept, among(up_sent, 3), needs=[arrived1], carried=messages[3:4]
    )
    arrived3 = along(message3, 1)
    down_kept, down_sent = halve(down_kept, among(down_sent, 1), needs=[done])
    feedback, done = feedback_of(message1, arrived1, 1, feedback, True)
    up_parts = split(up_kept, among(up_sent, 1), needs=[arrived2])
    down_parts = split(down_kept, among(down_sent, 3), needs=[done])
    grad_up = finish([among(up_parts[half], 0, half, -1) for half in range(2)])
    grad_down = finish([among(down_parts[half], 0, half, 1) for half in range(2)])
    feedback = feedback_of(message2, arrived2, 2, feedback)[0]
    feedback = feedback_of(message3, arrived3, 3, feedback)[0]
    return (feedback[None], grad_down[None], grad_up[None])


def solution(mesh):
    in_specs = (
        P("section", "dp", None),
        P("section", "dp", None),
        P("section", "dp", None),
        P("section", "dp"),
        P("section", "dp", None),
        P("section", "dp", None),
        P("section", None),
        P("section", None, None),
        P("section", None, None),
    )
    out_specs = (P("section", "dp", None), P("section", "dp", None), P("section", "dp", None))
    return jax.shard_map(body, mesh=mesh, in_specs=in_specs, out_specs=out_specs, check_vma=False)
```

```python
import functools
import math

import jax
import jax.numpy as jnp
from jax import lax
from jax.experimental import pallas as pl
from jax.experimental.pallas import tpu as pltpu
from jax.sharding import PartitionSpec as P

D = 6144
R = 128
TOK = 384
PIECE = D // 8
F32 = jnp.float32
BF16 = jnp.bfloat16
TILE = 48
BLOCK = 768
WORDS = BLOCK // 3
CODES = BLOCK // 32
HALF = D // 2
SPANS = (96, 48, 96, 96, 48)
MIB = 1 << 20
ROOT_2_PI = math.sqrt(2.0 / math.pi)
VMEM = pl.BlockSpec(memory_space=pltpu.VMEM)
ANY = pl.BlockSpec(memory_space=pl.ANY)


def array(shape, dtype):
    return jax.ShapeDtypeStruct(shape, dtype)


def launch(
    kernel, name, ins, outs, scratch=(), grid=(), aliases=None, needs=(), carried=(), grant=14
):
    n_in, n_out = len(ins), len(outs)
    first_carried = n_in + len(needs)
    n_all = first_carried + len(carried)
    aliases = dict(aliases or {})
    for k in range(len(carried)):
        aliases[first_carried + k] = n_out + k

    def wrapped(*refs):
        rest = refs[n_all + n_out + len(carried) :]
        kernel(*refs[:n_in], *refs[n_all : n_all + n_out], *rest)

    return pl.pallas_call(
        wrapped,
        grid=grid,
        in_specs=[spec for _, spec in ins] + [ANY] * (len(needs) + len(carried)),
        out_specs=[spec for _, spec in outs] + [ANY] * len(carried),
        out_shape=[out for out, _ in outs] + [array(c.shape, c.dtype) for c in carried],
        scratch_shapes=scratch,
        input_output_aliases=aliases,
        compiler_params=pltpu.CompilerParams(vmem_limit_bytes=grant * MIB),
        cost_estimate=pl.CostEstimate(flops=1, bytes_accessed=1, transcendentals=0),
        name=name,
    )(*[value for value, _ in ins], *needs, *carried)


def lanes(shape):
    return lax.broadcasted_iota(jnp.int32, shape, 1)


def block_at(b):
    return pl.ds(pl.multiple_of(b * BLOCK, 128), BLOCK)


def spreader():
    shape = (32, BLOCK)
    return (lax.broadcasted_iota(jnp.int32, shape, 0) == lanes(shape) // 32).astype(F32).astype(
        BF16
    )


def turn_scales(scales_ref, turned_ref, rows):
    padding = jnp.zeros((32 - CODES, TOK), F32)
    for b in range(D // BLOCK):
        part = scales_ref[b * CODES : (b + 1) * CODES, :].astype(F32)
        turned_ref[b] = jnp.concatenate([part, padding], axis=0).T[rows].astype(BF16)


def exact(left, right):
    return jnp.dot(left, right, preferred_element_type=F32)


def chunks_of(out_refs):
    found, start = [], 0
    for ref in out_refs:
        count = ref.shape[0]
        for row in range(0, count, 96):
            found.append((ref, row, start + row, min(96, count - row)))
        start += count
    return found


def message_kernel(first, codes_ref, scales_ref, base_ref, ids_ref, *refs):
    *out_refs, stats_ref, turned_ref, picks_ref, pivot_ref, sum_ref, square_ref = refs
    count = stats_ref.shape[0]
    mine = slice(first, first + count)
    turn_scales(scales_ref, turned_ref, mine)
    spread = spreader()
    hits = lax.broadcasted_iota(jnp.int32, (32, TOK), 0) == ids_ref[...]
    picks_ref[...] = hits.astype(F32).T[mine].astype(BF16)
    chunks = chunks_of(out_refs)

    def decode(b, take):
        base_block = base_ref[:, block_at(b)]
        for ref, row, at, n in chunks:
            rows = slice(at, at + n)
            scale = exact(turned_ref[b, rows, :], spread)
            base = exact(picks_ref[rows, :], base_block)
            lane = lanes((n, 128))
            values = []
            for k in range(WORDS // 128):
                words_at = pl.ds(pl.multiple_of(b * WORDS + k * 128, 128), 128)
                words = codes_ref[first + at : first + at + n, words_at]
                for j in range(3):
                    spot = lane + 128 * j
                    word = jnp.take_along_axis(words, spot // 3, axis=1)
                    code = jnp.right_shift(word, (spot % 3) * 4) & 15
                    tile = 3 * k + j
                    part = slice(tile * 128, (tile + 1) * 128)
                    value = base[:, part] + scale[:, part] * (code - 8).astype(F32)
                    value = value.astype(BF16)
                    to = pl.ds(pl.multiple_of(b * BLOCK + tile * 128, 128), 128)
                    ref[row : row + n, to] = value
                    values.append(value.astype(F32))
            take(rows, n, values)

    def begin(rows, n, values):
        pivot = jnp.sum(sum(values), axis=1, keepdims=True) / BLOCK
        pivot = jnp.broadcast_to(pivot, (n, 128))
        pivot_ref[rows, :] = pivot
        away = [value - pivot for value in values]
        sum_ref[rows, :] = sum(away)
        square_ref[rows, :] = sum(v * v for v in away)

    def go_on(rows, n, values):
        pivot = pivot_ref[rows, :]
        away = [value - pivot for value in values]
        sum_ref[rows, :] += sum(away)
        square_ref[rows, :] += sum(v * v for v in away)

    def one_block(b, carry):
        decode(b, go_on)
        return carry

    decode(0, begin)
    lax.fori_loop(1, D // BLOCK, one_block, 0)
    shift = jnp.sum(sum_ref[...], axis=1, keepdims=True) * (1.0 / D)
    square = jnp.sum(square_ref[...], axis=1, keepdims=True) * (1.0 / D)
    variance = jnp.maximum(square - shift * shift, 0.0)
    stats_ref[:, :128] = pivot_ref[...] + shift
    stats_ref[:, 128:] = jnp.broadcast_to(lax.rsqrt(variance + 1e-05), (count, 128))


def make_messages(codes, scales, base, ids, first, spans, **ties):
    count = sum(spans)
    return launch(
        functools.partial(message_kernel, first), "message",
        [(value, VMEM) for value in (codes, scales, base, ids)],
        [(array((span, D), BF16), VMEM) for span in spans] + [(array((count, 256), F32), VMEM)],
        [pltpu.VMEM((D // BLOCK, count, 32), BF16), pltpu.VMEM((count, 32), BF16)]
        + [pltpu.VMEM((count, 128), F32)] * 3,
        **ties,
    )


def gradient_kernel(codes_ref, scales_ref, out_ref, turned_ref):
    turn_scales(scales_ref, turned_ref, slice(0, TOK))
    spread = spreader()

    def one_block(b, carry):
        for at in range(0, TOK, 96):
            rows = slice(at, at + 96)
            scale = exact(turned_ref[b, rows, :], spread)
            codes = codes_ref[rows, block_at(b)].astype(F32)
            out_ref[rows, block_at(b)] = (scale * (codes - 128.0)).astype(BF16)
        return carry

    lax.fori_loop(0, D // BLOCK, one_block, 0)


def make_gradient(codes, scales, **ties):
    return launch(
        gradient_kernel, "gradient", [(codes, VMEM), (scales, VMEM)],
        [(array((TOK, D), BF16), VMEM)], [pltpu.VMEM((D // BLOCK, TOK, 32), BF16)], **ties,
    )[0]


def tanh_of(pre):
    return jnp.tanh(ROOT_2_PI * (pre + 0.044715 * (pre * pre * pre)))


def stage_down_kernel(weight_hbm, gain_ref, out_ref, rows_ref, sems):
    copy = pltpu.make_async_copy(weight_hbm, out_ref.at[pl.ds(0, D)], sems.at[0])
    copy.start()
    for k in range(D // 128):
        rows_ref[k : k + 1, :] = gain_ref[:, k * 128 : (k + 1) * 128]
    gain = rows_ref[...]
    high = gain.astype(BF16)
    out_ref[D : D + D // 128, :] = high
    out_ref[D + D // 128 :, :] = (gain - high.astype(F32)).astype(BF16)
    copy.wait()


def stage_down(weight, gain):
    return launch(
        stage_down_kernel, "stage_down", [(weight, ANY), (gain, VMEM)],
        [(array((D + D // 64, R), BF16), VMEM)],
        [pltpu.VMEM((D // 128, 128), F32), pltpu.SemaphoreType.DMA((1,))],
    )[0]


def down_kernel(n, weight_ref, *refs):
    message_refs, stats_refs = refs[:n], refs[n:-4]
    hidden_ref, pre_ref, act_ref, gain_ref = refs[-4:]
    gain_ref[...] = weight_ref[D : D + D // 128, :].astype(F32) + weight_ref[
        D + D // 128 :, :
    ].astype(F32)
    messages, stats = [
        [(ref, at) for ref, row, _, rows in chunks_of(found) for at in range(row, row + rows, TILE)]
        for found in (message_refs, stats_refs)
    ]

    def one_block(b, carry):
        for c in range(BLOCK // 128):
            at = pl.ds(pl.multiple_of(b * BLOCK + c * 128, 128), 128)
            gain = gain_ref[pl.ds(b * (BLOCK // 128) + c, 1), :]
            for t, ((ref, row), (stats_ref, stats_row)) in enumerate(zip(messages, stats)):
                x = ref[row : row + TILE, at].astype(F32)
                mean = stats_ref[stats_row : stats_row + TILE, :128]
                scale = stats_ref[stats_row : stats_row + TILE, 128:]
                hidden_ref[t * TILE : (t + 1) * TILE, at] = (gain * (x - mean) * scale).astype(
                    BF16
                )
        weight = weight_ref[pl.ds(pl.multiple_of(b * BLOCK, 128), BLOCK), :]
        pre_ref[...] += jnp.dot(
            hidden_ref[:, block_at(b)], weight, preferred_element_type=F32
        )
        return carry

    pre_ref[...] = jnp.zeros_like(pre_ref)
    lax.fori_loop(0, D // BLOCK, one_block, 0)
    pre = pre_ref[...]
    act_ref[...] = (0.5 * pre * (1.0 + tanh_of(pre))).astype(BF16)


def project_down(messages, stats, staged, **ties):
    return launch(
        functools.partial(down_kernel, len(messages)), "down",
        [(value, VMEM) for value in (staged, *messages, *stats)],
        [
            (array((TOK, D), BF16), VMEM), (array((TOK, R), F32), VMEM),
            (array((TOK, R), BF16), VMEM),
        ],
        [pltpu.VMEM((D // 128, 128), F32)], **ties,
    )


def stage_kernel(weight_hbm, whole_ref, half_ref, sems):
    half = lax.rem(lax.axis_index("dp"), 2)
    rows = pl.ds(pl.multiple_of(half * HALF, HALF), HALF)
    copies = [
        pltpu.make_async_copy(weight_hbm.at[rows], half_ref, sems.at[0]),
        pltpu.make_async_copy(weight_hbm, whole_ref, sems.at[1]),
    ]
    for copy in copies:
        copy.start()
    for copy in copies:
        copy.wait()


def stage(weight):
    return launch(
        stage_kernel, "stage", [(weight, ANY)],
        [(array((D, R), BF16), VMEM), (array((HALF, R), BF16), VMEM)],
        [pltpu.SemaphoreType.DMA((2,))],
    )


def back_kernel(grad_ref, chip_ref, mine_ref, other_ref, out_ref):
    half = lax.rem(lax.axis_index("dp"), 2)
    total = jnp.zeros((TOK, R), F32)
    for where, part_ref in ((half, mine_ref), (1 - half, other_ref)):
        at = pl.ds(pl.multiple_of(where * HALF, HALF), HALF)
        weight = part_ref[...] + chip_ref[at, :]
        total += jnp.dot(grad_ref[:, at], weight, preferred_element_type=F32)
    out_ref[...] = total.astype(BF16)


def project_back(grad, chip, mine, other, **ties):
    return launch(
        back_kernel, "back", [(value, VMEM) for value in (grad, chip, mine, other)],
        [(array((TOK, R), BF16), VMEM)], **ties,
    )


def transposed(left, right):
    return lax.dot_general(left, right, (((0,), (0,)), ((), ())), preferred_element_type=F32)


def grad_kernel(narrow_of, flips, wide_ref, *refs):
    *narrow_refs, kept_ref, sent_ref = refs
    narrow = narrow_of(*narrow_refs)
    replica = lax.axis_index("dp")
    x_at, y_at = lax.rem(replica, 4), lax.div(replica, 4)
    for i, flip in enumerate(flips):
        for half in range(2):
            piece = (y_at ^ half) * 4 + (x_at ^ flip)
            columns = pl.ds(pl.multiple_of(piece * PIECE, 128), PIECE)
            total = transposed(narrow, wide_ref[:, columns])
            if i < 2:
                kept_ref[2 * i + half] = total
            else:
                sent_ref[2 * i - 4 + half] = total.astype(BF16)


def read_act(act_ref):
    return act_ref[...]


def make_dpre(pre_ref, dact_ref):
    pre = pre_ref[...]
    t = tanh_of(pre)
    slope = 0.5 * (1.0 + t) + (0.5 * ROOT_2_PI) * pre * (1.0 - t * t) * (
        1.0 + (3.0 * 0.044715) * (pre * pre)
    )
    return (dact_ref[...].astype(F32) * slope).astype(BF16)


def partial_grad(narrow_of, name, flips, wide, *narrow, **ties):
    return launch(
        functools.partial(grad_kernel, narrow_of, flips), name,
        [(value, VMEM) for value in (wide, *narrow)],
        [(array((4, R, PIECE), F32), VMEM), (array((4, R, PIECE), BF16), VMEM)], **ties,
    )


def halve_kernel(kept_ref, came_ref, keep_ref, send_ref):
    keep_ref[...] = kept_ref[:2] + came_ref[:2].astype(F32)
    send_ref[...] = (kept_ref[2:] + came_ref[2:].astype(F32)).astype(BF16)


def halve(kept, came, **ties):
    return launch(
        halve_kernel, "halve", [(kept, VMEM), (came, VMEM)],
        [(array((2, R, PIECE), F32), VMEM), (array((2, R, PIECE), BF16), VMEM)], **ties,
    )


def split_kernel(kept_ref, came_ref, *out_refs):
    for half, out_ref in enumerate(out_refs):
        out_ref[...] = (kept_ref[half] + came_ref[half].astype(F32)).astype(BF16)


def split(kept, came, **ties):
    return launch(
        split_kernel, "split", [(kept, VMEM), (came, VMEM)],
        [(array((R, PIECE), BF16), VMEM)] * 2, **ties,
    )


def finish_kernel(one_ref, two_ref, out_ref):
    out_ref[...] = (one_ref[...].astype(F32) + two_ref[...].astype(F32)).T


def finish(parts):
    return launch(
        finish_kernel, "finish", [(part, VMEM) for part in parts],
        [(array((PIECE, R), F32), pl.BlockSpec((PIECE, R)))],
    )[0]


def feedback_kernel(first, count, before, x_ref, own_ref, act_ref, weight_ref, *refs):
    *rest, out_ref, out_sems = refs
    if before:
        rest = rest[1:]
    out_hbm = rest[0]
    for done_ref in rest[1:]:
        done_ref[...] = jnp.zeros_like(done_ref)
    copies = []
    for i in range(count // TILE):
        rows = slice(i * TILE, (i + 1) * TILE)
        act = act_ref[first + i * TILE : first + (i + 1) * TILE, :]
        for part in range(4):
            at = slice(part * 2 * PIECE, (part + 1) * 2 * PIECE)
            lifted = lax.dot_general(
                act, weight_ref[at, :], (((1,), (1,)), ((), ())), preferred_element_type=F32
            )
            value = x_ref[rows, at].astype(F32) + lifted - own_ref[rows, at].astype(F32)
            out_ref[rows, at] = value.astype(BF16)
        copies.append(
            pltpu.make_async_copy(
                out_ref.at[pl.ds(i * TILE, TILE)],
                out_hbm.at[pl.ds(first + i * TILE, TILE)],
                out_sems.at[i],
            )
        )
        copies[-1].start()
    for copy in copies:
        copy.wait()


def make_feedback(x, own, act, weight, first, before, marked):
    count = x.shape[0]
    ins = [(x, VMEM), (own, VMEM), (act, VMEM), (weight, VMEM)]
    if before is not None:
        ins.append((before, ANY))
    return launch(
        functools.partial(feedback_kernel, first, count, before is not None), "feedback", ins,
        [(array((TOK, D), BF16), ANY)] + [(array((8, 128), F32), VMEM)] * marked,
        [pltpu.VMEM((count, D), BF16), pltpu.SemaphoreType.DMA((count // TILE,))],
        aliases={} if before is None else {4: 0},
    )


def body(
    forward_codes,
    forward_scales,
    stored_base,
    sample_ids,
    backward_codes,
    backward_scales,
    norm_gain,
    w_down,
    w_up,
):
    sections = lax.axis_size("section")
    replicas = lax.axis_size("dp")
    across = replicas // 2
    both = ("section", "dp")

    def along(value, distance):
        pairs = [(s, (s + distance) % sections) for s in range(sections)]
        return lax.ppermute(value, "section", pairs)

    def among(value, flip_x, flip_y=0, section_step=0, stride=1):
        pairs = []
        for s in range(0, sections, stride):
            for d in range(replicas):
                y, x = divmod(d, across)
                source = (y ^ flip_y) * across + (x ^ flip_x)
                goal = ((s + section_step) % sections) * replicas + d
                pairs.append((s * replicas + source, goal))
        return lax.ppermute(value, both, pairs)

    down_next = along(stage_down(w_down[0], norm_gain), -1)
    up, up_half = stage(w_up[0])
    odd_to_even = [(s, (s + 1) % sections) for s in range(1, sections, 2)]
    even_to_odd = [(s, s + 1) for s in range(0, sections, 2)]
    up_mine = lax.ppermute(up_half, "section", odd_to_even)
    up_chip = lax.ppermute(up, "section", even_to_odd)
    up_other = among(up_mine, 1, stride=2)

    codes, base = forward_codes[0], stored_base[0]
    scales = forward_scales[0].T
    firsts = [sum(SPANS[:k]) for k in range(len(SPANS))]
    message0, stats0 = make_messages(codes, scales, base, sample_ids, 0, SPANS[:1])
    *later, stats1 = make_messages(
        codes, scales, base, sample_ids, firsts[1], SPANS[1:], needs=[message0]
    )
    messages = [message0, *later]
    gradient = make_gradient(backward_codes[0], backward_scales[0].T, needs=[later[0]])

    hidden, pre_next, act_next = project_down(
        messages, [stats0, stats1], down_next, needs=[up_chip, gradient]
    )
    act_before = along(act_next, 2)
    act_own = along(act_next, 1)
    arrived0 = along(messages[0], 1)
    arrived1 = along(messages[1], 1)
    dact_before = project_back(
        gradient, up_chip, up_mine, up_other, needs=[act_next]
    )[0]
    dact_next = along(dact_before, -2)

    def feedback_of(own, x, at, before, marked=False):
        return make_feedback(x, own, act_own, up, firsts[at], before, marked)

    up_kept, up_sent, message2, message3 = partial_grad(
        read_act, "grad_up", (0, 1, 3, 2), gradient, act_before,
        needs=[act_own, arrived0, arrived1, dact_next], carried=messages[2:4],
    )
    arrived2 = along(message2, 1)
    arrived3 = along(message3, 1)
    down_kept, down_sent = partial_grad(
        make_dpre, "grad_down", (0, 3, 1, 2), hidden, pre_next, dact_next,
    )
    feedback = feedback_of(messages[0], arrived0, 0, None)[0]
    feedback, done = feedback_of(messages[1], arrived1, 1, feedback, True)
    up_kept, up_sent, message4 = halve(
        up_kept, among(up_sent, 3), needs=[arrived2], carried=messages[4:5]
    )
    arrived4 = along(message4, 1)
    down_kept, down_sent = halve(down_kept, among(down_sent, 1), needs=[done])
    feedback, done = feedback_of(message2, arrived2, 2, feedback, True)
    up_parts = split(up_kept, among(up_sent, 1), needs=[arrived3])
    down_parts = split(down_kept, among(down_sent, 3), needs=[done])
    grad_up = finish([among(up_parts[half], 0, half, -1) for half in range(2)])
    grad_down = finish([among(down_parts[half], 0, half, 1) for half in range(2)])
    feedback = feedback_of(message3, arrived3, 3, feedback)[0]
    feedback = feedback_of(message4, arrived4, 4, feedback)[0]
    return (feedback[None], grad_down[None], grad_up[None])


def solution(mesh):
    in_specs = (
        P("section", "dp", None),
        P("section", "dp", None),
        P("section", "dp", None),
        P("section", "dp"),
        P("section", "dp", None),
        P("section", "dp", None),
        P("section", None),
        P("section", None, None),
        P("section", None, None),
    )
    out_specs = (P("section", "dp", None), P("section", "dp", None), P("section", "dp", None))
    return jax.shard_map(body, mesh=mesh, in_specs=in_specs, out_specs=out_specs, check_vma=False)
```

```python
import functools
import math

import jax
import jax.numpy as jnp
from jax import lax
from jax.experimental import pallas as pl
from jax.experimental.pallas import tpu as pltpu
from jax.sharding import PartitionSpec as P

D = 6144
R = 128
TOK = 384
PIECE = D // 8
F32 = jnp.float32
BF16 = jnp.bfloat16
TILE = 48
BLOCK = 768
WORDS = BLOCK // 3
CODES = BLOCK // 32
SPANS = (96, 144, 96, 48)
MIB = 1 << 20
ROOT_2_PI = math.sqrt(2.0 / math.pi)
VMEM = pl.BlockSpec(memory_space=pltpu.VMEM)
ANY = pl.BlockSpec(memory_space=pl.ANY)


def array(shape, dtype):
    return jax.ShapeDtypeStruct(shape, dtype)


def launch(
    kernel, name, ins, outs, scratch=(), grid=(), aliases=None, needs=(), carried=(), grant=14
):
    n_in, n_out = len(ins), len(outs)
    first_carried = n_in + len(needs)
    n_all = first_carried + len(carried)
    aliases = dict(aliases or {})
    for k in range(len(carried)):
        aliases[first_carried + k] = n_out + k

    def wrapped(*refs):
        rest = refs[n_all + n_out + len(carried) :]
        kernel(*refs[:n_in], *refs[n_all : n_all + n_out], *rest)

    return pl.pallas_call(
        wrapped,
        grid=grid,
        in_specs=[spec for _, spec in ins] + [ANY] * (len(needs) + len(carried)),
        out_specs=[spec for _, spec in outs] + [ANY] * len(carried),
        out_shape=[out for out, _ in outs] + [array(c.shape, c.dtype) for c in carried],
        scratch_shapes=scratch,
        input_output_aliases=aliases,
        compiler_params=pltpu.CompilerParams(vmem_limit_bytes=grant * MIB),
        cost_estimate=pl.CostEstimate(flops=1, bytes_accessed=1, transcendentals=0),
        name=name,
    )(*[value for value, _ in ins], *needs, *carried)


def lanes(shape):
    return lax.broadcasted_iota(jnp.int32, shape, 1)


def block_at(b):
    return pl.ds(pl.multiple_of(b * BLOCK, 128), BLOCK)


def spreader():
    shape = (32, BLOCK)
    return (lax.broadcasted_iota(jnp.int32, shape, 0) == lanes(shape) // 32).astype(F32).astype(
        BF16
    )


def turn_scales(scales_ref, turned_ref, rows):
    padding = jnp.zeros((32 - CODES, TOK), F32)
    for b in range(D // BLOCK):
        part = scales_ref[b * CODES : (b + 1) * CODES, :].astype(F32)
        turned_ref[b] = jnp.concatenate([part, padding], axis=0).T[rows].astype(BF16)


def exact(left, right):
    return jnp.dot(left, right, preferred_element_type=F32)


def chunks_of(out_refs):
    found, start = [], 0
    for ref in out_refs:
        count = ref.shape[0]
        for row in range(0, count, 96):
            found.append((ref, row, start + row, min(96, count - row)))
        start += count
    return found


def message_kernel(first, codes_ref, scales_ref, base_ref, ids_ref, *refs):
    *out_refs, stats_ref, turned_ref, picks_ref, pivot_ref, sum_ref, square_ref = refs
    count = stats_ref.shape[0]
    mine = slice(first, first + count)
    turn_scales(scales_ref, turned_ref, mine)
    spread = spreader()
    hits = lax.broadcasted_iota(jnp.int32, (32, TOK), 0) == ids_ref[...]
    picks_ref[...] = hits.astype(F32).T[mine].astype(BF16)
    chunks = chunks_of(out_refs)

    def decode(b, take):
        base_block = base_ref[:, block_at(b)]
        for ref, row, at, n in chunks:
            rows = slice(at, at + n)
            scale = exact(turned_ref[b, rows, :], spread)
            base = exact(picks_ref[rows, :], base_block)
            lane = lanes((n, 128))
            values = []
            for k in range(WORDS // 128):
                words_at = pl.ds(pl.multiple_of(b * WORDS + k * 128, 128), 128)
                words = codes_ref[first + at : first + at + n, words_at]
                for j in range(3):
                    spot = lane + 128 * j
                    word = jnp.take_along_axis(words, spot // 3, axis=1)
                    code = jnp.right_shift(word, (spot % 3) * 4) & 15
                    tile = 3 * k + j
                    part = slice(tile * 128, (tile + 1) * 128)
                    value = base[:, part] + scale[:, part] * (code - 8).astype(F32)
                    value = value.astype(BF16)
                    to = pl.ds(pl.multiple_of(b * BLOCK + tile * 128, 128), 128)
                    ref[row : row + n, to] = value
                    values.append(value.astype(F32))
            take(rows, n, values)

    def begin(rows, n, values):
        pivot = jnp.sum(sum(values), axis=1, keepdims=True) / BLOCK
        pivot = jnp.broadcast_to(pivot, (n, 128))
        pivot_ref[rows, :] = pivot
        away = [value - pivot for value in values]
        sum_ref[rows, :] = sum(away)
        square_ref[rows, :] = sum(v * v for v in away)

    def go_on(rows, n, values):
        pivot = pivot_ref[rows, :]
        away = [value - pivot for value in values]
        sum_ref[rows, :] += sum(away)
        square_ref[rows, :] += sum(v * v for v in away)

    def one_block(b, carry):
        decode(b, go_on)
        return carry

    decode(0, begin)
    lax.fori_loop(1, D // BLOCK, one_block, 0)
    shift = jnp.sum(sum_ref[...], axis=1, keepdims=True) * (1.0 / D)
    square = jnp.sum(square_ref[...], axis=1, keepdims=True) * (1.0 / D)
    variance = jnp.maximum(square - shift * shift, 0.0)
    stats_ref[:, :128] = pivot_ref[...] + shift
    stats_ref[:, 128:] = jnp.broadcast_to(lax.rsqrt(variance + 1e-05), (count, 128))


def make_messages(codes, scales, base, ids, first, spans, **ties):
    count = sum(spans)
    return launch(
        functools.partial(message_kernel, first), "message",
        [(value, VMEM) for value in (codes, scales, base, ids)],
        [(array((span, D), BF16), VMEM) for span in spans] + [(array((count, 256), F32), VMEM)],
        [pltpu.VMEM((D // BLOCK, count, 32), BF16), pltpu.VMEM((count, 32), BF16)]
        + [pltpu.VMEM((count, 128), F32)] * 3,
        **ties,
    )


def gradient_kernel(codes_ref, scales_ref, out_ref, turned_ref):
    turn_scales(scales_ref, turned_ref, slice(0, TOK))
    spread = spreader()

    def one_block(b, carry):
        for at in range(0, TOK, 96):
            rows = slice(at, at + 96)
            scale = exact(turned_ref[b, rows, :], spread)
            codes = codes_ref[rows, block_at(b)].astype(F32)
            out_ref[rows, block_at(b)] = (scale * (codes - 128.0)).astype(BF16)
        return carry

    lax.fori_loop(0, D // BLOCK, one_block, 0)


def make_gradient(codes, scales, **ties):
    return launch(
        gradient_kernel, "gradient", [(codes, VMEM), (scales, VMEM)],
        [(array((TOK, D), BF16), VMEM)], [pltpu.VMEM((D // BLOCK, TOK, 32), BF16)], **ties,
    )[0]


def tanh_of(pre):
    return jnp.tanh(ROOT_2_PI * (pre + 0.044715 * (pre * pre * pre)))


def hidden_kernel(n, gain_ref, *refs):
    message_refs, stats_refs, out_ref = refs[:n], refs[n:-1], refs[-1]
    messages, stats = [
        [(ref, at) for ref, row, _, rows in chunks_of(found) for at in range(row, row + rows, TILE)]
        for found in (message_refs, stats_refs)
    ]
    for t, ((ref, row), (stats_ref, stats_row)) in enumerate(zip(messages, stats)):
        rows = slice(stats_row, stats_row + TILE)
        mean, scale = stats_ref[rows, :128], stats_ref[rows, 128:]

        def one_block(b, carry, ref=ref, row=row, t=t, mean=mean, scale=scale):
            for c in range(BLOCK // 128):
                at = pl.ds(pl.multiple_of(b * BLOCK + c * 128, 128), 128)
                x = ref[row : row + TILE, at].astype(F32)
                value = gain_ref[:, at] * (x - mean) * scale
                out_ref[t * TILE : (t + 1) * TILE, at] = value.astype(BF16)
            return carry

        lax.fori_loop(0, D // BLOCK, one_block, 0)


def make_hidden(messages, stats, gain, **ties):
    return launch(
        functools.partial(hidden_kernel, len(messages)), "hidden",
        [(value, VMEM) for value in (gain, *messages, *stats)],
        [(array((TOK, D), BF16), VMEM)], **ties,
    )[0]


def down_kernel(hidden_ref, weight_ref, pre_ref, act_ref):
    pre = jnp.dot(hidden_ref[...], weight_ref[...], preferred_element_type=F32)
    pre_ref[...] = pre
    act_ref[...] = (0.5 * pre * (1.0 + tanh_of(pre))).astype(BF16)


def project_down(hidden, weight, **ties):
    return launch(
        down_kernel, "down", [(hidden, VMEM), (weight, VMEM)],
        [(array((TOK, R), F32), VMEM), (array((TOK, R), BF16), VMEM)], **ties,
    )


def back_kernel(grad_ref, weight_ref, out_ref):
    out_ref[...] = jnp.dot(
        grad_ref[...], weight_ref[...], preferred_element_type=F32
    ).astype(BF16)


def project_back(grad, weight, **ties):
    return launch(
        back_kernel, "back", [(grad, VMEM), (weight, VMEM)],
        [(array((TOK, R), BF16), VMEM)], **ties,
    )


def transposed(left, right):
    return lax.dot_general(left, right, (((0,), (0,)), ((), ())), preferred_element_type=F32)


def grad_kernel(narrow_of, flips, wide_ref, *refs):
    *narrow_refs, kept_ref, sent_ref = refs
    narrow = narrow_of(*narrow_refs)
    replica = lax.axis_index("dp")
    x_at, y_at = lax.rem(replica, 4), lax.div(replica, 4)
    for i, flip in enumerate(flips):
        for half in range(2):
            piece = (y_at ^ half) * 4 + (x_at ^ flip)
            columns = pl.ds(pl.multiple_of(piece * PIECE, 128), PIECE)
            total = transposed(narrow, wide_ref[:, columns])
            if i < 2:
                kept_ref[2 * i + half] = total
            else:
                sent_ref[2 * i - 4 + half] = total.astype(BF16)


def read_act(act_ref):
    return act_ref[...]


def make_dpre(pre_ref, dact_ref):
    pre = pre_ref[...]
    t = tanh_of(pre)
    slope = 0.5 * (1.0 + t) + (0.5 * ROOT_2_PI) * pre * (1.0 - t * t) * (
        1.0 + (3.0 * 0.044715) * (pre * pre)
    )
    return (dact_ref[...].astype(F32) * slope).astype(BF16)


def partial_grad(narrow_of, name, flips, wide, *narrow, **ties):
    return launch(
        functools.partial(grad_kernel, narrow_of, flips), name,
        [(value, VMEM) for value in (wide, *narrow)],
        [(array((4, R, PIECE), F32), VMEM), (array((4, R, PIECE), BF16), VMEM)], **ties,
    )


def halve_kernel(kept_ref, came_ref, keep_ref, send_ref):
    keep_ref[...] = kept_ref[:2] + came_ref[:2].astype(F32)
    send_ref[...] = (kept_ref[2:] + came_ref[2:].astype(F32)).astype(BF16)


def halve(kept, came, **ties):
    return launch(
        halve_kernel, "halve", [(kept, VMEM), (came, VMEM)],
        [(array((2, R, PIECE), F32), VMEM), (array((2, R, PIECE), BF16), VMEM)], **ties,
    )


def split_kernel(kept_ref, came_ref, *out_refs):
    for half, out_ref in enumerate(out_refs):
        out_ref[...] = (kept_ref[half] + came_ref[half].astype(F32)).astype(BF16)


def split(kept, came, **ties):
    return launch(
        split_kernel, "split", [(kept, VMEM), (came, VMEM)],
        [(array((R, PIECE), BF16), VMEM)] * 2, **ties,
    )


def finish_kernel(one_ref, two_ref, out_ref):
    out_ref[...] = (one_ref[...].astype(F32) + two_ref[...].astype(F32)).T


def finish(parts):
    return launch(
        finish_kernel, "finish", [(part, VMEM) for part in parts],
        [(array((PIECE, R), F32), pl.BlockSpec((PIECE, R)))],
    )[0]


def feedback_kernel(first, count, before, x_ref, own_ref, act_ref, weight_ref, *refs):
    *rest, out_ref, out_sems = refs
    if before:
        rest = rest[1:]
    out_hbm = rest[0]
    for done_ref in rest[1:]:
        done_ref[...] = jnp.zeros_like(done_ref)
    copies = []
    for i in range(count // TILE):
        rows = slice(i * TILE, (i + 1) * TILE)
        act = act_ref[first + i * TILE : first + (i + 1) * TILE, :]
        for part in range(4):
            at = slice(part * 2 * PIECE, (part + 1) * 2 * PIECE)
            lifted = lax.dot_general(
                act, weight_ref[at, :], (((1,), (1,)), ((), ())), preferred_element_type=F32
            )
            value = x_ref[rows, at].astype(F32) + lifted - own_ref[rows, at].astype(F32)
            out_ref[rows, at] = value.astype(BF16)
        copies.append(
            pltpu.make_async_copy(
                out_ref.at[pl.ds(i * TILE, TILE)],
                out_hbm.at[pl.ds(first + i * TILE, TILE)],
                out_sems.at[i],
            )
        )
        copies[-1].start()
    for copy in copies:
        copy.wait()


def make_feedback(x, own, act, weight, first, before, marked):
    count = x.shape[0]
    ins = [(x, VMEM), (own, VMEM), (act, VMEM), (weight, VMEM)]
    if before is not None:
        ins.append((before, ANY))
    return launch(
        functools.partial(feedback_kernel, first, count, before is not None), "feedback", ins,
        [(array((TOK, D), BF16), ANY)] + [(array((8, 128), F32), VMEM)] * marked,
        [pltpu.VMEM((count, D), BF16), pltpu.SemaphoreType.DMA((count // TILE,))],
        aliases={} if before is None else {4: 0},
    )


def body(
    forward_codes,
    forward_scales,
    stored_base,
    sample_ids,
    backward_codes,
    backward_scales,
    norm_gain,
    w_down,
    w_up,
):
    sections = lax.axis_size("section")
    replicas = lax.axis_size("dp")
    across = replicas // 2
    both = ("section", "dp")

    def along(value, distance):
        pairs = [(s, (s + distance) % sections) for s in range(sections)]
        return lax.ppermute(value, "section", pairs)

    def among(value, flip_x, flip_y=0, section_step=0):
        pairs = []
        for s in range(sections):
            for d in range(replicas):
                y, x = divmod(d, across)
                source = (y ^ flip_y) * across + (x ^ flip_x)
                goal = ((s + section_step) % sections) * replicas + d
                pairs.append((s * replicas + source, goal))
        return lax.ppermute(value, both, pairs)

    up = w_up[0]
    up_before = along(up, 1)
    down_next = along(w_down[0], -1)
    gain_next = along(norm_gain, -1)

    codes, base = forward_codes[0], stored_base[0]
    scales = forward_scales[0].T
    firsts = [sum(SPANS[:k]) for k in range(len(SPANS))]
    message0, stats0 = make_messages(codes, scales, base, sample_ids, 0, SPANS[:1])
    *later, stats1 = make_messages(
        codes, scales, base, sample_ids, firsts[1], SPANS[1:], needs=[message0]
    )
    messages = [message0, *later]
    gradient = make_gradient(backward_codes[0], backward_scales[0].T, needs=[later[0]])

    hidden = make_hidden(messages, [stats0, stats1], gain_next, needs=[gradient])
    pre_next, act_next = project_down(hidden, down_next, needs=[up_before])
    act_before = along(act_next, 2)
    act_own = along(act_next, 1)
    arrived0 = along(messages[0], 1)
    dact_before = project_back(gradient, up_before, needs=[act_next])[0]
    dact_next = along(dact_before, -2)

    def feedback_of(own, x, at, before, marked=False):
        return make_feedback(x, own, act_own, up, firsts[at], before, marked)

    up_kept, up_sent, message1, message2 = partial_grad(
        read_act, "grad_up", (0, 1, 3, 2), gradient, act_before,
        needs=[act_own, arrived0, dact_next], carried=messages[1:3],
    )
    arrived1 = along(message1, 1)
    arrived2 = along(message2, 1)
    down_kept, down_sent = partial_grad(
        make_dpre, "grad_down", (0, 3, 1, 2), hidden, pre_next, dact_next,
    )
    feedback, done = feedback_of(messages[0], arrived0, 0, None, True)
    up_kept, up_sent, message3 = halve(
        up_kept, among(up_sent, 3), needs=[arrived1], carried=messages[3:4]
    )
    arrived3 = along(message3, 1)
    down_kept, down_sent = halve(down_kept, among(down_sent, 1), needs=[done])
    feedback, done = feedback_of(message1, arrived1, 1, feedback, True)
    up_parts = split(up_kept, among(up_sent, 1), needs=[arrived2])
    down_parts = split(down_kept, among(down_sent, 3), needs=[done])
    grad_up = finish([among(up_parts[half], 0, half, -1) for half in range(2)])
    grad_down = finish([among(down_parts[half], 0, half, 1) for half in range(2)])
    feedback = feedback_of(message2, arrived2, 2, feedback)[0]
    feedback = feedback_of(message3, arrived3, 3, feedback)[0]
    return (feedback[None], grad_down[None], grad_up[None])


def solution(mesh):
    in_specs = (
        P("section", "dp", None),
        P("section", "dp", None),
        P("section", "dp", None),
        P("section", "dp"),
        P("section", "dp", None),
        P("section", "dp", None),
        P("section", None),
        P("section", None, None),
        P("section", None, None),
    )
    out_specs = (P("section", "dp", None), P("section", "dp", None), P("section", "dp", None))
    return jax.shard_map(body, mesh=mesh, in_specs=in_specs, out_specs=out_specs, check_vma=False)
```

```python
import functools
import math

import jax
import jax.numpy as jnp
from jax import lax
from jax.experimental import pallas as pl
from jax.experimental.pallas import tpu as pltpu
from jax.sharding import PartitionSpec as P

D = 6144
R = 128
TOK = 384
PIECE = D // 8
F32 = jnp.float32
BF16 = jnp.bfloat16
TILE = 48
BLOCK = 768
WORDS = BLOCK // 3
CODES = BLOCK // 32
SPANS = (48, 144, 96, 96)
MIB = 1 << 20
ROOT_2_PI = math.sqrt(2.0 / math.pi)
VMEM = pl.BlockSpec(memory_space=pltpu.VMEM)
ANY = pl.BlockSpec(memory_space=pl.ANY)


def array(shape, dtype):
    return jax.ShapeDtypeStruct(shape, dtype)


def launch(
    kernel, name, ins, outs, scratch=(), grid=(), aliases=None, needs=(), carried=(), grant=14
):
    n_in, n_out = len(ins), len(outs)
    first_carried = n_in + len(needs)
    n_all = first_carried + len(carried)
    aliases = dict(aliases or {})
    for k in range(len(carried)):
        aliases[first_carried + k] = n_out + k

    def wrapped(*refs):
        rest = refs[n_all + n_out + len(carried) :]
        kernel(*refs[:n_in], *refs[n_all : n_all + n_out], *rest)

    return pl.pallas_call(
        wrapped,
        grid=grid,
        in_specs=[spec for _, spec in ins] + [ANY] * (len(needs) + len(carried)),
        out_specs=[spec for _, spec in outs] + [ANY] * len(carried),
        out_shape=[out for out, _ in outs] + [array(c.shape, c.dtype) for c in carried],
        scratch_shapes=scratch,
        input_output_aliases=aliases,
        compiler_params=pltpu.CompilerParams(vmem_limit_bytes=grant * MIB),
        cost_estimate=pl.CostEstimate(flops=1, bytes_accessed=1, transcendentals=0),
        name=name,
    )(*[value for value, _ in ins], *needs, *carried)


def lanes(shape):
    return lax.broadcasted_iota(jnp.int32, shape, 1)


def block_at(b):
    return pl.ds(pl.multiple_of(b * BLOCK, 128), BLOCK)


def spreader():
    shape = (32, BLOCK)
    return (lax.broadcasted_iota(jnp.int32, shape, 0) == lanes(shape) // 32).astype(F32).astype(
        BF16
    )


def turn_scales(scales_ref, turned_ref, rows):
    padding = jnp.zeros((32 - CODES, TOK), F32)
    for b in range(D // BLOCK):
        part = scales_ref[b * CODES : (b + 1) * CODES, :].astype(F32)
        turned_ref[b] = jnp.concatenate([part, padding], axis=0).T[rows].astype(BF16)


def exact(left, right):
    return jnp.dot(left, right, preferred_element_type=F32)


def chunks_of(out_refs):
    found, start = [], 0
    for ref in out_refs:
        count = ref.shape[0]
        for row in range(0, count, 96):
            found.append((ref, row, start + row, min(96, count - row)))
        start += count
    return found


def message_kernel(first, codes_ref, scales_ref, base_ref, ids_ref, *refs):
    *out_refs, stats_ref, turned_ref, picks_ref, pivot_ref, sum_ref, square_ref = refs
    count = stats_ref.shape[0]
    mine = slice(first, first + count)
    turn_scales(scales_ref, turned_ref, mine)
    spread = spreader()
    hits = lax.broadcasted_iota(jnp.int32, (32, TOK), 0) == ids_ref[...]
    picks_ref[...] = hits.astype(F32).T[mine].astype(BF16)
    chunks = chunks_of(out_refs)

    def decode(b, take):
        base_block = base_ref[:, block_at(b)]
        for ref, row, at, n in chunks:
            rows = slice(at, at + n)
            scale = exact(turned_ref[b, rows, :], spread)
            base = exact(picks_ref[rows, :], base_block)
            lane = lanes((n, 128))
            values = []
            for k in range(WORDS // 128):
                words_at = pl.ds(pl.multiple_of(b * WORDS + k * 128, 128), 128)
                words = codes_ref[first + at : first + at + n, words_at]
                for j in range(3):
                    spot = lane + 128 * j
                    word = jnp.take_along_axis(words, spot // 3, axis=1)
                    code = jnp.right_shift(word, (spot % 3) * 4) & 15
                    tile = 3 * k + j
                    part = slice(tile * 128, (tile + 1) * 128)
                    value = base[:, part] + scale[:, part] * (code - 8).astype(F32)
                    value = value.astype(BF16)
                    to = pl.ds(pl.multiple_of(b * BLOCK + tile * 128, 128), 128)
                    ref[row : row + n, to] = value
                    values.append(value.astype(F32))
            take(rows, n, values)

    def begin(rows, n, values):
        pivot = jnp.sum(sum(values), axis=1, keepdims=True) / BLOCK
        pivot = jnp.broadcast_to(pivot, (n, 128))
        pivot_ref[rows, :] = pivot
        away = [value - pivot for value in values]
        sum_ref[rows, :] = sum(away)
        square_ref[rows, :] = sum(v * v for v in away)

    def go_on(rows, n, values):
        pivot = pivot_ref[rows, :]
        away = [value - pivot for value in values]
        sum_ref[rows, :] += sum(away)
        square_ref[rows, :] += sum(v * v for v in away)

    def one_block(b, carry):
        decode(b, go_on)
        return carry

    decode(0, begin)
    lax.fori_loop(1, D // BLOCK, one_block, 0)
    shift = jnp.sum(sum_ref[...], axis=1, keepdims=True) * (1.0 / D)
    square = jnp.sum(square_ref[...], axis=1, keepdims=True) * (1.0 / D)
    variance = jnp.maximum(square - shift * shift, 0.0)
    stats_ref[:, :128] = pivot_ref[...] + shift
    stats_ref[:, 128:] = jnp.broadcast_to(lax.rsqrt(variance + 1e-05), (count, 128))


def make_messages(codes, scales, base, ids, first, spans, **ties):
    count = sum(spans)
    return launch(
        functools.partial(message_kernel, first), "message",
        [(value, VMEM) for value in (codes, scales, base, ids)],
        [(array((span, D), BF16), VMEM) for span in spans] + [(array((count, 256), F32), VMEM)],
        [pltpu.VMEM((D // BLOCK, count, 32), BF16), pltpu.VMEM((count, 32), BF16)]
        + [pltpu.VMEM((count, 128), F32)] * 3,
        **ties,
    )


def gradient_kernel(codes_ref, scales_ref, out_ref, turned_ref):
    turn_scales(scales_ref, turned_ref, slice(0, TOK))
    spread = spreader()

    def one_block(b, carry):
        for at in range(0, TOK, 96):
            rows = slice(at, at + 96)
            scale = exact(turned_ref[b, rows, :], spread)
            codes = codes_ref[rows, block_at(b)].astype(F32)
            out_ref[rows, block_at(b)] = (scale * (codes - 128.0)).astype(BF16)
        return carry

    lax.fori_loop(0, D // BLOCK, one_block, 0)


def make_gradient(codes, scales, **ties):
    return launch(
        gradient_kernel, "gradient", [(codes, VMEM), (scales, VMEM)],
        [(array((TOK, D), BF16), VMEM)], [pltpu.VMEM((D // BLOCK, TOK, 32), BF16)], **ties,
    )[0]


def tanh_of(pre):
    return jnp.tanh(ROOT_2_PI * (pre + 0.044715 * (pre * pre * pre)))


def hidden_kernel(n, gain_ref, *refs):
    message_refs, stats_refs, out_ref = refs[:n], refs[n:-1], refs[-1]
    messages, stats = [
        [(ref, at) for ref, row, _, rows in chunks_of(found) for at in range(row, row + rows, TILE)]
        for found in (message_refs, stats_refs)
    ]
    for t, ((ref, row), (stats_ref, stats_row)) in enumerate(zip(messages, stats)):
        rows = slice(stats_row, stats_row + TILE)
        mean, scale = stats_ref[rows, :128], stats_ref[rows, 128:]

        def one_block(b, carry, ref=ref, row=row, t=t, mean=mean, scale=scale):
            for c in range(BLOCK // 128):
                at = pl.ds(pl.multiple_of(b * BLOCK + c * 128, 128), 128)
                x = ref[row : row + TILE, at].astype(F32)
                value = gain_ref[:, at] * (x - mean) * scale
                out_ref[t * TILE : (t + 1) * TILE, at] = value.astype(BF16)
            return carry

        lax.fori_loop(0, D // BLOCK, one_block, 0)


def make_hidden(messages, stats, gain, **ties):
    return launch(
        functools.partial(hidden_kernel, len(messages)), "hidden",
        [(value, VMEM) for value in (gain, *messages, *stats)],
        [(array((TOK, D), BF16), VMEM)], **ties,
    )[0]


def down_kernel(hidden_ref, weight_ref, pre_ref, act_ref):
    pre = jnp.dot(hidden_ref[...], weight_ref[...], preferred_element_type=F32)
    pre_ref[...] = pre
    act_ref[...] = (0.5 * pre * (1.0 + tanh_of(pre))).astype(BF16)


def project_down(hidden, weight, **ties):
    return launch(
        down_kernel, "down", [(hidden, VMEM), (weight, VMEM)],
        [(array((TOK, R), F32), VMEM), (array((TOK, R), BF16), VMEM)], **ties,
    )


def back_kernel(grad_ref, weight_ref, out_ref):
    out_ref[...] = jnp.dot(
        grad_ref[...], weight_ref[...], preferred_element_type=F32
    ).astype(BF16)


def project_back(grad, weight, **ties):
    return launch(
        back_kernel, "back", [(grad, VMEM), (weight, VMEM)],
        [(array((TOK, R), BF16), VMEM)], **ties,
    )


def transposed(left, right):
    return lax.dot_general(left, right, (((0,), (0,)), ((), ())), preferred_element_type=F32)


def grad_kernel(narrow_of, flips, wide_ref, *refs):
    *narrow_refs, kept_ref, sent_ref = refs
    narrow = narrow_of(*narrow_refs)
    replica = lax.axis_index("dp")
    x_at, y_at = lax.rem(replica, 4), lax.div(replica, 4)
    for i, flip in enumerate(flips):
        for half in range(2):
            piece = (y_at ^ half) * 4 + (x_at ^ flip)
            columns = pl.ds(pl.multiple_of(piece * PIECE, 128), PIECE)
            total = transposed(narrow, wide_ref[:, columns])
            if i < 2:
                kept_ref[2 * i + half] = total
            else:
                sent_ref[2 * i - 4 + half] = total.astype(BF16)


def read_act(act_ref):
    return act_ref[...]


def make_dpre(pre_ref, dact_ref):
    pre = pre_ref[...]
    t = tanh_of(pre)
    slope = 0.5 * (1.0 + t) + (0.5 * ROOT_2_PI) * pre * (1.0 - t * t) * (
        1.0 + (3.0 * 0.044715) * (pre * pre)
    )
    return (dact_ref[...].astype(F32) * slope).astype(BF16)


def partial_grad(narrow_of, name, flips, wide, *narrow, **ties):
    return launch(
        functools.partial(grad_kernel, narrow_of, flips), name,
        [(value, VMEM) for value in (wide, *narrow)],
        [(array((4, R, PIECE), F32), VMEM), (array((4, R, PIECE), BF16), VMEM)], **ties,
    )


def halve_kernel(kept_ref, came_ref, keep_ref, send_ref):
    keep_ref[...] = kept_ref[:2] + came_ref[:2].astype(F32)
    send_ref[...] = (kept_ref[2:] + came_ref[2:].astype(F32)).astype(BF16)


def halve(kept, came, **ties):
    return launch(
        halve_kernel, "halve", [(kept, VMEM), (came, VMEM)],
        [(array((2, R, PIECE), F32), VMEM), (array((2, R, PIECE), BF16), VMEM)], **ties,
    )


def split_kernel(kept_ref, came_ref, *out_refs):
    for half, out_ref in enumerate(out_refs):
        out_ref[...] = (kept_ref[half] + came_ref[half].astype(F32)).astype(BF16)


def split(kept, came, **ties):
    return launch(
        split_kernel, "split", [(kept, VMEM), (came, VMEM)],
        [(array((R, PIECE), BF16), VMEM)] * 2, **ties,
    )


def finish_kernel(one_ref, two_ref, out_ref):
    out_ref[...] = (one_ref[...].astype(F32) + two_ref[...].astype(F32)).T


def finish(parts):
    return launch(
        finish_kernel, "finish", [(part, VMEM) for part in parts],
        [(array((PIECE, R), F32), pl.BlockSpec((PIECE, R)))],
    )[0]


def feedback_kernel(first, count, before, x_ref, own_ref, act_ref, weight_ref, *refs):
    *rest, out_ref, out_sems = refs
    if before:
        rest = rest[1:]
    out_hbm = rest[0]
    for done_ref in rest[1:]:
        done_ref[...] = jnp.zeros_like(done_ref)
    copies = []
    for i in range(count // TILE):
        rows = slice(i * TILE, (i + 1) * TILE)
        act = act_ref[first + i * TILE : first + (i + 1) * TILE, :]
        for part in range(4):
            at = slice(part * 2 * PIECE, (part + 1) * 2 * PIECE)
            lifted = lax.dot_general(
                act, weight_ref[at, :], (((1,), (1,)), ((), ())), preferred_element_type=F32
            )
            value = x_ref[rows, at].astype(F32) + lifted - own_ref[rows, at].astype(F32)
            out_ref[rows, at] = value.astype(BF16)
        copies.append(
            pltpu.make_async_copy(
                out_ref.at[pl.ds(i * TILE, TILE)],
                out_hbm.at[pl.ds(first + i * TILE, TILE)],
                out_sems.at[i],
            )
        )
        copies[-1].start()
    for copy in copies:
        copy.wait()


def make_feedback(x, own, act, weight, first, before, marked):
    count = x.shape[0]
    ins = [(x, VMEM), (own, VMEM), (act, VMEM), (weight, VMEM)]
    if before is not None:
        ins.append((before, ANY))
    return launch(
        functools.partial(feedback_kernel, first, count, before is not None), "feedback", ins,
        [(array((TOK, D), BF16), ANY)] + [(array((8, 128), F32), VMEM)] * marked,
        [pltpu.VMEM((count, D), BF16), pltpu.SemaphoreType.DMA((count // TILE,))],
        aliases={} if before is None else {4: 0},
    )


def body(
    forward_codes,
    forward_scales,
    stored_base,
    sample_ids,
    backward_codes,
    backward_scales,
    norm_gain,
    w_down,
    w_up,
):
    sections = lax.axis_size("section")
    replicas = lax.axis_size("dp")
    across = replicas // 2
    both = ("section", "dp")

    def along(value, distance):
        pairs = [(s, (s + distance) % sections) for s in range(sections)]
        return lax.ppermute(value, "section", pairs)

    def among(value, flip_x, flip_y=0, section_step=0):
        pairs = []
        for s in range(sections):
            for d in range(replicas):
                y, x = divmod(d, across)
                source = (y ^ flip_y) * across + (x ^ flip_x)
                goal = ((s + section_step) % sections) * replicas + d
                pairs.append((s * replicas + source, goal))
        return lax.ppermute(value, both, pairs)

    up = w_up[0]
    up_before = along(up, 1)
    down_next = along(w_down[0], -1)
    gain_next = along(norm_gain, -1)

    codes, base = forward_codes[0], stored_base[0]
    scales = forward_scales[0].T
    firsts = [sum(SPANS[:k]) for k in range(len(SPANS))]
    message0, stats0 = make_messages(codes, scales, base, sample_ids, 0, SPANS[:1])
    *later, stats1 = make_messages(
        codes, scales, base, sample_ids, firsts[1], SPANS[1:], needs=[message0]
    )
    messages = [message0, *later]
    gradient = make_gradient(backward_codes[0], backward_scales[0].T, needs=[later[0]])

    hidden = make_hidden(messages, [stats0, stats1], gain_next, needs=[gradient])
    pre_next, act_next = project_down(hidden, down_next, needs=[up_before])
    act_before = along(act_next, 2)
    act_own = along(act_next, 1)
    arrived0 = along(messages[0], 1)
    dact_before = project_back(gradient, up_before, needs=[act_next])[0]
    dact_next = along(dact_before, -2)

    def feedback_of(own, x, at, before, marked=False):
        return make_feedback(x, own, act_own, up, firsts[at], before, marked)

    up_kept, up_sent, message1, message2 = partial_grad(
        read_act, "grad_up", (0, 1, 3, 2), gradient, act_before,
        needs=[act_own, arrived0, dact_next], carried=messages[1:3],
    )
    arrived1 = along(message1, 1)
    arrived2 = along(message2, 1)
    down_kept, down_sent = partial_grad(
        make_dpre, "grad_down", (0, 3, 1, 2), hidden, pre_next, dact_next,
    )
    feedback, done = feedback_of(messages[0], arrived0, 0, None, True)
    up_kept, up_sent, message3 = halve(
        up_kept, among(up_sent, 3), needs=[arrived1], carried=messages[3:4]
    )
    arrived3 = along(message3, 1)
    down_kept, down_sent = halve(down_kept, among(down_sent, 1), needs=[done])
    feedback, done = feedback_of(message1, arrived1, 1, feedback, True)
    up_parts = split(up_kept, among(up_sent, 1), needs=[arrived2])
    down_parts = split(down_kept, among(down_sent, 3), needs=[done])
    grad_up = finish([among(up_parts[half], 0, half, -1) for half in range(2)])
    grad_down = finish([among(down_parts[half], 0, half, 1) for half in range(2)])
    feedback = feedback_of(message2, arrived2, 2, feedback)[0]
    feedback = feedback_of(message3, arrived3, 3, feedback)[0]
    return (feedback[None], grad_down[None], grad_up[None])


def solution(mesh):
    in_specs = (
        P("section", "dp", None),
        P("section", "dp", None),
        P("section", "dp", None),
        P("section", "dp"),
        P("section", "dp", None),
        P("section", "dp", None),
        P("section", None),
        P("section", None, None),
        P("section", None, None),
    )
    out_specs = (P("section", "dp", None), P("section", "dp", None), P("section", "dp", None))
    return jax.shard_map(body, mesh=mesh, in_specs=in_specs, out_specs=out_specs, check_vma=False)
```

```python
import functools
import math

import jax
import jax.numpy as jnp
from jax import lax
from jax.experimental import pallas as pl
from jax.experimental.pallas import tpu as pltpu
from jax.sharding import PartitionSpec as P

D = 6144
R = 128
TOK = 384
PIECE = D // 8
F32 = jnp.float32
BF16 = jnp.bfloat16
TILE = 48
BLOCK = 768
WORDS = BLOCK // 3
CODES = BLOCK // 32
SPANS = (48, 96, 96, 96, 48)
MIB = 1 << 20
ROOT_2_PI = math.sqrt(2.0 / math.pi)
VMEM = pl.BlockSpec(memory_space=pltpu.VMEM)
ANY = pl.BlockSpec(memory_space=pl.ANY)


def array(shape, dtype):
    return jax.ShapeDtypeStruct(shape, dtype)


def launch(
    kernel, name, ins, outs, scratch=(), grid=(), aliases=None, needs=(), carried=(), grant=14
):
    n_in, n_out = len(ins), len(outs)
    first_carried = n_in + len(needs)
    n_all = first_carried + len(carried)
    aliases = dict(aliases or {})
    for k in range(len(carried)):
        aliases[first_carried + k] = n_out + k

    def wrapped(*refs):
        rest = refs[n_all + n_out + len(carried) :]
        kernel(*refs[:n_in], *refs[n_all : n_all + n_out], *rest)

    return pl.pallas_call(
        wrapped,
        grid=grid,
        in_specs=[spec for _, spec in ins] + [ANY] * (len(needs) + len(carried)),
        out_specs=[spec for _, spec in outs] + [ANY] * len(carried),
        out_shape=[out for out, _ in outs] + [array(c.shape, c.dtype) for c in carried],
        scratch_shapes=scratch,
        input_output_aliases=aliases,
        compiler_params=pltpu.CompilerParams(vmem_limit_bytes=grant * MIB),
        cost_estimate=pl.CostEstimate(flops=1, bytes_accessed=1, transcendentals=0),
        name=name,
    )(*[value for value, _ in ins], *needs, *carried)


def lanes(shape):
    return lax.broadcasted_iota(jnp.int32, shape, 1)


def block_at(b):
    return pl.ds(pl.multiple_of(b * BLOCK, 128), BLOCK)


def spreader():
    shape = (32, BLOCK)
    return (lax.broadcasted_iota(jnp.int32, shape, 0) == lanes(shape) // 32).astype(F32).astype(
        BF16
    )


def turn_scales(scales_ref, turned_ref, rows):
    padding = jnp.zeros((32 - CODES, TOK), F32)
    for b in range(D // BLOCK):
        part = scales_ref[b * CODES : (b + 1) * CODES, :].astype(F32)
        turned_ref[b] = jnp.concatenate([part, padding], axis=0).T[rows].astype(BF16)


def exact(left, right):
    return jnp.dot(left, right, preferred_element_type=F32)


def chunks_of(out_refs):
    found, start = [], 0
    for ref in out_refs:
        count = ref.shape[0]
        for row in range(0, count, 96):
            found.append((ref, row, start + row, min(96, count - row)))
        start += count
    return found


def message_kernel(first, codes_ref, scales_ref, base_ref, ids_ref, *refs):
    *out_refs, stats_ref, turned_ref, picks_ref, pivot_ref, sum_ref, square_ref = refs
    count = stats_ref.shape[0]
    mine = slice(first, first + count)
    turn_scales(scales_ref, turned_ref, mine)
    spread = spreader()
    hits = lax.broadcasted_iota(jnp.int32, (32, TOK), 0) == ids_ref[...]
    picks_ref[...] = hits.astype(F32).T[mine].astype(BF16)
    chunks = chunks_of(out_refs)

    def decode(b, take):
        base_block = base_ref[:, block_at(b)]
        for ref, row, at, n in chunks:
            rows = slice(at, at + n)
            scale = exact(turned_ref[b, rows, :], spread)
            base = exact(picks_ref[rows, :], base_block)
            lane = lanes((n, 128))
            values = []
            for k in range(WORDS // 128):
                words_at = pl.ds(pl.multiple_of(b * WORDS + k * 128, 128), 128)
                words = codes_ref[first + at : first + at + n, words_at]
                for j in range(3):
                    spot = lane + 128 * j
                    word = jnp.take_along_axis(words, spot // 3, axis=1)
                    code = jnp.right_shift(word, (spot % 3) * 4) & 15
                    tile = 3 * k + j
                    part = slice(tile * 128, (tile + 1) * 128)
                    value = base[:, part] + scale[:, part] * (code - 8).astype(F32)
                    value = value.astype(BF16)
                    to = pl.ds(pl.multiple_of(b * BLOCK + tile * 128, 128), 128)
                    ref[row : row + n, to] = value
                    values.append(value.astype(F32))
            take(rows, n, values)

    def begin(rows, n, values):
        pivot = jnp.sum(sum(values), axis=1, keepdims=True) / BLOCK
        pivot = jnp.broadcast_to(pivot, (n, 128))
        pivot_ref[rows, :] = pivot
        away = [value - pivot for value in values]
        sum_ref[rows, :] = sum(away)
        square_ref[rows, :] = sum(v * v for v in away)

    def go_on(rows, n, values):
        pivot = pivot_ref[rows, :]
        away = [value - pivot for value in values]
        sum_ref[rows, :] += sum(away)
        square_ref[rows, :] += sum(v * v for v in away)

    def one_block(b, carry):
        decode(b, go_on)
        return carry

    decode(0, begin)
    lax.fori_loop(1, D // BLOCK, one_block, 0)
    shift = jnp.sum(sum_ref[...], axis=1, keepdims=True) * (1.0 / D)
    square = jnp.sum(square_ref[...], axis=1, keepdims=True) * (1.0 / D)
    variance = jnp.maximum(square - shift * shift, 0.0)
    stats_ref[:, :128] = pivot_ref[...] + shift
    stats_ref[:, 128:] = jnp.broadcast_to(lax.rsqrt(variance + 1e-05), (count, 128))


def make_messages(codes, scales, base, ids, first, spans, **ties):
    count = sum(spans)
    return launch(
        functools.partial(message_kernel, first), "message",
        [(value, VMEM) for value in (codes, scales, base, ids)],
        [(array((span, D), BF16), VMEM) for span in spans] + [(array((count, 256), F32), VMEM)],
        [pltpu.VMEM((D // BLOCK, count, 32), BF16), pltpu.VMEM((count, 32), BF16)]
        + [pltpu.VMEM((count, 128), F32)] * 3,
        **ties,
    )


def gradient_kernel(codes_ref, scales_ref, out_ref, turned_ref):
    turn_scales(scales_ref, turned_ref, slice(0, TOK))
    spread = spreader()

    def one_block(b, carry):
        for at in range(0, TOK, 96):
            rows = slice(at, at + 96)
            scale = exact(turned_ref[b, rows, :], spread)
            codes = codes_ref[rows, block_at(b)].astype(F32)
            out_ref[rows, block_at(b)] = (scale * (codes - 128.0)).astype(BF16)
        return carry

    lax.fori_loop(0, D // BLOCK, one_block, 0)


def make_gradient(codes, scales, **ties):
    return launch(
        gradient_kernel, "gradient", [(codes, VMEM), (scales, VMEM)],
        [(array((TOK, D), BF16), VMEM)], [pltpu.VMEM((D // BLOCK, TOK, 32), BF16)], **ties,
    )[0]


def tanh_of(pre):
    return jnp.tanh(ROOT_2_PI * (pre + 0.044715 * (pre * pre * pre)))


def hidden_kernel(n, gain_ref, *refs):
    message_refs, stats_refs, out_ref = refs[:n], refs[n:-1], refs[-1]
    messages, stats = [
        [(ref, at) for ref, row, _, rows in chunks_of(found) for at in range(row, row + rows, TILE)]
        for found in (message_refs, stats_refs)
    ]
    for t, ((ref, row), (stats_ref, stats_row)) in enumerate(zip(messages, stats)):
        rows = slice(stats_row, stats_row + TILE)
        mean, scale = stats_ref[rows, :128], stats_ref[rows, 128:]

        def one_block(b, carry, ref=ref, row=row, t=t, mean=mean, scale=scale):
            for c in range(BLOCK // 128):
                at = pl.ds(pl.multiple_of(b * BLOCK + c * 128, 128), 128)
                x = ref[row : row + TILE, at].astype(F32)
                value = gain_ref[:, at] * (x - mean) * scale
                out_ref[t * TILE : (t + 1) * TILE, at] = value.astype(BF16)
            return carry

        lax.fori_loop(0, D // BLOCK, one_block, 0)


def make_hidden(messages, stats, gain, **ties):
    return launch(
        functools.partial(hidden_kernel, len(messages)), "hidden",
        [(value, VMEM) for value in (gain, *messages, *stats)],
        [(array((TOK, D), BF16), VMEM)], **ties,
    )[0]


def down_kernel(hidden_ref, weight_ref, pre_ref, act_ref):
    pre = jnp.dot(hidden_ref[...], weight_ref[...], preferred_element_type=F32)
    pre_ref[...] = pre
    act_ref[...] = (0.5 * pre * (1.0 + tanh_of(pre))).astype(BF16)


def project_down(hidden, weight, **ties):
    return launch(
        down_kernel, "down", [(hidden, VMEM), (weight, VMEM)],
        [(array((TOK, R), F32), VMEM), (array((TOK, R), BF16), VMEM)], **ties,
    )


def back_kernel(grad_ref, weight_ref, out_ref):
    out_ref[...] = jnp.dot(
        grad_ref[...], weight_ref[...], preferred_element_type=F32
    ).astype(BF16)


def project_back(grad, weight, **ties):
    return launch(
        back_kernel, "back", [(grad, VMEM), (weight, VMEM)],
        [(array((TOK, R), BF16), VMEM)], **ties,
    )


def transposed(left, right):
    return lax.dot_general(left, right, (((0,), (0,)), ((), ())), preferred_element_type=F32)


def grad_kernel(narrow_of, flips, wide_ref, *refs):
    *narrow_refs, kept_ref, sent_ref = refs
    narrow = narrow_of(*narrow_refs)
    replica = lax.axis_index("dp")
    x_at, y_at = lax.rem(replica, 4), lax.div(replica, 4)
    for i, flip in enumerate(flips):
        for half in range(2):
            piece = (y_at ^ half) * 4 + (x_at ^ flip)
            columns = pl.ds(pl.multiple_of(piece * PIECE, 128), PIECE)
            total = transposed(narrow, wide_ref[:, columns])
            if i < 2:
                kept_ref[2 * i + half] = total
            else:
                sent_ref[2 * i - 4 + half] = total.astype(BF16)


def read_act(act_ref):
    return act_ref[...]


def make_dpre(pre_ref, dact_ref):
    pre = pre_ref[...]
    t = tanh_of(pre)
    slope = 0.5 * (1.0 + t) + (0.5 * ROOT_2_PI) * pre * (1.0 - t * t) * (
        1.0 + (3.0 * 0.044715) * (pre * pre)
    )
    return (dact_ref[...].astype(F32) * slope).astype(BF16)


def partial_grad(narrow_of, name, flips, wide, *narrow, **ties):
    return launch(
        functools.partial(grad_kernel, narrow_of, flips), name,
        [(value, VMEM) for value in (wide, *narrow)],
        [(array((4, R, PIECE), F32), VMEM), (array((4, R, PIECE), BF16), VMEM)], **ties,
    )


def halve_kernel(kept_ref, came_ref, keep_ref, send_ref):
    keep_ref[...] = kept_ref[:2] + came_ref[:2].astype(F32)
    send_ref[...] = (kept_ref[2:] + came_ref[2:].astype(F32)).astype(BF16)


def halve(kept, came, **ties):
    return launch(
        halve_kernel, "halve", [(kept, VMEM), (came, VMEM)],
        [(array((2, R, PIECE), F32), VMEM), (array((2, R, PIECE), BF16), VMEM)], **ties,
    )


def split_kernel(kept_ref, came_ref, *out_refs):
    for half, out_ref in enumerate(out_refs):
        out_ref[...] = (kept_ref[half] + came_ref[half].astype(F32)).astype(BF16)


def split(kept, came, **ties):
    return launch(
        split_kernel, "split", [(kept, VMEM), (came, VMEM)],
        [(array((R, PIECE), BF16), VMEM)] * 2, **ties,
    )


def finish_kernel(one_ref, two_ref, out_ref):
    out_ref[...] = (one_ref[...].astype(F32) + two_ref[...].astype(F32)).T


def finish(parts):
    return launch(
        finish_kernel, "finish", [(part, VMEM) for part in parts],
        [(array((PIECE, R), F32), pl.BlockSpec((PIECE, R)))],
    )[0]


def feedback_kernel(first, count, before, x_ref, own_ref, act_ref, weight_ref, *refs):
    *rest, out_ref, out_sems = refs
    if before:
        rest = rest[1:]
    out_hbm = rest[0]
    for done_ref in rest[1:]:
        done_ref[...] = jnp.zeros_like(done_ref)
    copies = []
    for i in range(count // TILE):
        rows = slice(i * TILE, (i + 1) * TILE)
        act = act_ref[first + i * TILE : first + (i + 1) * TILE, :]
        for part in range(4):
            at = slice(part * 2 * PIECE, (part + 1) * 2 * PIECE)
            lifted = lax.dot_general(
                act, weight_ref[at, :], (((1,), (1,)), ((), ())), preferred_element_type=F32
            )
            value = x_ref[rows, at].astype(F32) + lifted - own_ref[rows, at].astype(F32)
            out_ref[rows, at] = value.astype(BF16)
        copies.append(
            pltpu.make_async_copy(
                out_ref.at[pl.ds(i * TILE, TILE)],
                out_hbm.at[pl.ds(first + i * TILE, TILE)],
                out_sems.at[i],
            )
        )
        copies[-1].start()
    for copy in copies:
        copy.wait()


def make_feedback(x, own, act, weight, first, before, marked):
    count = x.shape[0]
    ins = [(x, VMEM), (own, VMEM), (act, VMEM), (weight, VMEM)]
    if before is not None:
        ins.append((before, ANY))
    return launch(
        functools.partial(feedback_kernel, first, count, before is not None), "feedback", ins,
        [(array((TOK, D), BF16), ANY)] + [(array((8, 128), F32), VMEM)] * marked,
        [pltpu.VMEM((count, D), BF16), pltpu.SemaphoreType.DMA((count // TILE,))],
        aliases={} if before is None else {4: 0},
    )


def body(
    forward_codes,
    forward_scales,
    stored_base,
    sample_ids,
    backward_codes,
    backward_scales,
    norm_gain,
    w_down,
    w_up,
):
    sections = lax.axis_size("section")
    replicas = lax.axis_size("dp")
    across = replicas // 2
    both = ("section", "dp")

    def along(value, distance):
        pairs = [(s, (s + distance) % sections) for s in range(sections)]
        return lax.ppermute(value, "section", pairs)

    def among(value, flip_x, flip_y=0, section_step=0):
        pairs = []
        for s in range(sections):
            for d in range(replicas):
                y, x = divmod(d, across)
                source = (y ^ flip_y) * across + (x ^ flip_x)
                goal = ((s + section_step) % sections) * replicas + d
                pairs.append((s * replicas + source, goal))
        return lax.ppermute(value, both, pairs)

    up = w_up[0]
    up_before = along(up, 1)
    down_next = along(w_down[0], -1)
    gain_next = along(norm_gain, -1)

    codes, base = forward_codes[0], stored_base[0]
    scales = forward_scales[0].T
    firsts = [sum(SPANS[:k]) for k in range(len(SPANS))]
    message0, stats0 = make_messages(codes, scales, base, sample_ids, 0, SPANS[:1])
    *later, stats1 = make_messages(
        codes, scales, base, sample_ids, firsts[1], SPANS[1:], needs=[message0]
    )
    messages = [message0, *later]
    gradient = make_gradient(backward_codes[0], backward_scales[0].T, needs=[later[0]])

    hidden = make_hidden(messages, [stats0, stats1], gain_next, needs=[gradient])
    pre_next, act_next = project_down(hidden, down_next, needs=[up_before])
    act_before = along(act_next, 2)
    act_own = along(act_next, 1)
    arrived0 = along(messages[0], 1)
    dact_before = project_back(gradient, up_before, needs=[act_next])[0]
    dact_next = along(dact_before, -2)

    def feedback_of(own, x, at, before, marked=False):
        return make_feedback(x, own, act_own, up, firsts[at], before, marked)

    up_kept, up_sent, message1, message2 = partial_grad(
        read_act, "grad_up", (0, 1, 3, 2), gradient, act_before,
        needs=[act_own, arrived0, dact_next], carried=messages[1:3],
    )
    arrived1 = along(message1, 1)
    arrived2 = along(message2, 1)
    down_kept, down_sent = partial_grad(
        make_dpre, "grad_down", (0, 3, 1, 2), hidden, pre_next, dact_next,
    )
    feedback, done = feedback_of(messages[0], arrived0, 0, None, True)
    up_kept, up_sent, message3 = halve(
        up_kept, among(up_sent, 3), needs=[arrived1, done], carried=messages[3:4]
    )
    arrived3 = along(message3, 1)
    down_kept, down_sent = halve(down_kept, among(down_sent, 1), needs=[up_sent])
    feedback, done = feedback_of(message1, arrived1, 1, feedback, True)
    *up_parts, message4 = split(
        up_kept, among(up_sent, 1), needs=[arrived2, done], carried=messages[4:5]
    )
    arrived4 = along(message4, 1)
    down_parts = split(down_kept, among(down_sent, 3), needs=[up_parts[0]])
    grad_up = finish([among(up_parts[half], 0, half, -1) for half in range(2)])
    grad_down = finish([among(down_parts[half], 0, half, 1) for half in range(2)])
    feedback = feedback_of(message2, arrived2, 2, feedback)[0]
    feedback = feedback_of(message3, arrived3, 3, feedback)[0]
    feedback = feedback_of(message4, arrived4, 4, feedback)[0]
    return (feedback[None], grad_down[None], grad_up[None])


def solution(mesh):
    in_specs = (
        P("section", "dp", None),
        P("section", "dp", None),
        P("section", "dp", None),
        P("section", "dp"),
        P("section", "dp", None),
        P("section", "dp", None),
        P("section", None),
        P("section", None, None),
        P("section", None, None),
    )
    out_specs = (P("section", "dp", None), P("section", "dp", None), P("section", "dp", None))
    return jax.shard_map(body, mesh=mesh, in_specs=in_specs, out_specs=out_specs, check_vma=False)
```

```python
import functools
import math

import jax
import jax.numpy as jnp
from jax import lax
from jax.experimental import pallas as pl
from jax.experimental.pallas import tpu as pltpu
from jax.sharding import PartitionSpec as P

D = 6144
R = 128
TOK = 384
PIECE = D // 8
F32 = jnp.float32
BF16 = jnp.bfloat16
TILE = 48
BLOCK = 768
HALF = D // 2
WORDS = BLOCK // 3
CODES = BLOCK // 32
SPANS = (96, 96, 96, 96)
MIB = 1 << 20
ROOT_2_PI = math.sqrt(2.0 / math.pi)
VMEM = pl.BlockSpec(memory_space=pltpu.VMEM)
ANY = pl.BlockSpec(memory_space=pl.ANY)


def array(shape, dtype):
    return jax.ShapeDtypeStruct(shape, dtype)


def launch(
    kernel, name, ins, outs, scratch=(), grid=(), aliases=None, needs=(), carried=(), grant=14
):
    n_in, n_out = len(ins), len(outs)
    first_carried = n_in + len(needs)
    n_all = first_carried + len(carried)
    aliases = dict(aliases or {})
    for k in range(len(carried)):
        aliases[first_carried + k] = n_out + k

    def wrapped(*refs):
        rest = refs[n_all + n_out + len(carried) :]
        kernel(*refs[:n_in], *refs[n_all : n_all + n_out], *rest)

    return pl.pallas_call(
        wrapped,
        grid=grid,
        in_specs=[spec for _, spec in ins] + [ANY] * (len(needs) + len(carried)),
        out_specs=[spec for _, spec in outs] + [ANY] * len(carried),
        out_shape=[out for out, _ in outs] + [array(c.shape, c.dtype) for c in carried],
        scratch_shapes=scratch,
        input_output_aliases=aliases,
        compiler_params=pltpu.CompilerParams(vmem_limit_bytes=grant * MIB),
        cost_estimate=pl.CostEstimate(flops=1, bytes_accessed=1, transcendentals=0),
        name=name,
    )(*[value for value, _ in ins], *needs, *carried)


def hand_on(value, after):
    return launch(lambda: None, "hand_on", [], [], needs=[after], carried=[value], grant=1)[0]


def lanes(shape):
    return lax.broadcasted_iota(jnp.int32, shape, 1)


def block_at(b):
    return pl.ds(pl.multiple_of(b * BLOCK, 128), BLOCK)


def spreader():
    shape = (32, BLOCK)
    return (lax.broadcasted_iota(jnp.int32, shape, 0) == lanes(shape) // 32).astype(F32).astype(
        BF16
    )


def turn_scales(scales_ref, turned_ref, rows):
    padding = jnp.zeros((32 - CODES, TOK), F32)
    for b in range(D // BLOCK):
        part = scales_ref[b * CODES : (b + 1) * CODES, :].astype(F32)
        turned_ref[b] = jnp.concatenate([part, padding], axis=0).T[rows].astype(BF16)


def exact(left, right):
    return jnp.dot(left, right, preferred_element_type=F32)


def chunks_of(out_refs):
    found, start = [], 0
    for ref in out_refs:
        count = ref.shape[0]
        for row in range(0, count, 96):
            found.append((ref, row, start + row, min(96, count - row)))
        start += count
    return found


def message_kernel(first, codes_ref, scales_ref, base_ref, ids_ref, *refs):
    *out_refs, stats_ref, turned_ref, picks_ref, pivot_ref, sum_ref, square_ref = refs
    count = stats_ref.shape[0]
    mine = slice(first, first + count)
    turn_scales(scales_ref, turned_ref, mine)
    spread = spreader()
    hits = lax.broadcasted_iota(jnp.int32, (32, TOK), 0) == ids_ref[...]
    picks_ref[...] = hits.astype(F32).T[mine].astype(BF16)
    chunks = chunks_of(out_refs)

    def decode(b, take):
        base_block = base_ref[:, block_at(b)]
        for ref, row, at, n in chunks:
            rows = slice(at, at + n)
            scale = exact(turned_ref[b, rows, :], spread)
            base = exact(picks_ref[rows, :], base_block)
            lane = lanes((n, 128))
            values = []
            for k in range(WORDS // 128):
                words_at = pl.ds(pl.multiple_of(b * WORDS + k * 128, 128), 128)
                words = codes_ref[first + at : first + at + n, words_at]
                for j in range(3):
                    spot = lane + 128 * j
                    word = jnp.take_along_axis(words, spot // 3, axis=1)
                    code = jnp.right_shift(word, (spot % 3) * 4) & 15
                    tile = 3 * k + j
                    part = slice(tile * 128, (tile + 1) * 128)
                    value = base[:, part] + scale[:, part] * (code - 8).astype(F32)
                    value = value.astype(BF16)
                    to = pl.ds(pl.multiple_of(b * BLOCK + tile * 128, 128), 128)
                    ref[row : row + n, to] = value
                    values.append(value.astype(F32))
            take(rows, n, values)

    def begin(rows, n, values):
        pivot = jnp.sum(sum(values), axis=1, keepdims=True) / BLOCK
        pivot = jnp.broadcast_to(pivot, (n, 128))
        pivot_ref[rows, :] = pivot
        away = [value - pivot for value in values]
        sum_ref[rows, :] = sum(away)
        square_ref[rows, :] = sum(v * v for v in away)

    def go_on(rows, n, values):
        pivot = pivot_ref[rows, :]
        away = [value - pivot for value in values]
        sum_ref[rows, :] += sum(away)
        square_ref[rows, :] += sum(v * v for v in away)

    def one_block(b, carry):
        decode(b, go_on)
        return carry

    decode(0, begin)
    lax.fori_loop(1, D // BLOCK, one_block, 0)
    shift = jnp.sum(sum_ref[...], axis=1, keepdims=True) * (1.0 / D)
    square = jnp.sum(square_ref[...], axis=1, keepdims=True) * (1.0 / D)
    variance = jnp.maximum(square - shift * shift, 0.0)
    stats_ref[:, :128] = pivot_ref[...] + shift
    stats_ref[:, 128:] = jnp.broadcast_to(lax.rsqrt(variance + 1e-05), (count, 128))


def make_messages(codes, scales, base, ids, first, spans, **ties):
    count = sum(spans)
    return launch(
        functools.partial(message_kernel, first), "message",
        [(value, VMEM) for value in (codes, scales, base, ids)],
        [(array((span, D), BF16), VMEM) for span in spans] + [(array((count, 256), F32), VMEM)],
        [pltpu.VMEM((D // BLOCK, count, 32), BF16), pltpu.VMEM((count, 32), BF16)]
        + [pltpu.VMEM((count, 128), F32)] * 3,
        **ties,
    )


def gradient_kernel(codes_ref, scales_ref, out_ref, turned_ref):
    turn_scales(scales_ref, turned_ref, slice(0, TOK))
    spread = spreader()

    def one_block(b, carry):
        for at in range(0, TOK, 96):
            rows = slice(at, at + 96)
            scale = exact(turned_ref[b, rows, :], spread)
            codes = codes_ref[rows, block_at(b)].astype(F32)
            out_ref[rows, block_at(b)] = (scale * (codes - 128.0)).astype(BF16)
        return carry

    lax.fori_loop(0, D // BLOCK, one_block, 0)


def make_gradient(codes, scales, **ties):
    return launch(
        gradient_kernel, "gradient", [(codes, VMEM), (scales, VMEM)],
        [(array((TOK, D), BF16), VMEM)], [pltpu.VMEM((D // BLOCK, TOK, 32), BF16)], **ties,
    )[0]


def tanh_of(pre):
    return jnp.tanh(ROOT_2_PI * (pre + 0.044715 * (pre * pre * pre)))


def hidden_kernel(n, gain_ref, *refs):
    message_refs, stats_refs, out_ref = refs[:n], refs[n:-1], refs[-1]
    messages, stats = [
        [(ref, at) for ref, row, _, rows in chunks_of(found) for at in range(row, row + rows, TILE)]
        for found in (message_refs, stats_refs)
    ]
    for t, ((ref, row), (stats_ref, stats_row)) in enumerate(zip(messages, stats)):
        rows = slice(stats_row, stats_row + TILE)
        mean, scale = stats_ref[rows, :128], stats_ref[rows, 128:]

        def one_block(b, carry, ref=ref, row=row, t=t, mean=mean, scale=scale):
            for c in range(BLOCK // 128):
                at = pl.ds(pl.multiple_of(b * BLOCK + c * 128, 128), 128)
                x = ref[row : row + TILE, at].astype(F32)
                value = gain_ref[:, at] * (x - mean) * scale
                out_ref[t * TILE : (t + 1) * TILE, at] = value.astype(BF16)
            return carry

        lax.fori_loop(0, D // BLOCK, one_block, 0)


def make_hidden(messages, stats, gain, **ties):
    return launch(
        functools.partial(hidden_kernel, len(messages)), "hidden",
        [(value, VMEM) for value in (gain, *messages, *stats)],
        [(array((TOK, D), BF16), VMEM)], **ties,
    )[0]


def down_kernel(hidden_ref, weight_ref, pre_ref, act_ref):
    pre = jnp.dot(hidden_ref[...], weight_ref[...], preferred_element_type=F32)
    pre_ref[...] = pre
    act_ref[...] = (0.5 * pre * (1.0 + tanh_of(pre))).astype(BF16)


def project_down(hidden, weight, **ties):
    return launch(
        down_kernel, "down", [(hidden, VMEM), (weight, VMEM)],
        [(array((TOK, R), F32), VMEM), (array((TOK, R), BF16), VMEM)], **ties,
    )


def pick_half_kernel(weight_ref, out_ref, sem):
    half = lax.rem(lax.axis_index("dp"), 2)
    rows = pl.ds(pl.multiple_of(half * HALF, HALF), HALF)
    copy = pltpu.make_async_copy(weight_ref.at[rows], out_ref, sem.at[0])
    copy.start()
    copy.wait()


def pick_half(weight):
    return launch(
        pick_half_kernel, "pick_half", [(weight, ANY)], [(array((HALF, R), BF16), VMEM)],
        [pltpu.SemaphoreType.DMA((1,))],
    )[0]


def back_kernel(grad_ref, chip_ref, mine_ref, other_ref, out_ref):
    half = lax.rem(lax.axis_index("dp"), 2)
    total = jnp.zeros((TOK, R), F32)
    for where, part_ref in ((half, mine_ref), (1 - half, other_ref)):
        at = pl.ds(pl.multiple_of(where * HALF, HALF), HALF)
        weight = part_ref[...] + chip_ref[at, :]
        total += jnp.dot(grad_ref[:, at], weight, preferred_element_type=F32)
    out_ref[...] = total.astype(BF16)


def project_back(grad, chip, mine, other, **ties):
    return launch(
        back_kernel, "back", [(value, VMEM) for value in (grad, chip, mine, other)],
        [(array((TOK, R), BF16), VMEM)], **ties,
    )


def transposed(left, right):
    return lax.dot_general(left, right, (((0,), (0,)), ((), ())), preferred_element_type=F32)


def grad_kernel(narrow_of, flips, wide_ref, *refs):
    *narrow_refs, kept_ref, sent_ref = refs
    narrow = narrow_of(*narrow_refs)
    replica = lax.axis_index("dp")
    x_at, y_at = lax.rem(replica, 4), lax.div(replica, 4)
    for i, flip in enumerate(flips):
        for half in range(2):
            piece = (y_at ^ half) * 4 + (x_at ^ flip)
            columns = pl.ds(pl.multiple_of(piece * PIECE, 128), PIECE)
            total = transposed(narrow, wide_ref[:, columns])
            if i < 2:
                kept_ref[2 * i + half] = total
            else:
                sent_ref[2 * i - 4 + half] = total.astype(BF16)


def read_act(act_ref):
    return act_ref[...]


def make_dpre(pre_ref, dact_ref):
    pre = pre_ref[...]
    t = tanh_of(pre)
    slope = 0.5 * (1.0 + t) + (0.5 * ROOT_2_PI) * pre * (1.0 - t * t) * (
        1.0 + (3.0 * 0.044715) * (pre * pre)
    )
    return (dact_ref[...].astype(F32) * slope).astype(BF16)


def partial_grad(narrow_of, name, flips, wide, *narrow, **ties):
    return launch(
        functools.partial(grad_kernel, narrow_of, flips), name,
        [(value, VMEM) for value in (wide, *narrow)],
        [(array((4, R, PIECE), F32), VMEM), (array((4, R, PIECE), BF16), VMEM)], **ties,
    )


def halve_kernel(kept_ref, came_ref, keep_ref, send_ref):
    keep_ref[...] = kept_ref[:2] + came_ref[:2].astype(F32)
    send_ref[...] = (kept_ref[2:] + came_ref[2:].astype(F32)).astype(BF16)


def halve(kept, came, **ties):
    return launch(
        halve_kernel, "halve", [(kept, VMEM), (came, VMEM)],
        [(array((2, R, PIECE), F32), VMEM), (array((2, R, PIECE), BF16), VMEM)], **ties,
    )


def split_kernel(kept_ref, came_ref, *out_refs):
    for half, out_ref in enumerate(out_refs):
        out_ref[...] = (kept_ref[half] + came_ref[half].astype(F32)).astype(BF16)


def split(kept, came, **ties):
    return launch(
        split_kernel, "split", [(kept, VMEM), (came, VMEM)],
        [(array((R, PIECE), BF16), VMEM)] * 2, **ties,
    )


def finish_kernel(one_ref, two_ref, out_ref):
    out_ref[...] = (one_ref[...].astype(F32) + two_ref[...].astype(F32)).T


def finish(parts):
    return launch(
        finish_kernel, "finish", [(part, VMEM) for part in parts],
        [(array((PIECE, R), F32), pl.BlockSpec((PIECE, R)))],
    )[0]


def feedback_kernel(first, count, before, x_ref, own_ref, act_ref, weight_ref, *refs):
    *rest, out_ref, out_sems = refs
    if before:
        rest = rest[1:]
    out_hbm = rest[0]
    for done_ref in rest[1:]:
        done_ref[...] = jnp.zeros_like(done_ref)
    copies = []
    for i in range(count // TILE):
        rows = slice(i * TILE, (i + 1) * TILE)
        act = act_ref[first + i * TILE : first + (i + 1) * TILE, :]
        for part in range(4):
            at = slice(part * 2 * PIECE, (part + 1) * 2 * PIECE)
            lifted = lax.dot_general(
                act, weight_ref[at, :], (((1,), (1,)), ((), ())), preferred_element_type=F32
            )
            value = x_ref[rows, at].astype(F32) + lifted - own_ref[rows, at].astype(F32)
            out_ref[rows, at] = value.astype(BF16)
        copies.append(
            pltpu.make_async_copy(
                out_ref.at[pl.ds(i * TILE, TILE)],
                out_hbm.at[pl.ds(first + i * TILE, TILE)],
                out_sems.at[i],
            )
        )
        copies[-1].start()
    for copy in copies:
        copy.wait()


def make_feedback(x, own, act, weight, first, before, marked):
    count = x.shape[0]
    ins = [(x, VMEM), (own, VMEM), (act, VMEM), (weight, VMEM)]
    if before is not None:
        ins.append((before, ANY))
    return launch(
        functools.partial(feedback_kernel, first, count, before is not None), "feedback", ins,
        [(array((TOK, D), BF16), ANY)] + [(array((8, 128), F32), VMEM)] * marked,
        [pltpu.VMEM((count, D), BF16), pltpu.SemaphoreType.DMA((count // TILE,))],
        aliases={} if before is None else {4: 0},
    )


def body(
    forward_codes,
    forward_scales,
    stored_base,
    sample_ids,
    backward_codes,
    backward_scales,
    norm_gain,
    w_down,
    w_up,
):
    sections = lax.axis_size("section")
    replicas = lax.axis_size("dp")
    across = replicas // 2
    both = ("section", "dp")

    def along(value, distance):
        pairs = [(s, (s + distance) % sections) for s in range(sections)]
        return lax.ppermute(value, "section", pairs)

    def among(value, flip_x, flip_y=0, section_step=0, stride=1):
        pairs = []
        for s in range(0, sections, stride):
            for d in range(replicas):
                y, x = divmod(d, across)
                source = (y ^ flip_y) * across + (x ^ flip_x)
                goal = ((s + section_step) % sections) * replicas + d
                pairs.append((s * replicas + source, goal))
        return lax.ppermute(value, both, pairs)

    up = w_up[0]
    odd_to_even = [(s, (s + 1) % sections) for s in range(1, sections, 2)]
    even_to_odd = [(s, s + 1) for s in range(0, sections, 2)]
    up_chip = lax.ppermute(up, "section", even_to_odd)
    up_mine = lax.ppermute(pick_half(up), "section", odd_to_even)
    down_next = along(w_down[0], -1)
    gain_next = along(norm_gain, -1)

    codes, base = forward_codes[0], stored_base[0]
    scales = forward_scales[0].T
    firsts = [sum(SPANS[:k]) for k in range(len(SPANS))]
    message0, stats0 = make_messages(codes, scales, base, sample_ids, 0, SPANS[:1])
    *later, stats1 = make_messages(
        codes, scales, base, sample_ids, firsts[1], SPANS[1:], needs=[message0]
    )
    messages = [message0, *later]
    up_mine = hand_on(up_mine, stats1)
    up_other = among(up_mine, 1, stride=2)
    gradient = make_gradient(backward_codes[0], backward_scales[0].T, needs=[later[0]])

    hidden = make_hidden(messages, [stats0, stats1], gain_next, needs=[gradient])
    pre_next, act_next = project_down(hidden, down_next, needs=[up_chip])
    act_before = along(act_next, 2)
    act_own = along(act_next, 1)
    arrived0 = along(messages[0], 1)
    dact_before = project_back(
        gradient, up_chip, up_mine, up_other, needs=[act_before, act_own]
    )[0]
    dact_next = along(dact_before, -2)

    def feedback_of(own, x, at, before, marked=False):
        return make_feedback(x, own, act_own, up, firsts[at], before, marked)

    up_kept, up_sent, message1, message2 = partial_grad(
        read_act, "grad_up", (0, 1, 3, 2), gradient, act_before,
        needs=[arrived0, dact_before], carried=messages[1:3],
    )
    arrived1 = along(message1, 1)
    arrived2 = along(message2, 1)
    down_kept, down_sent = partial_grad(
        make_dpre, "grad_down", (0, 3, 1, 2), hidden, pre_next, dact_next,
    )
    feedback, done = feedback_of(messages[0], arrived0, 0, None, True)
    up_kept, up_sent, message3 = halve(
        up_kept, among(up_sent, 3), needs=[arrived1, done], carried=messages[3:4]
    )
    arrived3 = along(message3, 1)
    down_kept, down_sent = halve(down_kept, among(down_sent, 1), needs=[up_sent])
    feedback, done = feedback_of(message1, arrived1, 1, feedback, True)
    up_parts = split(up_kept, among(up_sent, 1), needs=[arrived2, done])
    down_parts = split(down_kept, among(down_sent, 3), needs=[up_parts[0]])
    grad_up = finish([among(up_parts[half], 0, half, -1) for half in range(2)])
    grad_down = finish([among(down_parts[half], 0, half, 1) for half in range(2)])
    feedback = feedback_of(message2, arrived2, 2, feedback)[0]
    feedback = feedback_of(message3, arrived3, 3, feedback)[0]
    return (feedback[None], grad_down[None], grad_up[None])


def solution(mesh):
    in_specs = (
        P("section", "dp", None),
        P("section", "dp", None),
        P("section", "dp", None),
        P("section", "dp"),
        P("section", "dp", None),
        P("section", "dp", None),
        P("section", None),
        P("section", None, None),
        P("section", None, None),
    )
    out_specs = (P("section", "dp", None), P("section", "dp", None), P("section", "dp", None))
    return jax.shard_map(body, mesh=mesh, in_specs=in_specs, out_specs=out_specs, check_vma=False)
```

```python
import functools
import math

import jax
import jax.numpy as jnp
from jax import lax
from jax.experimental import pallas as pl
from jax.experimental.pallas import tpu as pltpu
from jax.sharding import PartitionSpec as P

D = 6144
R = 128
TOK = 384
PIECE = D // 8
F32 = jnp.float32
BF16 = jnp.bfloat16
TILE = 64
BLOCK = 768
HALF = D // 2
WORDS = BLOCK // 3
CODES = BLOCK // 32
SPANS = (128, 128, 64, 64)
MIB = 1 << 20
ROOT_2_PI = math.sqrt(2.0 / math.pi)
VMEM = pl.BlockSpec(memory_space=pltpu.VMEM)
ANY = pl.BlockSpec(memory_space=pl.ANY)


def array(shape, dtype):
    return jax.ShapeDtypeStruct(shape, dtype)


def launch(
    kernel, name, ins, outs, scratch=(), grid=(), aliases=None, needs=(), carried=(), grant=14
):
    n_in, n_out = len(ins), len(outs)
    first_carried = n_in + len(needs)
    n_all = first_carried + len(carried)
    aliases = dict(aliases or {})
    for k in range(len(carried)):
        aliases[first_carried + k] = n_out + k

    def wrapped(*refs):
        rest = refs[n_all + n_out + len(carried) :]
        kernel(*refs[:n_in], *refs[n_all : n_all + n_out], *rest)

    return pl.pallas_call(
        wrapped,
        grid=grid,
        in_specs=[spec for _, spec in ins] + [ANY] * (len(needs) + len(carried)),
        out_specs=[spec for _, spec in outs] + [ANY] * len(carried),
        out_shape=[out for out, _ in outs] + [array(c.shape, c.dtype) for c in carried],
        scratch_shapes=scratch,
        input_output_aliases=aliases,
        compiler_params=pltpu.CompilerParams(vmem_limit_bytes=grant * MIB),
        cost_estimate=pl.CostEstimate(flops=1, bytes_accessed=1, transcendentals=0),
        name=name,
    )(*[value for value, _ in ins], *needs, *carried)


def lanes(shape):
    return lax.broadcasted_iota(jnp.int32, shape, 1)


def block_at(b):
    return pl.ds(pl.multiple_of(b * BLOCK, 128), BLOCK)


def spreader():
    shape = (32, BLOCK)
    return (lax.broadcasted_iota(jnp.int32, shape, 0) == lanes(shape) // 32).astype(F32).astype(
        BF16
    )


def turn_scales(scales_ref, turned_ref, rows):
    padding = jnp.zeros((32 - CODES, TOK), F32)
    for b in range(D // BLOCK):
        part = scales_ref[b * CODES : (b + 1) * CODES, :].astype(F32)
        turned_ref[b] = jnp.concatenate([part, padding], axis=0).T[rows].astype(BF16)


def exact(left, right):
    return jnp.dot(left, right, preferred_element_type=F32)


def chunks_of(out_refs):
    found, start = [], 0
    for ref in out_refs:
        count = ref.shape[0]
        for row in range(0, count, TILE):
            found.append((ref, row, start + row, TILE))
        start += count
    return found


def message_kernel(first, codes_ref, scales_ref, base_ref, ids_ref, *refs):
    *out_refs, stats_ref, turned_ref, picks_ref, pivot_ref, sum_ref, square_ref = refs
    count = stats_ref.shape[0]
    mine = slice(first, first + count)
    turn_scales(scales_ref, turned_ref, mine)
    spread = spreader()
    hits = lax.broadcasted_iota(jnp.int32, (32, TOK), 0) == ids_ref[...]
    picks_ref[...] = hits.astype(F32).T[mine].astype(BF16)
    chunks = chunks_of(out_refs)

    def decode(b, take):
        base_block = base_ref[:, block_at(b)]
        for ref, row, at, n in chunks:
            rows = slice(at, at + n)
            scale = exact(turned_ref[b, rows, :], spread)
            base = exact(picks_ref[rows, :], base_block)
            lane = lanes((n, 128))
            values = []
            for k in range(WORDS // 128):
                words_at = pl.ds(pl.multiple_of(b * WORDS + k * 128, 128), 128)
                words = codes_ref[first + at : first + at + n, words_at]
                for j in range(3):
                    spot = lane + 128 * j
                    word = jnp.take_along_axis(words, spot // 3, axis=1)
                    code = jnp.right_shift(word, (spot % 3) * 4) & 15
                    tile = 3 * k + j
                    part = slice(tile * 128, (tile + 1) * 128)
                    value = base[:, part] + scale[:, part] * (code - 8).astype(F32)
                    value = value.astype(BF16)
                    to = pl.ds(pl.multiple_of(b * BLOCK + tile * 128, 128), 128)
                    ref[row : row + n, to] = value
                    values.append(value.astype(F32))
            take(rows, n, values)

    def begin(rows, n, values):
        pivot = jnp.sum(sum(values), axis=1, keepdims=True) / BLOCK
        pivot = jnp.broadcast_to(pivot, (n, 128))
        pivot_ref[rows, :] = pivot
        away = [value - pivot for value in values]
        sum_ref[rows, :] = sum(away)
        square_ref[rows, :] = sum(v * v for v in away)

    def go_on(rows, n, values):
        pivot = pivot_ref[rows, :]
        away = [value - pivot for value in values]
        sum_ref[rows, :] += sum(away)
        square_ref[rows, :] += sum(v * v for v in away)

    def one_block(b, carry):
        decode(b, go_on)
        return carry

    decode(0, begin)
    lax.fori_loop(1, D // BLOCK, one_block, 0)
    shift = jnp.sum(sum_ref[...], axis=1, keepdims=True) * (1.0 / D)
    square = jnp.sum(square_ref[...], axis=1, keepdims=True) * (1.0 / D)
    variance = jnp.maximum(square - shift * shift, 0.0)
    stats_ref[:, :128] = pivot_ref[...] + shift
    stats_ref[:, 128:] = jnp.broadcast_to(lax.rsqrt(variance + 1e-05), (count, 128))


def make_messages(codes, scales, base, ids, first, spans, **ties):
    count = sum(spans)
    return launch(
        functools.partial(message_kernel, first), "message",
        [(value, VMEM) for value in (codes, scales, base, ids)],
        [(array((span, D), BF16), VMEM) for span in spans] + [(array((count, 256), F32), VMEM)],
        [pltpu.VMEM((D // BLOCK, count, 32), BF16), pltpu.VMEM((count, 32), BF16)]
        + [pltpu.VMEM((count, 128), F32)] * 3,
        **ties,
    )


def gradient_kernel(codes_ref, scales_ref, out_ref, turned_ref):
    turn_scales(scales_ref, turned_ref, slice(0, TOK))
    spread = spreader()

    def one_block(b, carry):
        for at in range(0, TOK, 96):
            rows = slice(at, at + 96)
            scale = exact(turned_ref[b, rows, :], spread)
            codes = codes_ref[rows, block_at(b)].astype(F32)
            out_ref[rows, block_at(b)] = (scale * (codes - 128.0)).astype(BF16)
        return carry

    lax.fori_loop(0, D // BLOCK, one_block, 0)


def make_gradient(codes, scales, **ties):
    return launch(
        gradient_kernel, "gradient", [(codes, VMEM), (scales, VMEM)],
        [(array((TOK, D), BF16), VMEM)], [pltpu.VMEM((D // BLOCK, TOK, 32), BF16)], **ties,
    )[0]


def tanh_of(pre):
    return jnp.tanh(ROOT_2_PI * (pre + 0.044715 * (pre * pre * pre)))


def hidden_kernel(n, gain_ref, *refs):
    message_refs, stats_refs, out_ref = refs[:n], refs[n:-1], refs[-1]
    messages, stats = [
        [(ref, at) for ref, row, _, rows in chunks_of(found) for at in range(row, row + rows, TILE)]
        for found in (message_refs, stats_refs)
    ]
    for t, ((ref, row), (stats_ref, stats_row)) in enumerate(zip(messages, stats)):
        rows = slice(stats_row, stats_row + TILE)
        mean, scale = stats_ref[rows, :128], stats_ref[rows, 128:]

        def one_block(b, carry, ref=ref, row=row, t=t, mean=mean, scale=scale):
            for c in range(BLOCK // 128):
                at = pl.ds(pl.multiple_of(b * BLOCK + c * 128, 128), 128)
                x = ref[row : row + TILE, at].astype(F32)
                value = gain_ref[:, at] * (x - mean) * scale
                out_ref[t * TILE : (t + 1) * TILE, at] = value.astype(BF16)
            return carry

        lax.fori_loop(0, D // BLOCK, one_block, 0)


def make_hidden(messages, stats, gain, **ties):
    return launch(
        functools.partial(hidden_kernel, len(messages)), "hidden",
        [(value, VMEM) for value in (gain, *messages, *stats)],
        [(array((TOK, D), BF16), VMEM)], **ties,
    )[0]


def down_kernel(hidden_ref, weight_ref, pre_ref, act_ref):
    pre = jnp.dot(hidden_ref[...], weight_ref[...], preferred_element_type=F32)
    pre_ref[...] = pre
    act_ref[...] = (0.5 * pre * (1.0 + tanh_of(pre))).astype(BF16)


def project_down(hidden, weight, **ties):
    return launch(
        down_kernel, "down", [(hidden, VMEM), (weight, VMEM)],
        [(array((TOK, R), F32), VMEM), (array((TOK, R), BF16), VMEM)], **ties,
    )


def pick_half_kernel(weight_ref, out_ref, sem):
    half = lax.rem(lax.axis_index("dp"), 2)
    rows = pl.ds(pl.multiple_of(half * HALF, HALF), HALF)
    copy = pltpu.make_async_copy(weight_ref.at[rows], out_ref, sem.at[0])
    copy.start()
    copy.wait()


def pick_half(weight):
    return launch(
        pick_half_kernel, "pick_half", [(weight, ANY)], [(array((HALF, R), BF16), VMEM)],
        [pltpu.SemaphoreType.DMA((1,))],
    )[0]


def back_kernel(grad_ref, chip_ref, mine_ref, other_ref, out_ref):
    half = lax.rem(lax.axis_index("dp"), 2)
    total = jnp.zeros((TOK, R), F32)
    for where, part_ref in ((half, mine_ref), (1 - half, other_ref)):
        at = pl.ds(pl.multiple_of(where * HALF, HALF), HALF)
        weight = part_ref[...] + chip_ref[at, :]
        total += jnp.dot(grad_ref[:, at], weight, preferred_element_type=F32)
    out_ref[...] = total.astype(BF16)


def project_back(grad, chip, mine, other, **ties):
    return launch(
        back_kernel, "back", [(value, VMEM) for value in (grad, chip, mine, other)],
        [(array((TOK, R), BF16), VMEM)], **ties,
    )


def transposed(left, right):
    return lax.dot_general(left, right, (((0,), (0,)), ((), ())), preferred_element_type=F32)


def grad_kernel(narrow_of, flips, wide_ref, *refs):
    *narrow_refs, kept_ref, sent_ref = refs
    narrow = narrow_of(*narrow_refs)
    replica = lax.axis_index("dp")
    x_at, y_at = lax.rem(replica, 4), lax.div(replica, 4)
    for i, flip in enumerate(flips):
        for half in range(2):
            piece = (y_at ^ half) * 4 + (x_at ^ flip)
            columns = pl.ds(pl.multiple_of(piece * PIECE, 128), PIECE)
            total = transposed(narrow, wide_ref[:, columns])
            if i < 2:
                kept_ref[2 * i + half] = total
            else:
                sent_ref[2 * i - 4 + half] = total.astype(BF16)


def read_act(act_ref):
    return act_ref[...]


def make_dpre(pre_ref, dact_ref):
    pre = pre_ref[...]
    t = tanh_of(pre)
    slope = 0.5 * (1.0 + t) + (0.5 * ROOT_2_PI) * pre * (1.0 - t * t) * (
        1.0 + (3.0 * 0.044715) * (pre * pre)
    )
    return (dact_ref[...].astype(F32) * slope).astype(BF16)


def partial_grad(narrow_of, name, flips, wide, *narrow, **ties):
    return launch(
        functools.partial(grad_kernel, narrow_of, flips), name,
        [(value, VMEM) for value in (wide, *narrow)],
        [(array((4, R, PIECE), F32), VMEM), (array((4, R, PIECE), BF16), VMEM)], **ties,
    )


def halve_kernel(kept_ref, came_ref, keep_ref, send_ref):
    keep_ref[...] = kept_ref[:2] + came_ref[:2].astype(F32)
    send_ref[...] = (kept_ref[2:] + came_ref[2:].astype(F32)).astype(BF16)


def halve(kept, came, **ties):
    return launch(
        halve_kernel, "halve", [(kept, VMEM), (came, VMEM)],
        [(array((2, R, PIECE), F32), VMEM), (array((2, R, PIECE), BF16), VMEM)], **ties,
    )


def split_kernel(kept_ref, came_ref, *out_refs):
    for half, out_ref in enumerate(out_refs):
        out_ref[...] = (kept_ref[half] + came_ref[half].astype(F32)).astype(BF16)


def split(kept, came, **ties):
    return launch(
        split_kernel, "split", [(kept, VMEM), (came, VMEM)],
        [(array((R, PIECE), BF16), VMEM)] * 2, **ties,
    )


def finish_kernel(one_ref, two_ref, out_ref, done_ref):
    out_ref[...] = (one_ref[...].astype(F32) + two_ref[...].astype(F32)).T
    done_ref[...] = jnp.zeros_like(done_ref)


def finish(parts, **ties):
    return launch(
        finish_kernel, "finish", [(part, VMEM) for part in parts],
        [
            (array((PIECE, R), F32), pl.BlockSpec((PIECE, R))),
            (array((8, 128), F32), VMEM),
        ],
        **ties,
    )


def feedback_kernel(first, count, before, x_ref, own_ref, act_ref, weight_ref, *refs):
    *rest, out_ref, out_sems = refs
    if before:
        rest = rest[1:]
    out_hbm = rest[0]
    for done_ref in rest[1:]:
        done_ref[...] = jnp.zeros_like(done_ref)
    copies = []
    for i in range(count // TILE):
        rows = slice(i * TILE, (i + 1) * TILE)
        act = act_ref[first + i * TILE : first + (i + 1) * TILE, :]
        for part in range(4):
            at = slice(part * 2 * PIECE, (part + 1) * 2 * PIECE)
            lifted = lax.dot_general(
                act, weight_ref[at, :], (((1,), (1,)), ((), ())), preferred_element_type=F32
            )
            value = x_ref[rows, at].astype(F32) + lifted - own_ref[rows, at].astype(F32)
            out_ref[rows, at] = value.astype(BF16)
        copies.append(
            pltpu.make_async_copy(
                out_ref.at[pl.ds(i * TILE, TILE)],
                out_hbm.at[pl.ds(first + i * TILE, TILE)],
                out_sems.at[i],
            )
        )
        copies[-1].start()
    for copy in copies:
        copy.wait()


def make_feedback(x, own, act, weight, first, before, marked):
    count = x.shape[0]
    ins = [(x, VMEM), (own, VMEM), (act, VMEM), (weight, VMEM)]
    if before is not None:
        ins.append((before, ANY))
    return launch(
        functools.partial(feedback_kernel, first, count, before is not None), "feedback", ins,
        [(array((TOK, D), BF16), ANY)] + [(array((8, 128), F32), VMEM)] * marked,
        [pltpu.VMEM((count, D), BF16), pltpu.SemaphoreType.DMA((count // TILE,))],
        aliases={} if before is None else {4: 0},
    )


def body(
    forward_codes,
    forward_scales,
    stored_base,
    sample_ids,
    backward_codes,
    backward_scales,
    norm_gain,
    w_down,
    w_up,
):
    sections = lax.axis_size("section")
    replicas = lax.axis_size("dp")
    across = replicas // 2
    both = ("section", "dp")

    def along(value, distance):
        pairs = [(s, (s + distance) % sections) for s in range(sections)]
        return lax.ppermute(value, "section", pairs)

    def among(value, flip_x, flip_y=0, section_step=0, stride=1):
        pairs = []
        for s in range(0, sections, stride):
            for d in range(replicas):
                y, x = divmod(d, across)
                source = (y ^ flip_y) * across + (x ^ flip_x)
                goal = ((s + section_step) % sections) * replicas + d
                pairs.append((s * replicas + source, goal))
        return lax.ppermute(value, both, pairs)

    up = w_up[0]
    odd_to_even = [(s, (s + 1) % sections) for s in range(1, sections, 2)]
    even_to_odd = [(s, s + 1) for s in range(0, sections, 2)]
    up_chip = lax.ppermute(up, "section", even_to_odd)
    up_mine = lax.ppermute(pick_half(up), "section", odd_to_even)
    up_other = among(up_mine, 1, stride=2)
    down_next = along(w_down[0], -1)
    gain_next = along(norm_gain, -1)

    codes, base = forward_codes[0], stored_base[0]
    scales = forward_scales[0].T
    firsts = [sum(SPANS[:k]) for k in range(len(SPANS))]
    message0, stats0 = make_messages(codes, scales, base, sample_ids, 0, SPANS[:1])
    *later, stats1 = make_messages(
        codes, scales, base, sample_ids, firsts[1], SPANS[1:], needs=[message0]
    )
    messages = [message0, *later]
    gradient = make_gradient(backward_codes[0], backward_scales[0].T, needs=[later[0]])

    hidden = make_hidden(messages, [stats0, stats1], gain_next, needs=[gradient])
    pre_next, act_next = project_down(hidden, down_next, needs=[up_chip])
    act_before = along(act_next, 2)
    act_own = along(act_next, 1)
    arrived0 = along(messages[0], 1)
    dact_before = project_back(
        gradient, up_chip, up_mine, up_other, needs=[act_next]
    )[0]
    dact_next = along(dact_before, -2)

    def feedback_of(own, x, at, before, marked=False):
        return make_feedback(x, own, act_own, up, firsts[at], before, marked)

    up_kept, up_sent, message1, message2 = partial_grad(
        read_act, "grad_up", (0, 1, 3, 2), gradient, act_before,
        needs=[act_own, arrived0, dact_next], carried=messages[1:3],
    )
    arrived1 = along(message1, 1)
    arrived2 = along(message2, 1)
    down_kept, down_sent = partial_grad(
        make_dpre, "grad_down", (0, 3, 1, 2), hidden, pre_next, dact_next,
    )
    feedback, done = feedback_of(messages[0], arrived0, 0, None, True)
    up_kept, up_sent, message3 = halve(
        up_kept, among(up_sent, 3), needs=[arrived1, done], carried=messages[3:4]
    )
    arrived3 = along(message3, 1)
    down_kept, down_sent = halve(down_kept, among(down_sent, 1), needs=[up_sent])
    feedback, done = feedback_of(message1, arrived1, 1, feedback, True)
    up_parts = split(up_kept, among(up_sent, 1), needs=[arrived2, done])
    down_parts = split(down_kept, among(down_sent, 3), needs=[up_parts[0]])
    feedback = feedback_of(message2, arrived2, 2, feedback)[0]
    feedback, done = feedback_of(message3, arrived3, 3, feedback, True)
    grad_up, done_up = finish([among(up_parts[half], 0, half, -1) for half in range(2)])
    grad_down = finish(
        [among(down_parts[half], 0, half, 1) for half in range(2)], needs=[done, done_up]
    )[0]
    return (feedback[None], grad_down[None], grad_up[None])


def solution(mesh):
    in_specs = (
        P("section", "dp", None),
        P("section", "dp", None),
        P("section", "dp", None),
        P("section", "dp"),
        P("section", "dp", None),
        P("section", "dp", None),
        P("section", None),
        P("section", None, None),
        P("section", None, None),
    )
    out_specs = (P("section", "dp", None), P("section", "dp", None), P("section", "dp", None))
    return jax.shard_map(body, mesh=mesh, in_specs=in_specs, out_specs=out_specs, check_vma=False)
```

```python
import functools
import math

import jax
import jax.numpy as jnp
from jax import lax
from jax.experimental import pallas as pl
from jax.experimental.pallas import tpu as pltpu
from jax.sharding import PartitionSpec as P

D = 6144
R = 128
TOK = 384
PIECE = D // 8
F32 = jnp.float32
BF16 = jnp.bfloat16
TILE = 48
BLOCK = 768
WORDS = BLOCK // 3
CODES = BLOCK // 32
SPANS = (96, 144, 96, 48)
MIB = 1 << 20
ROOT_2_PI = math.sqrt(2.0 / math.pi)
VMEM = pl.BlockSpec(memory_space=pltpu.VMEM)
ANY = pl.BlockSpec(memory_space=pl.ANY)


def array(shape, dtype):
    return jax.ShapeDtypeStruct(shape, dtype)


def launch(
    kernel, name, ins, outs, scratch=(), grid=(), aliases=None, needs=(), carried=(), grant=14
):
    n_in, n_out = len(ins), len(outs)
    first_carried = n_in + len(needs)
    n_all = first_carried + len(carried)
    aliases = dict(aliases or {})
    for k in range(len(carried)):
        aliases[first_carried + k] = n_out + k

    def wrapped(*refs):
        rest = refs[n_all + n_out + len(carried) :]
        kernel(*refs[:n_in], *refs[n_all : n_all + n_out], *rest)

    return pl.pallas_call(
        wrapped,
        grid=grid,
        in_specs=[spec for _, spec in ins] + [ANY] * (len(needs) + len(carried)),
        out_specs=[spec for _, spec in outs] + [ANY] * len(carried),
        out_shape=[out for out, _ in outs] + [array(c.shape, c.dtype) for c in carried],
        scratch_shapes=scratch,
        input_output_aliases=aliases,
        compiler_params=pltpu.CompilerParams(vmem_limit_bytes=grant * MIB),
        cost_estimate=pl.CostEstimate(flops=1, bytes_accessed=1, transcendentals=0),
        name=name,
    )(*[value for value, _ in ins], *needs, *carried)


def lanes(shape):
    return lax.broadcasted_iota(jnp.int32, shape, 1)


def block_at(b):
    return pl.ds(pl.multiple_of(b * BLOCK, 128), BLOCK)


def spreader():
    shape = (32, BLOCK)
    return (lax.broadcasted_iota(jnp.int32, shape, 0) == lanes(shape) // 32).astype(F32).astype(
        BF16
    )


def turn_scales(scales_ref, turned_ref, rows):
    padding = jnp.zeros((32 - CODES, TOK), F32)
    for b in range(D // BLOCK):
        part = scales_ref[b * CODES : (b + 1) * CODES, :].astype(F32)
        turned_ref[b] = jnp.concatenate([part, padding], axis=0).T[rows].astype(BF16)


def exact(left, right):
    return jnp.dot(left, right, preferred_element_type=F32)


def chunks_of(out_refs):
    found, start = [], 0
    for ref in out_refs:
        count = ref.shape[0]
        for row in range(0, count, 96):
            found.append((ref, row, start + row, min(96, count - row)))
        start += count
    return found


def message_kernel(first, codes_ref, scales_ref, base_ref, ids_ref, *refs):
    *out_refs, stats_ref, turned_ref, picks_ref, pivot_ref, sum_ref, square_ref = refs
    count = stats_ref.shape[0]
    mine = slice(first, first + count)
    turn_scales(scales_ref, turned_ref, mine)
    spread = spreader()
    hits = lax.broadcasted_iota(jnp.int32, (32, TOK), 0) == ids_ref[...]
    picks_ref[...] = hits.astype(F32).T[mine].astype(BF16)
    chunks = chunks_of(out_refs)

    def decode(b, take):
        base_block = base_ref[:, block_at(b)]
        for ref, row, at, n in chunks:
            rows = slice(at, at + n)
            scale = exact(turned_ref[b, rows, :], spread)
            base = exact(picks_ref[rows, :], base_block)
            lane = lanes((n, 128))
            values = []
            for k in range(WORDS // 128):
                words_at = pl.ds(pl.multiple_of(b * WORDS + k * 128, 128), 128)
                words = codes_ref[first + at : first + at + n, words_at]
                for j in range(3):
                    spot = lane + 128 * j
                    word = jnp.take_along_axis(words, spot // 3, axis=1)
                    code = jnp.right_shift(word, (spot % 3) * 4) & 15
                    tile = 3 * k + j
                    part = slice(tile * 128, (tile + 1) * 128)
                    value = base[:, part] + scale[:, part] * (code - 8).astype(F32)
                    value = value.astype(BF16)
                    to = pl.ds(pl.multiple_of(b * BLOCK + tile * 128, 128), 128)
                    ref[row : row + n, to] = value
                    values.append(value.astype(F32))
            take(rows, n, values)

    def begin(rows, n, values):
        pivot = jnp.sum(sum(values), axis=1, keepdims=True) / BLOCK
        pivot = jnp.broadcast_to(pivot, (n, 128))
        pivot_ref[rows, :] = pivot
        away = [value - pivot for value in values]
        sum_ref[rows, :] = sum(away)
        square_ref[rows, :] = sum(v * v for v in away)

    def go_on(rows, n, values):
        pivot = pivot_ref[rows, :]
        away = [value - pivot for value in values]
        sum_ref[rows, :] += sum(away)
        square_ref[rows, :] += sum(v * v for v in away)

    def one_block(b, carry):
        decode(b, go_on)
        return carry

    decode(0, begin)
    lax.fori_loop(1, D // BLOCK, one_block, 0)
    shift = jnp.sum(sum_ref[...], axis=1, keepdims=True) * (1.0 / D)
    square = jnp.sum(square_ref[...], axis=1, keepdims=True) * (1.0 / D)
    variance = jnp.maximum(square - shift * shift, 0.0)
    stats_ref[:, :128] = pivot_ref[...] + shift
    stats_ref[:, 128:] = jnp.broadcast_to(lax.rsqrt(variance + 1e-05), (count, 128))


def make_messages(codes, scales, base, ids, first, spans, **ties):
    count = sum(spans)
    return launch(
        functools.partial(message_kernel, first), "message",
        [(value, VMEM) for value in (codes, scales, base, ids)],
        [(array((span, D), BF16), VMEM) for span in spans] + [(array((count, 256), F32), VMEM)],
        [pltpu.VMEM((D // BLOCK, count, 32), BF16), pltpu.VMEM((count, 32), BF16)]
        + [pltpu.VMEM((count, 128), F32)] * 3,
        **ties,
    )


def gradient_kernel(codes_ref, scales_ref, out_ref, turned_ref):
    turn_scales(scales_ref, turned_ref, slice(0, TOK))
    spread = spreader()

    def one_block(b, carry):
        for at in range(0, TOK, 96):
            rows = slice(at, at + 96)
            scale = exact(turned_ref[b, rows, :], spread)
            codes = codes_ref[rows, block_at(b)].astype(F32)
            out_ref[rows, block_at(b)] = (scale * (codes - 128.0)).astype(BF16)
        return carry

    lax.fori_loop(0, D // BLOCK, one_block, 0)


def make_gradient(codes, scales, **ties):
    return launch(
        gradient_kernel, "gradient", [(codes, VMEM), (scales, VMEM)],
        [(array((TOK, D), BF16), VMEM)], [pltpu.VMEM((D // BLOCK, TOK, 32), BF16)], **ties,
    )[0]


def tanh_of(pre):
    return jnp.tanh(ROOT_2_PI * (pre + 0.044715 * (pre * pre * pre)))


def hidden_kernel(n, gain_ref, *refs):
    message_refs, stats_refs, out_ref = refs[:n], refs[n:-1], refs[-1]
    messages, stats = [
        [(ref, at) for ref, row, _, rows in chunks_of(found) for at in range(row, row + rows, TILE)]
        for found in (message_refs, stats_refs)
    ]
    for t, ((ref, row), (stats_ref, stats_row)) in enumerate(zip(messages, stats)):
        rows = slice(stats_row, stats_row + TILE)
        mean, scale = stats_ref[rows, :128], stats_ref[rows, 128:]

        def one_block(b, carry, ref=ref, row=row, t=t, mean=mean, scale=scale):
            for c in range(BLOCK // 128):
                at = pl.ds(pl.multiple_of(b * BLOCK + c * 128, 128), 128)
                x = ref[row : row + TILE, at].astype(F32)
                value = gain_ref[:, at] * (x - mean) * scale
                out_ref[t * TILE : (t + 1) * TILE, at] = value.astype(BF16)
            return carry

        lax.fori_loop(0, D // BLOCK, one_block, 0)


def make_hidden(messages, stats, gain, **ties):
    return launch(
        functools.partial(hidden_kernel, len(messages)), "hidden",
        [(value, VMEM) for value in (gain, *messages, *stats)],
        [(array((TOK, D), BF16), VMEM)], **ties,
    )[0]


def down_kernel(hidden_ref, weight_ref, pre_ref, act_ref):
    pre = jnp.dot(hidden_ref[...], weight_ref[...], preferred_element_type=F32)
    pre_ref[...] = pre
    act_ref[...] = (0.5 * pre * (1.0 + tanh_of(pre))).astype(BF16)


def project_down(hidden, weight, **ties):
    return launch(
        down_kernel, "down", [(hidden, VMEM), (weight, VMEM)],
        [(array((TOK, R), F32), VMEM), (array((TOK, R), BF16), VMEM)], **ties,
    )


def back_kernel(grad_ref, weight_ref, out_ref):
    out_ref[...] = jnp.dot(
        grad_ref[...], weight_ref[...], preferred_element_type=F32
    ).astype(BF16)


def project_back(grad, weight, **ties):
    return launch(
        back_kernel, "back", [(grad, VMEM), (weight, VMEM)],
        [(array((TOK, R), BF16), VMEM)], **ties,
    )


def transposed(left, right):
    return lax.dot_general(left, right, (((0,), (0,)), ((), ())), preferred_element_type=F32)


def grad_kernel(narrow_of, flips, wide_ref, *refs):
    *narrow_refs, kept_ref, sent_ref = refs
    narrow = narrow_of(*narrow_refs)
    replica = lax.axis_index("dp")
    x_at, y_at = lax.rem(replica, 4), lax.div(replica, 4)
    for i, flip in enumerate(flips):
        for half in range(2):
            piece = (y_at ^ half) * 4 + (x_at ^ flip)
            columns = pl.ds(pl.multiple_of(piece * PIECE, 128), PIECE)
            total = transposed(narrow, wide_ref[:, columns])
            if i < 2:
                kept_ref[2 * i + half] = total
            else:
                sent_ref[2 * i - 4 + half] = total.astype(BF16)


def read_act(act_ref):
    return act_ref[...]


def make_dpre(pre_ref, dact_ref):
    pre = pre_ref[...]
    t = tanh_of(pre)
    slope = 0.5 * (1.0 + t) + (0.5 * ROOT_2_PI) * pre * (1.0 - t * t) * (
        1.0 + (3.0 * 0.044715) * (pre * pre)
    )
    return (dact_ref[...].astype(F32) * slope).astype(BF16)


def partial_grad(narrow_of, name, flips, wide, *narrow, **ties):
    return launch(
        functools.partial(grad_kernel, narrow_of, flips), name,
        [(value, VMEM) for value in (wide, *narrow)],
        [(array((4, R, PIECE), F32), VMEM), (array((4, R, PIECE), BF16), VMEM)], **ties,
    )


def halve_kernel(kept_ref, came_ref, keep_ref, send_ref):
    keep_ref[...] = kept_ref[:2] + came_ref[:2].astype(F32)
    send_ref[...] = (kept_ref[2:] + came_ref[2:].astype(F32)).astype(BF16)


def halve(kept, came, **ties):
    return launch(
        halve_kernel, "halve", [(kept, VMEM), (came, VMEM)],
        [(array((2, R, PIECE), F32), VMEM), (array((2, R, PIECE), BF16), VMEM)], **ties,
    )


def split_kernel(kept_ref, came_ref, *out_refs):
    for half, out_ref in enumerate(out_refs):
        out_ref[...] = (kept_ref[half] + came_ref[half].astype(F32)).astype(BF16)


def split(kept, came, **ties):
    return launch(
        split_kernel, "split", [(kept, VMEM), (came, VMEM)],
        [(array((R, PIECE), BF16), VMEM)] * 2, **ties,
    )


def finish_kernel(one_ref, two_ref, out_ref, done_ref):
    out_ref[...] = (one_ref[...].astype(F32) + two_ref[...].astype(F32)).T
    done_ref[...] = jnp.zeros_like(done_ref)


def finish(parts, **ties):
    return launch(
        finish_kernel, "finish", [(part, VMEM) for part in parts],
        [
            (array((PIECE, R), F32), pl.BlockSpec((PIECE, R))),
            (array((8, 128), F32), VMEM),
        ],
        **ties,
    )


def feedback_kernel(first, count, before, x_ref, own_ref, act_ref, weight_ref, *refs):
    *rest, out_ref, out_sems = refs
    if before:
        rest = rest[1:]
    out_hbm = rest[0]
    for done_ref in rest[1:]:
        done_ref[...] = jnp.zeros_like(done_ref)
    copies = []
    for i in range(count // TILE):
        rows = slice(i * TILE, (i + 1) * TILE)
        act = act_ref[first + i * TILE : first + (i + 1) * TILE, :]
        for part in range(4):
            at = slice(part * 2 * PIECE, (part + 1) * 2 * PIECE)
            lifted = lax.dot_general(
                act, weight_ref[at, :], (((1,), (1,)), ((), ())), preferred_element_type=F32
            )
            value = x_ref[rows, at].astype(F32) + lifted - own_ref[rows, at].astype(F32)
            out_ref[rows, at] = value.astype(BF16)
        copies.append(
            pltpu.make_async_copy(
                out_ref.at[pl.ds(i * TILE, TILE)],
                out_hbm.at[pl.ds(first + i * TILE, TILE)],
                out_sems.at[i],
            )
        )
        copies[-1].start()
    for copy in copies:
        copy.wait()


def make_feedback(x, own, act, weight, first, before, marked):
    count = x.shape[0]
    ins = [(x, VMEM), (own, VMEM), (act, VMEM), (weight, VMEM)]
    if before is not None:
        ins.append((before, ANY))
    return launch(
        functools.partial(feedback_kernel, first, count, before is not None), "feedback", ins,
        [(array((TOK, D), BF16), ANY)] + [(array((8, 128), F32), VMEM)] * marked,
        [pltpu.VMEM((count, D), BF16), pltpu.SemaphoreType.DMA((count // TILE,))],
        aliases={} if before is None else {4: 0},
    )


def body(
    forward_codes,
    forward_scales,
    stored_base,
    sample_ids,
    backward_codes,
    backward_scales,
    norm_gain,
    w_down,
    w_up,
):
    sections = lax.axis_size("section")
    replicas = lax.axis_size("dp")
    across = replicas // 2
    both = ("section", "dp")

    def along(value, distance):
        pairs = [(s, (s + distance) % sections) for s in range(sections)]
        return lax.ppermute(value, "section", pairs)

    def among(value, flip_x, flip_y=0, section_step=0):
        pairs = []
        for s in range(sections):
            for d in range(replicas):
                y, x = divmod(d, across)
                source = (y ^ flip_y) * across + (x ^ flip_x)
                goal = ((s + section_step) % sections) * replicas + d
                pairs.append((s * replicas + source, goal))
        return lax.ppermute(value, both, pairs)

    up = w_up[0]
    up_before = along(up, 1)
    down_next = along(w_down[0], -1)
    gain_next = along(norm_gain, -1)

    codes, base = forward_codes[0], stored_base[0]
    scales = forward_scales[0].T
    firsts = [sum(SPANS[:k]) for k in range(len(SPANS))]
    message0, stats0 = make_messages(codes, scales, base, sample_ids, 0, SPANS[:1])
    *later, stats1 = make_messages(
        codes, scales, base, sample_ids, firsts[1], SPANS[1:], needs=[message0]
    )
    messages = [message0, *later]
    gradient = make_gradient(backward_codes[0], backward_scales[0].T, needs=[later[0]])

    hidden = make_hidden(messages, [stats0, stats1], gain_next, needs=[gradient])
    pre_next, act_next = project_down(hidden, down_next, needs=[up_before])
    act_before = along(act_next, 2)
    act_own = along(act_next, 1)
    arrived0 = along(messages[0], 1)
    dact_before = project_back(gradient, up_before, needs=[act_next])[0]
    dact_next = along(dact_before, -2)

    def feedback_of(own, x, at, before, marked=False):
        return make_feedback(x, own, act_own, up, firsts[at], before, marked)

    up_kept, up_sent, message1, message2 = partial_grad(
        read_act, "grad_up", (0, 1, 3, 2), gradient, act_before,
        needs=[act_own, arrived0, dact_next], carried=messages[1:3],
    )
    arrived1 = along(message1, 1)
    arrived2 = along(message2, 1)
    down_kept, down_sent = partial_grad(
        make_dpre, "grad_down", (0, 3, 1, 2), hidden, pre_next, dact_next,
    )
    feedback, done = feedback_of(messages[0], arrived0, 0, None, True)
    up_kept, up_sent, message3 = halve(
        up_kept, among(up_sent, 3), needs=[arrived1, done], carried=messages[3:4]
    )
    arrived3 = along(message3, 1)
    down_kept, down_sent = halve(down_kept, among(down_sent, 1), needs=[up_sent])
    feedback, done = feedback_of(message1, arrived1, 1, feedback, True)
    up_parts = split(up_kept, among(up_sent, 1), needs=[done])
    down_parts = split(down_kept, among(down_sent, 3), needs=[up_parts[0], arrived2])
    feedback = feedback_of(message2, arrived2, 2, feedback)[0]
    feedback, done = feedback_of(message3, arrived3, 3, feedback, True)
    grad_up, done_up = finish([among(up_parts[half], 0, half, -1) for half in range(2)])
    grad_down = finish(
        [among(down_parts[half], 0, half, 1) for half in range(2)], needs=[done, done_up]
    )[0]
    return (feedback[None], grad_down[None], grad_up[None])


def solution(mesh):
    in_specs = (
        P("section", "dp", None),
        P("section", "dp", None),
        P("section", "dp", None),
        P("section", "dp"),
        P("section", "dp", None),
        P("section", "dp", None),
        P("section", None),
        P("section", None, None),
        P("section", None, None),
    )
    out_specs = (P("section", "dp", None), P("section", "dp", None), P("section", "dp", None))
    return jax.shard_map(body, mesh=mesh, in_specs=in_specs, out_specs=out_specs, check_vma=False)
```
